128 devices in a mesh: tx: 8 (over x_hi, z), ty: 16 (over x_lo, y, core).
Axes of the slice: x: 4 (x_hi: 2, x_lo: 2; x = x_hi * 2 + x_lo), y: 4, z: 4, core: 2. Of those that a mesh axis runs over, the one named last changes fastest.
Arguments:
- atm_state: bfloat16 [128, 512, 256], P('ty', 'tx'), may hold values from -6 to 6
- kernel_taps: float32 [3, 3, 256], replicated, may hold values from -2 to 2
- atm_gain: float32 [256], replicated, may hold values from 0.1 to 1.9
- atm_up: bfloat16 [256, 512], replicated, may hold values from -0.375 to 0.375
- atm_down: bfloat16 [512, 256], replicated, may hold values from -0.25 to 0.25
- couple_weight: bfloat16 [256, 128], replicated, may hold values from -0.375 to 0.375
- ocean_gain: float32 [128], replicated, may hold values from 0.1 to 1.9
- ocean_up: bfloat16 [128, 256], replicated, may hold values from -0.5 to 0.5
- ocean_down: bfloat16 [256, 128], replicated, may hold values from -0.375 to 0.375
- ocean_state: bfloat16 [32768, 32, 128], P(('tx', 'ty')), may hold values from -6 to 6
- land_mask: int32 [32768, 32], P(('tx', 'ty')), may hold values 0 or 1
- margin_cell: int32 [32768, 4, 32], P(('tx', 'ty')), may hold values from 0 to 511
- margin_area: float32 [32768, 4, 32], P(('tx', 'ty')), may hold values from 0.1 to 1
- owner_slot: int32 [32768], P(('tx', 'ty')), may hold values from 0 to 32767, as said below
- atm_cotangent: bfloat16 [128, 512, 256], P('ty', 'tx'), may hold values from -0.0234375 to 0.0234375
- ocean_cotangent: bfloat16 [32768, 32, 128], P(('tx', 'ty')), may hold values from -0.005859375 to 0.005859375
Outputs:
- atm_new: bfloat16 [128, 512, 256], P('ty', 'tx')
- ocean_new: bfloat16 [32768, 32, 128], P(('tx', 'ty'))
- grad_taps: float32 [3, 3, 256], replicated
- grad_atm_gain: float32 [256], replicated
- grad_atm_up: float32 [256, 512], replicated
- grad_atm_down: float32 [512, 256], replicated
- grad_couple: float32 [256, 128], replicated
- grad_ocean_gain: float32 [128], replicated
- grad_ocean_up: float32 [128, 256], replicated
- grad_ocean_down: float32 [256, 128], replicated
The draws below stay inside these ranges and needn't reach their ends.
Inputs may be any that keep to these rules, and one draw needn't show every extreme that they name: Every slot number appears exactly once. Geographic block b lies under atmosphere tile b // 256; it is owned by device owner_slot[b] // 256 of tx+ty, device numbers being 16 * (tx index) + ty index. The blocks of one tile go to every device, exactly 2 to each.
All inputs are finite; a program needn't handle non-finite values. No bound on the sum of `land_mask` on one device may be relied on, other than what follows from the above.
Results may differ from the reference program's by a relative error of at most 0.008.
Values may be sent and summed in bfloat16 or wider, within the bound.
A program may use at most 128 MiB of HBM per device.

```python
import math
import jax
import jax.numpy as jnp
from jax import lax

CA = 256
HA = 512
CO = 128
HO = 256
NOV = 4
BC = 32
AYD = 8
AXD = 64
BLK_DEV = 256
AY = 128
AX = 512
NB = 32768
N_TX = 8
N_TY = 16


def draw_owner_slot(key, part):
    key = jax.random.fold_in(key, 5)
    devices = N_TX * N_TY
    capacity = BLK_DEV // devices
    key_source, key_target = jax.random.split(key, 2)
    src_orders = jax.vmap(lambda inner_key: jax.random.permutation(inner_key, BLK_DEV))(jax.random.split(key_source, devices)).astype(jnp.int32)
    dst_orders = jax.vmap(lambda inner_key: jax.random.permutation(inner_key, BLK_DEV))(jax.random.split(key_target, devices)).astype(jnp.int32)
    source = jnp.arange(devices, dtype=jnp.int32)[:, None]
    position = jnp.arange(BLK_DEV, dtype=jnp.int32)[None, :]
    target = jnp.broadcast_to(position // capacity, (devices, BLK_DEV))
    local_index = position % capacity + source * capacity
    local_slot = dst_orders[target, local_index]
    slot_index = (target * BLK_DEV + local_slot).reshape(-1)
    geo_block = (source * BLK_DEV + src_orders).reshape(-1)
    return jnp.zeros((NB,), jnp.int32).at[geo_block].set(slot_index)


def touch_ends(drawn, rng, least, high):
    longest = drawn.shape.index(max(drawn.shape))
    spots = []
    for shift in (0, 1):
        where = [jax.random.randint(jax.random.fold_in(rng, axis), (), 0, length) for axis, length in enumerate(drawn.shape)]
        where[longest] = (where[longest] + shift) % drawn.shape[longest]
        spots.append(tuple(where))
    return drawn.at[spots[0]].set(least).at[spots[1]].set(high)


def levels(rng, dims, cuts, least, high):
    loudness, own = 1.0, jax.random.fold_in(rng, 6)
    for dim, parts in cuts:
        steps = jnp.exp(jax.random.uniform(jax.random.fold_in(own, dim), (parts,), jnp.float32, least / len(cuts), high / len(cuts)))
        loudness = loudness * jnp.repeat(steps, dims[dim] // parts).reshape([-1 if axis == dim else 1 for axis in range(len(dims))])
    return loudness


def bell_draw(rng, dims, spread, reach, shards=(), kind=jnp.bfloat16):
    values = spread * jax.random.normal(rng, dims, jnp.float32)
    if shards:
        values = values * levels(rng, dims, shards, -0.22, 0.18)
    return jnp.clip(values, -reach, reach).astype(kind)


def setup_inputs(seed: int = 0) -> dict:
    arg_keys = jax.random.split(jax.random.key(seed), 17)
    atm_state = bell_draw(arg_keys[0], (AY, AX, CA), 1.0, 6.0, ((0, 16), (1, 8)))
    kernel_taps = bell_draw(arg_keys[1], (3, 3, CA), 0.35, 2.0, (), jnp.float32)
    atm_gain = jnp.clip(1.0 + 0.18 * jax.random.normal(arg_keys[2], (CA,), jnp.float32), 0.1, 1.9)
    atm_up = bell_draw(arg_keys[3], (CA, HA), CA ** -0.5, 0.375)
    atm_down = bell_draw(arg_keys[4], (HA, CA), HA ** -0.5, 0.25)
    couple_weight = bell_draw(arg_keys[5], (CA, CO), CA ** -0.5, 0.375)
    ocean_gain = jnp.clip(1.0 + 0.18 * jax.random.normal(arg_keys[6], (CO,), jnp.float32), 0.1, 1.9)
    ocean_up = bell_draw(arg_keys[7], (CO, HO), CO ** -0.5, 0.5)
    ocean_down = bell_draw(arg_keys[8], (HO, CO), HO ** -0.5, 0.375)
    ocean_state = bell_draw(arg_keys[9], (NB, BC, CO), 1.0, 6.0, ((0, 128),))
    land_mask = touch_ends((jax.random.randint(arg_keys[10], (NB, BC), 0, 3) < 2).astype(jnp.int32), jax.random.fold_in(arg_keys[10], 1), 0, 1)
    margin_cell = touch_ends(jax.random.randint(arg_keys[11], (NB, NOV, BC), 0, AYD * AXD), jax.random.fold_in(arg_keys[11], 1), 0, (AYD * AXD) - 1).astype(jnp.int32)
    margin_area = jnp.clip(jnp.exp(math.log(1.0) - 2.3025851 * jax.random.uniform(arg_keys[12], (NB, NOV, BC), jnp.float32) ** levels(arg_keys[12], (NB, NOV, BC), ((0, 128),), -0.2, 0.2)), 0.1, 1.0)
    owner_slot = draw_owner_slot(jax.random.fold_in(arg_keys[16], 71), 0)
    atm_cotangent = bell_draw(arg_keys[14], (AY, AX, CA), (AY * AX) ** -0.5, 0.0234375, ((0, 16), (1, 8)))
    ocean_cotangent = bell_draw(arg_keys[15], (NB, BC, CO), (NB * BC) ** -0.5, 0.005859375, ((0, 128),))
    return {"atm_state": atm_state, "kernel_taps": kernel_taps, "atm_gain": atm_gain, "atm_up": atm_up, "atm_down": atm_down, "couple_weight": couple_weight, "ocean_gain": ocean_gain, "ocean_up": ocean_up, "ocean_down": ocean_down, "ocean_state": ocean_state, "land_mask": land_mask, "margin_cell": margin_cell, "margin_area": margin_area, "owner_slot": owner_slot, "atm_cotangent": atm_cotangent, "ocean_cotangent": ocean_cotangent}


EPS = 1e-06

def silu_grad(pre_act):
    logistic = jax.nn.sigmoid(pre_act)
    return logistic * (1.0 + pre_act * (1.0 - logistic))

def outer_sum(left, right):
    return lax.dot_general(left, right, (((0,), (0,)), ((), ())), preferred_element_type=jnp.float32)

def rms_norm(values, gain_vector):
    inverse_rms = lax.rsqrt(lax.optimization_barrier(jnp.mean(values * values, axis=-1, keepdims=True)) + EPS)
    unit_rows = values * inverse_rms
    return (unit_rows, inverse_rms, (unit_rows * gain_vector).astype(jnp.bfloat16))

def rms_back(normed_grad, unit_rows, inverse_rms, gain_vector):
    scaled = normed_grad * gain_vector
    gain_grad = lax.optimization_barrier(jnp.sum(normed_grad * unit_rows, axis=0))
    inner_mean = lax.optimization_barrier(jnp.mean(scaled * unit_rows, axis=-1, keepdims=True))
    return (inverse_rms * (scaled - unit_rows * inner_mean), gain_grad)

def stencil_sum(window, taps_array, height, breadth):
    running = jnp.zeros((height, breadth, window.shape[2]), jnp.float32)
    for lat_step in range(3):
        for lon_step in range(3):
            running = running + taps_array[lat_step, lon_step] * window[lat_step:lat_step + height, lon_step:lon_step + breadth]
    return running

def taps_grad(window, stencil_grad, height, breadth):
    rows_out = []
    for lat_step in range(3):
        for lon_step in range(3):
            rows_out.append(lax.optimization_barrier(jnp.sum(stencil_grad * window[lat_step:lat_step + height, lon_step:lon_step + breadth], axis=(0, 1))))
    return jnp.stack(rows_out).reshape(3, 3, -1)

def mlp_forward(normed, up_weight, down_weight):
    pre_act = jnp.dot(normed, up_weight, preferred_element_type=jnp.float32)
    activation = jax.nn.silu(pre_act).astype(jnp.bfloat16)
    return (pre_act, activation, jnp.dot(activation, down_weight, preferred_element_type=jnp.float32))

def mlp_backward(out_grad, normed, pre_act, activation, up_weight, down_weight):
    down_grad = outer_sum(activation, out_grad)
    act_grad = jnp.dot(out_grad, down_weight.T, preferred_element_type=jnp.float32)
    pre_grad = (act_grad * silu_grad(pre_act)).astype(jnp.bfloat16)
    up_grad = outer_sum(normed, pre_grad)
    normed_grad = jnp.dot(pre_grad, up_weight.T, preferred_element_type=jnp.float32)
    return (normed_grad, up_grad, down_grad)

def atm_forward(window, kernel_taps, atm_gain, atm_up, atm_down, height, breadth):
    channels = window.shape[2]
    stencil_rows = stencil_sum(window, kernel_taps, height, breadth).reshape(height * breadth, channels)
    unit_rows, inverse_rms, normed = rms_norm(stencil_rows, atm_gain)
    pre_act, activation, output = mlp_forward(normed, atm_up, atm_down)
    centre = window[1:1 + height, 1:1 + breadth].reshape(height * breadth, channels)
    fresh_rows = (centre.astype(jnp.float32) + output).astype(jnp.bfloat16)
    return (fresh_rows, (unit_rows, inverse_rms, normed, pre_act, activation))

def area_shares(margin_area):
    return margin_area / lax.optimization_barrier(jnp.sum(margin_area, axis=1, keepdims=True))

def regrid(fresh_rows, margin_cell, shares):
    picked = fresh_rows[margin_cell]
    return lax.optimization_barrier(jnp.sum(shares[..., None] * picked, axis=1)).astype(jnp.bfloat16)

def regrid_back(mixed_grad, margin_cell, shares, count_cells):
    weighted = shares[..., None] * mixed_grad[:, None]
    return jax.ops.segment_sum(weighted.reshape(-1, weighted.shape[-1]), margin_cell.reshape(-1), num_segments=count_cells)

def project(mixed_rows, couple_weight):
    flat_rows = mixed_rows.reshape(-1, mixed_rows.shape[2])
    result = jnp.dot(flat_rows, couple_weight, preferred_element_type=jnp.float32).astype(jnp.bfloat16)
    return result.reshape(mixed_rows.shape[0], mixed_rows.shape[1], -1)

def project_back(flux_grad, couple_weight):
    flat_rows = flux_grad.reshape(-1, flux_grad.shape[2])
    result = jnp.dot(flat_rows, couple_weight.T, preferred_element_type=jnp.float32).astype(jnp.bfloat16)
    return result.reshape(flux_grad.shape[0], flux_grad.shape[1], -1)

def ocean_step(ocean_rows, flux_own, land_mask, cotangent, ocean_gain, ocean_up, ocean_down):
    channels = ocean_rows.shape[2]
    flat_state = ocean_rows.reshape(-1, channels)
    total_rows = flat_state.astype(jnp.float32) + flux_own.reshape(-1, channels).astype(jnp.float32)
    unit_rows, inverse_rms, normed = rms_norm(total_rows, ocean_gain)
    pre_act, activation, output = mlp_forward(normed, ocean_up, ocean_down)
    wet_cells = land_mask.reshape(-1, 1)
    fresh_rows = (flat_state.astype(jnp.float32) + wet_cells.astype(jnp.float32) * output).astype(jnp.bfloat16)
    out_grad = cotangent.reshape(-1, channels) * wet_cells.astype(cotangent.dtype)
    normed_grad, up_grad, down_grad = mlp_backward(out_grad, normed, pre_act, activation, ocean_up, ocean_down)
    total_grad, gain_grad = rms_back(normed_grad, unit_rows, inverse_rms, ocean_gain)
    return (fresh_rows.reshape(ocean_rows.shape), total_grad.astype(jnp.bfloat16).reshape(ocean_rows.shape), gain_grad, up_grad, down_grad)

def reference(atm_state, kernel_taps, atm_gain, atm_up, atm_down, couple_weight, ocean_gain, ocean_up, ocean_down, ocean_state, land_mask, margin_cell, margin_area, owner_slot, atm_cotangent, ocean_cotangent):
    devices = N_TX * N_TY
    wrapped = jnp.concatenate([atm_state[:, -1:], atm_state, atm_state[:, :1]], axis=1)
    padded = jnp.pad(wrapped, ((1, 1), (0, 0), (0, 0)))
    tile_ids = jnp.arange(devices, dtype=jnp.int32)
    zero_index = jnp.zeros((), jnp.int32)

    def tile_corner(tile_id):
        return ((tile_id % N_TY * AYD).astype(jnp.int32), (tile_id // N_TY * AXD).astype(jnp.int32))

    def window_of(tile_id):
        lat_start, lon_start = tile_corner(tile_id)
        return lax.dynamic_slice(padded, (lat_start, lon_start, zero_index), (AYD + 2, AXD + 2, CA))

    def blocks_of(values_in, tile_id):
        return lax.dynamic_slice_in_dim(values_in, (tile_id * BLK_DEV).astype(jnp.int32), BLK_DEV, 0)

    def forward_tile(tile_id):
        fresh_rows, saved_parts = atm_forward(window_of(tile_id), kernel_taps, atm_gain, atm_up, atm_down, AYD, AXD)
        shares = area_shares(blocks_of(margin_area, tile_id))
        mixed_rows = regrid(fresh_rows, blocks_of(margin_cell, tile_id), shares)
        return (fresh_rows, mixed_rows, project(mixed_rows, couple_weight))
    fresh_tiles, mixed_tiles, flux_tiles = lax.map(forward_tile, tile_ids)
    atm_new = fresh_tiles.reshape(N_TX, N_TY, AYD, AXD, CA).transpose(1, 2, 0, 3, 4).reshape(AY, AX, CA)
    flux_geo = flux_tiles.reshape(NB, BC, CO)
    flux_own = jnp.zeros_like(flux_geo).at[owner_slot].set(flux_geo)

    def ocean_tile(tile_id):
        return ocean_step(blocks_of(ocean_state, tile_id), blocks_of(flux_own, tile_id), blocks_of(land_mask, tile_id), blocks_of(ocean_cotangent, tile_id), ocean_gain, ocean_up, ocean_down)
    ocean_tiles, grad_tiles, ocean_gain_parts, ocean_up_parts, ocean_down_parts = lax.map(ocean_tile, tile_ids)
    ocean_new = ocean_tiles.reshape(NB, BC, CO)
    flux_grad = grad_tiles.reshape(NB, BC, CO)[owner_slot]

    def backward_tile(tile_id):
        window = window_of(tile_id)
        fresh_rows, saved_parts = atm_forward(window, kernel_taps, atm_gain, atm_up, atm_down, AYD, AXD)
        unit_rows, inverse_rms, normed, pre_act, activation = saved_parts
        mixed_rows = mixed_tiles[tile_id]
        flux_part = blocks_of(flux_grad, tile_id)
        couple_grad = outer_sum(mixed_rows.reshape(-1, CA), flux_part.reshape(-1, CO))
        shares = area_shares(blocks_of(margin_area, tile_id))
        back_rows = regrid_back(project_back(flux_part, couple_weight), blocks_of(margin_cell, tile_id), shares, AYD * AXD)
        lat_start, lon_start = tile_corner(tile_id)
        cotangent = lax.dynamic_slice(atm_cotangent, (lat_start, lon_start, zero_index), (AYD, AXD, CA)).reshape(-1, CA)
        out_grad = (cotangent.astype(jnp.float32) + back_rows).astype(jnp.bfloat16)
        normed_grad, up_grad, down_grad = mlp_backward(out_grad, normed, pre_act, activation, atm_up, atm_down)
        stencil_grad, gain_grad = rms_back(normed_grad, unit_rows, inverse_rms, atm_gain)
        taps_part = taps_grad(window, stencil_grad.reshape(AYD, AXD, CA), AYD, AXD)
        return (taps_part, gain_grad, up_grad, down_grad, couple_grad)
    taps_parts, gain_parts, up_parts, down_parts, couple_parts = lax.map(backward_tile, tile_ids)
    return (atm_new, ocean_new, lax.optimization_barrier(jnp.sum(taps_parts, axis=0)), lax.optimization_barrier(jnp.sum(gain_parts, axis=0)), lax.optimization_barrier(jnp.sum(up_parts, axis=0)), lax.optimization_barrier(jnp.sum(down_parts, axis=0)), lax.optimization_barrier(jnp.sum(couple_parts, axis=0)), lax.optimization_barrier(jnp.sum(ocean_gain_parts, axis=0)), lax.optimization_barrier(jnp.sum(ocean_up_parts, axis=0)), lax.optimization_barrier(jnp.sum(ocean_down_parts, axis=0)))
```

```python
import functools

import jax
import jax.numpy as jnp
from jax import lax
from jax.experimental import pallas as pl
from jax.experimental.pallas import tpu as pltpu
from jax.sharding import PartitionSpec as P

EPS = 1e-06
MESH = pl.DeviceIdType.MESH
F32, BF16, I32 = jnp.float32, jnp.bfloat16, jnp.int32
DEVICES = 128
MIX = 37
UNMIX = pow(MIX, -1, DEVICES)
ROWS = 64
GROUP = 8
GROUPS = DEVICES // GROUP


def digits(tx, ty):
    return (tx // 4) * 2 + ty // 8, (ty // 2) % 4, tx % 4, ty % 2


def offset_device(me, step, sign):
    code = (step * MIX) % DEVICES
    x = (me[0] + 4 + sign * ((code // 2) % 4)) % 4
    y = (me[1] + 4 + sign * ((code // 8) % 4)) % 4
    z = (me[2] + 4 + sign * (code // 32)) % 4
    c = (me[3] + code) % 2
    return ((x // 2) * 4 + z, (x % 2) * 8 + y * 2 + c)


def sigmoid(v):
    return 0.5 * jnp.tanh(0.5 * v) + 0.5


def dot(a, b):
    return jnp.dot(a, b, preferred_element_type=F32)


def dot_t(a, b):
    return lax.dot_general(a, b, (((1,), (1,)), ((), ())), preferred_element_type=F32)


def t_dot(a, b):
    return lax.dot_general(a, b, (((0,), (0,)), ((), ())), preferred_element_type=F32)


def loop(n, f):
    lax.fori_loop(0, n, lambda i, c: (f(i), c)[1], 0)


def kernel(
    atm, taps, again, up, down, couple, ogain, oup, odown, mask, cells, shares, slots_out, acot, ostate_hbm, ocot_hbm,
    anew, onew_hbm, gtaps, gagain, gup, gdown, gcouple, gogain, goup, godown,
    ostate, ocot, wet, spread, flux_out, flux_in, back_out, back_in, onew, onew_arr, slots_in, inv_v, slots_s, inv_s,
    win, unit, inv_rms, normed, pre, act, gather, sgrad,
    edge_w, edge_e, halo_n, halo_s, halo_c,
    load_sem, halo_ssem, halo_rsem, slot_ssem, slot_rsem, flux_ssem, flux_rsem, back_ssem, back_rsem, misc_sem,
):
    tx, ty = lax.axis_index("tx"), lax.axis_index("ty")
    me = digits(tx, ty)
    height, breadth = atm.shape[0], atm.shape[1]
    n_cells = height * breadth

    barrier = pltpu.get_barrier_semaphore()
    loads = [
        pltpu.make_async_copy(ostate_hbm, ostate, load_sem.at[0]),
        pltpu.make_async_copy(ocot_hbm, ocot, load_sem.at[1]),
    ]
    for load in loads:
        load.start()

    def greet(i):
        pl.semaphore_signal(barrier, inc=1, device_id=offset_device(me, i + 1, 1), device_id_type=MESH)

    loop(DEVICES - 1, greet)

    edge_w[...] = jnp.zeros_like(edge_w)
    edge_e[...] = jnp.zeros_like(edge_e)

    def own_rows(y):
        win[y + 1, 8 : 8 + breadth, :] = atm[y].astype(F32)

    loop(height, own_rows)
    west = jnp.concatenate([win[y + 1, 8:9, :] for y in range(height)], axis=0)
    east = jnp.concatenate([win[y + 1, 7 + breadth : 8 + breadth, :] for y in range(height)], axis=0)
    nothing = jnp.zeros_like(west)
    edge_w[...] = jnp.concatenate([west, nothing], axis=0).astype(BF16)
    edge_e[...] = jnp.concatenate([east, nothing], axis=0).astype(BF16)

    ones = jnp.ones((mask.shape[1], 128), BF16)

    def wet_rows(i):
        rows = lax.broadcasted_iota(I32, (512, 16), 0)
        cols = lax.broadcasted_iota(I32, (512, 16), 1)
        pick = (rows // 32 == cols).astype(F32).astype(BF16)
        wide = dot(pick, mask[pl.ds(pl.multiple_of(i * 16, 16), 16), :].astype(F32).astype(BF16))
        r2 = lax.broadcasted_iota(I32, wide.shape, 0)
        c2 = lax.broadcasted_iota(I32, wide.shape, 1)
        wide = jnp.where(r2 % 32 == c2, wide, 0.0).astype(BF16)
        wet[pl.ds(pl.multiple_of(i * 16, 16), 16)] = dot(wide, ones).astype(BF16).reshape(16, 32, 128)

    loop(16, wet_rows)

    def spread_columns(i):
        here = pl.ds(pl.multiple_of(i * 128, 128), 128)
        rows = lax.broadcasted_iota(I32, (n_cells, 128), 0)
        total = jnp.where(rows == cells[0:1, here], shares[0:1, here], 0.0)
        for k in range(1, 4):
            total = total + jnp.where(rows == cells[k : k + 1, here], shares[k : k + 1, here], 0.0)
        spread[:, here] = total.astype(BF16)

    loop(32, spread_columns)

    pl.semaphore_wait(barrier, DEVICES - 1)

    te, tw = (tx + 1) % 8, (tx + 7) % 8
    north, south = ty > 0, ty < 15

    def halo(i, src, dst, dx, dy):
        return pltpu.make_async_remote_copy(
            src, dst, halo_ssem.at[i], halo_rsem.at[i], device_id=(dx, dy), device_id_type=MESH
        )

    copies = [
        (south, halo(0, atm.at[height - 1], halo_n, tx, (ty + 1) % 16)),
        (north, halo(1, atm.at[0], halo_s, tx, (ty + 15) % 16)),
        (None, halo(2, edge_e, halo_c.at[0], te, ty)),
        (None, halo(3, edge_w, halo_c.at[1], tw, ty)),
        (south, halo(4, edge_e, halo_c.at[2], te, (ty + 1) % 16)),
        (south, halo(5, edge_w, halo_c.at[3], tw, (ty + 1) % 16)),
        (north, halo(6, edge_e, halo_c.at[4], te, (ty + 15) % 16)),
        (north, halo(7, edge_w, halo_c.at[5], tw, (ty + 15) % 16)),
    ]

    def when(cond, f):
        if cond is None:
            f()
        else:
            pl.when(cond)(f)

    for cond, copy in copies:
        when(cond, copy.start)

    def slot_copy(step, sign):
        return pltpu.make_async_remote_copy(
            slots_out.at[step], slots_in.at[step], slot_ssem, slot_rsem,
            device_id=offset_device(me, step, sign), device_id_type=MESH,
        )

    loop(DEVICES - 1, lambda i: slot_copy(i + 1, 1).start())
    slots_in[0] = slots_out[0]

    loop(32, lambda i: spread_columns(i + 32))

    for cond, copy in copies:
        when(cond, copy.wait_send)
    receives = [north, south, None, None, north, north, south, south]
    for cond, (_, copy) in zip(receives, copies):
        when(cond, copy.wait_recv)

    @pl.when(north)
    def _():
        win[0, 8 : 8 + breadth, :] = halo_n[...].astype(F32)
        win[0, 7:8, :] = halo_c[2].astype(F32)[height - 1 : height]
        win[0, 8 + breadth : 9 + breadth, :] = halo_c[3].astype(F32)[height - 1 : height]

    @pl.when(jnp.logical_not(north))
    def _():
        win[0] = jnp.zeros(win.shape[1:], F32)

    @pl.when(south)
    def _():
        win[height + 1, 8 : 8 + breadth, :] = halo_s[...].astype(F32)
        win[height + 1, 7:8, :] = halo_c[4].astype(F32)[0:1]
        win[height + 1, 8 + breadth : 9 + breadth, :] = halo_c[5].astype(F32)[0:1]

    @pl.when(jnp.logical_not(south))
    def _():
        win[height + 1] = jnp.zeros(win.shape[1:], F32)

    west, east = halo_c[0].astype(F32), halo_c[1].astype(F32)
    for y in range(height):
        win[y + 1, 7:8, :] = west[y : y + 1]
        win[y + 1, 8 + breadth : 9 + breadth, :] = east[y : y + 1]

    def stencil_row(y):
        total = jnp.zeros((breadth, 256), F32)
        for a in range(3):
            for b in range(3):
                total = total + taps[3 * a + b : 3 * a + b + 1, :] * win[y + a, 7 + b : 7 + b + breadth, :]
        inv = lax.rsqrt(jnp.mean(total * total, axis=-1, keepdims=True) + EPS)
        here = pl.ds(pl.multiple_of(y * breadth, breadth), breadth)
        u = total * inv
        unit[here, :] = u
        inv_rms[here, :] = jnp.broadcast_to(inv, (breadth, 128))
        normed[here, :] = (u * again[...]).astype(BF16)

    loop(height, stencil_row)

    def atm_mlp(i):
        here = pl.ds(pl.multiple_of(i * 128, 128), 128)
        v = dot(normed[here, :], up[...])
        pre[here, :] = v
        a = (v * sigmoid(v)).astype(BF16)
        act[here, :] = a
        old = atm[pl.ds(i * 2, 2)].reshape(128, 256).astype(F32)
        anew[pl.ds(i * 2, 2)] = (old + dot(a, down[...])).astype(BF16).reshape(2, breadth, 256)

    loop(4, atm_mlp)
    fresh = anew[...].reshape(n_cells, 256)
    coupled = dot(fresh, couple[...]).astype(BF16)
    gather[...] = coupled

    def flux_copy(step, sign):
        here = pl.ds(pl.multiple_of(step * ROWS, ROWS), ROWS)
        return pltpu.make_async_remote_copy(
            flux_out.at[here], flux_in.at[here], flux_ssem, flux_rsem.at[step // GROUP],
            device_id=offset_device(me, step, sign), device_id_type=MESH,
        )

    def flux_chunk(i):
        here = pl.ds(pl.multiple_of(i * 256, 256), 256)
        flux_out[here, :] = t_dot(spread[:, here], gather[...]).astype(BF16)
        for j in range(4):
            step = i * 4 + j
            if j == 0:
                pl.when(step > 0)(lambda: flux_copy(step, 1).start())
            else:
                flux_copy(step, 1).start()

    loop(DEVICES // 4, flux_chunk)
    flux_in[0:ROWS, :] = flux_out[0:ROWS, :]

    rest = slots_in.at[pl.ds(1, DEVICES - 1)]
    slots = pltpu.make_async_remote_copy(
        rest, rest, slot_ssem, slot_rsem, device_id=offset_device(me, 1, 1), device_id_type=MESH
    )
    slots.wait_recv()
    slots.wait_send()
    slot_rows = slots_in[...].reshape(DEVICES, 128)
    lane = lax.broadcasted_iota(I32, (DEVICES, 256), 1)
    step_row = lax.broadcasted_iota(I32, (DEVICES, 256), 0)
    found = jnp.where(slot_rows[:, 0:1] == lane, 2 * step_row, 0) + jnp.where(
        slot_rows[:, 1:2] == lane, 2 * step_row + 1, 0
    )
    inv_v[...] = jnp.broadcast_to(jnp.max(found, axis=0, keepdims=True), inv_v.shape)
    to_scalar = [
        pltpu.make_async_copy(slots_in, slots_s, misc_sem.at[0]),
        pltpu.make_async_copy(inv_v, inv_s, misc_sem.at[1]),
    ]
    for copy in to_scalar:
        copy.start()
    for copy in to_scalar:
        copy.wait()
    for load in loads:
        load.wait()

    goup[...] = jnp.zeros_like(goup)
    godown[...] = jnp.zeros_like(godown)
    gogain[...] = jnp.zeros_like(gogain)

    def back_copy(step, sign):
        here = pl.ds(pl.multiple_of(step * ROWS, ROWS), ROWS)
        return pltpu.make_async_remote_copy(
            back_out.at[here], back_in.at[here], back_ssem, back_rsem.at[step // GROUP],
            device_id=offset_device(me, step, sign), device_id_type=MESH,
        )

    def wait_group(g, buf, ssem, rsem):
        def first():
            some = buf.at[pl.ds(ROWS, (GROUP - 1) * ROWS)]
            pltpu.make_async_remote_copy(
                some, some, ssem, rsem.at[0], device_id=offset_device(me, 1, 1), device_id_type=MESH
            ).wait_recv()

        def later():
            some = buf.at[pl.ds(pl.multiple_of(g * (GROUP * ROWS), GROUP * ROWS), GROUP * ROWS)]
            pltpu.make_async_remote_copy(
                some, some, ssem, rsem.at[g], device_id=offset_device(me, 1, 1), device_id_type=MESH
            ).wait_recv()

        pl.when(g == 0)(first)
        pl.when(g > 0)(later)

    def ocean_group(g):
        wait_group(g, flux_in, flux_ssem, flux_rsem)
        here = pl.ds(pl.multiple_of(g * (GROUP * ROWS), GROUP * ROWS), GROUP * ROWS)
        slot = [slots_s[g * GROUP + j // 2, 0, j % 2] & 255 for j in range(2 * GROUP)]
        state = jnp.concatenate([ostate[s] for s in slot], axis=0).astype(F32)
        wets = jnp.concatenate([wet[s] for s in slot], axis=0)
        out_grad = jnp.concatenate([ocot[s] for s in slot], axis=0) * wets
        total = state + flux_in[here, :].astype(F32)
        inv = lax.rsqrt(jnp.mean(total * total, axis=-1, keepdims=True) + EPS)
        u = total * inv
        nrm = (u * ogain[...]).astype(BF16)
        v = dot(nrm, oup[...])
        s = sigmoid(v)
        a = (v * s).astype(BF16)
        onew_arr[pl.ds(g * (2 * GROUP), 2 * GROUP)] = (
            (state + wets.astype(F32) * dot(a, odown[...])).astype(BF16).reshape(2 * GROUP, 32, 128)
        )
        godown[...] += t_dot(a, out_grad)
        pg = (dot_t(out_grad, odown[...]) * (s * (1.0 + v * (1.0 - s)))).astype(BF16)
        goup[...] += t_dot(nrm, pg)
        ng = dot_t(pg, oup[...])
        gogain[...] += jnp.sum(ng * u, axis=0, keepdims=True)
        gg = ng * ogain[...]
        tg = inv * (gg - u * jnp.mean(gg * u, axis=-1, keepdims=True))
        back_out[here, :] = tg.astype(BF16)

        def send(j):
            step = g * GROUP + j
            pl.when(step > 0)(lambda: back_copy(step, -1).start())

        loop(GROUP, send)

    loop(GROUPS, ocean_group)
    back_in[0:ROWS, :] = back_out[0:ROWS, :]

    def place(i):
        for j in range(8):
            onew[i * 8 + j] = onew_arr[inv_s[0, i * 8 + j] & 255]

    loop(32, place)
    store = pltpu.make_async_copy(onew, onew_hbm, misc_sem.at[2])
    store.start()

    sgrad[:, 0:128] = jnp.zeros((n_cells, 128), F32)

    def back_group(g):
        wait_group(g, back_in, back_ssem, back_rsem)
        here = pl.ds(pl.multiple_of(g * (GROUP * ROWS), GROUP * ROWS), GROUP * ROWS)
        sgrad[:, 0:128] += dot(spread[:, here], back_in[here, :])

    loop(GROUPS, back_group)
    gathered = sgrad[:, 0:128].astype(BF16)
    gather[...] = gathered
    gcouple[...] = t_dot(anew[...].reshape(n_cells, 256), gathered)

    gup[...] = jnp.zeros_like(gup)
    gdown[...] = jnp.zeros_like(gdown)
    gagain[...] = jnp.zeros_like(gagain)
    gtaps[...] = jnp.zeros_like(gtaps)

    def atm_back(i):
        here = pl.ds(pl.multiple_of(i * 128, 128), 128)
        cot = acot[pl.ds(i * 2, 2)].reshape(128, 256).astype(F32)
        out_grad = (cot + dot_t(gather[here, :], couple[...])).astype(BF16)
        gdown[...] += t_dot(act[here, :], out_grad)
        v = pre[here, :]
        s = sigmoid(v)
        pg = (dot_t(out_grad, down[...]) * (s * (1.0 + v * (1.0 - s)))).astype(BF16)
        gup[...] += t_dot(normed[here, :], pg)
        ng = dot_t(pg, up[...])
        u = unit[here, :]
        gagain[...] += jnp.sum(ng * u, axis=0, keepdims=True)
        gg = ng * again[...]
        sgrad[here, :] = inv_rms[here, 0:1] * (gg - u * jnp.mean(gg * u, axis=-1, keepdims=True))

    loop(4, atm_back)

    def taps_row(y):
        sg = sgrad[pl.ds(pl.multiple_of(y * breadth, breadth), breadth), :]
        for a in range(3):
            for b in range(3):
                gtaps[3 * a + b : 3 * a + b + 1, :] += jnp.sum(
                    sg * win[y + a, 7 + b : 7 + b + breadth, :], axis=0, keepdims=True
                )

    loop(height, taps_row)

    sent = flux_out.at[pl.ds(ROWS, (DEVICES - 1) * ROWS)]
    pltpu.make_async_remote_copy(
        sent, sent, flux_ssem, flux_rsem.at[0], device_id=offset_device(me, 1, 1), device_id_type=MESH
    ).wait_send()
    sent = back_out.at[pl.ds(ROWS, (DEVICES - 1) * ROWS)]
    pltpu.make_async_remote_copy(
        sent, sent, back_ssem, back_rsem.at[0], device_id=offset_device(me, 1, 1), device_id_type=MESH
    ).wait_send()
    store.wait()


def body(
    atm_state, kernel_taps, atm_gain, atm_up, atm_down, couple_weight, ocean_gain, ocean_up, ocean_down,
    ocean_state, land_mask, margin_cell, margin_area, owner_slot, atm_cotangent, ocean_cotangent,
):
    height, breadth, channels = atm_state.shape
    blocks = ocean_state.shape[0]
    n_rows = blocks * 32

    target = owner_slot // blocks
    mine = digits(lax.axis_index("tx"), lax.axis_index("ty"))
    theirs = digits(target // 16, target % 16)
    dx, dy, dz, dc = [(t - m) % n for t, m, n in zip(theirs, mine, (4, 4, 4, 2))]
    step = ((((dz * 4 + dy) * 4 + dx) * 2 + dc) * UNMIX) % DEVICES
    index = jnp.arange(blocks, dtype=I32)
    earlier = (target[:, None] == target[None, :]) & (index[:, None] < index[None, :])
    place = 2 * step + jnp.sum(earlier.astype(I32), axis=0)
    order = (place[None, :] == index[:, None]).astype(F32)
    shares = margin_area / jnp.sum(margin_area, axis=1, keepdims=True)
    table = jnp.concatenate(
        [
            margin_cell.reshape(blocks, -1).astype(F32),
            shares.reshape(blocks, -1),
            (owner_slot % blocks).astype(F32)[:, None],
        ],
        axis=1,
    )
    table = jnp.dot(order, table, precision=lax.Precision.HIGHEST, preferred_element_type=F32)
    cells = jnp.round(table[:, :128]).astype(I32).reshape(blocks, 4, 32).transpose(1, 0, 2).reshape(4, n_rows)
    shares = table[:, 128:256].reshape(blocks, 4, 32).transpose(1, 0, 2).reshape(4, n_rows)
    slots = jnp.round(table[:, 256]).astype(I32).reshape(DEVICES, 1, 2)
    slots = jnp.pad(slots, ((0, 0), (0, 0), (0, 126)))

    vmem, any_ = pl.BlockSpec(memory_space=pltpu.VMEM), pl.BlockSpec(memory_space=pl.ANY)
    out_shape = [
        jax.ShapeDtypeStruct((height, breadth, channels), BF16),
        jax.ShapeDtypeStruct((blocks, 32, 128), BF16),
        jax.ShapeDtypeStruct((9, 256), F32),
        jax.ShapeDtypeStruct((1, 256), F32),
        jax.ShapeDtypeStruct((256, 512), F32),
        jax.ShapeDtypeStruct((512, 256), F32),
        jax.ShapeDtypeStruct((256, 128), F32),
        jax.ShapeDtypeStruct((1, 128), F32),
        jax.ShapeDtypeStruct((128, 256), F32),
        jax.ShapeDtypeStruct((256, 128), F32),
    ]
    block = lambda: pltpu.VMEM((blocks, 32, 128), BF16)
    flat = lambda: pltpu.VMEM((n_rows, 128), BF16)
    n_cells = height * breadth
    scratch = [
        block(), block(), block(),
        pltpu.VMEM((n_cells, n_rows), BF16),
        flat(), flat(), flat(), flat(),
        block(), block(),
        pltpu.VMEM((DEVICES, 1, 128), I32),
        pltpu.VMEM((8, 256), I32),
        pltpu.SMEM((DEVICES, 1, 128), I32),
        pltpu.SMEM((8, 256), I32),
        pltpu.VMEM((height + 2, breadth + 16, channels), F32),
        pltpu.VMEM((n_cells, 256), F32),
        pltpu.VMEM((n_cells, 128), F32),
        pltpu.VMEM((n_cells, 256), BF16),
        pltpu.VMEM((n_cells, 512), F32),
        pltpu.VMEM((n_cells, 512), BF16),
        pltpu.VMEM((n_cells, 128), BF16),
        pltpu.VMEM((n_cells, 256), F32),
        pltpu.VMEM((16, channels), BF16),
        pltpu.VMEM((16, channels), BF16),
        pltpu.VMEM((breadth, channels), BF16),
        pltpu.VMEM((breadth, channels), BF16),
        pltpu.VMEM((6, 16, channels), BF16),
        pltpu.SemaphoreType.DMA((2,)),
        pltpu.SemaphoreType.DMA((8,)),
        pltpu.SemaphoreType.DMA((8,)),
        pltpu.SemaphoreType.DMA,
        pltpu.SemaphoreType.DMA,
        pltpu.SemaphoreType.DMA,
        pltpu.SemaphoreType.DMA((GROUPS,)),
        pltpu.SemaphoreType.DMA,
        pltpu.SemaphoreType.DMA((GROUPS,)),
        pltpu.SemaphoreType.DMA((3,)),
    ]
    anew, onew, gtaps, *grads = pl.pallas_call(
        kernel,
        out_shape=out_shape,
        in_specs=[vmem] * 14 + [any_] * 2,
        out_specs=[vmem, any_] + [vmem] * 8,
        scratch_shapes=scratch,
        compiler_params=pltpu.CompilerParams(
            collective_id=0, has_side_effects=True, vmem_limit_bytes=56 * 1024 * 1024
        ),
    )(
        atm_state, kernel_taps.reshape(9, channels), atm_gain.reshape(1, -1), atm_up, atm_down, couple_weight,
        ocean_gain.reshape(1, -1), ocean_up, ocean_down, land_mask, cells, shares, slots,
        atm_cotangent, ocean_state, ocean_cotangent,
    )
    sums = lax.psum((gtaps, *grads), ("tx", "ty"))
    return (
        anew, onew, sums[0].reshape(3, 3, channels), sums[1].reshape(-1), sums[2], sums[3], sums[4],
        sums[5].reshape(-1), sums[6], sums[7],
    )


def solution(mesh):
    both = ("tx", "ty")
    return jax.shard_map(
        body,
        mesh=mesh,
        in_specs=(P("ty", "tx", None),) + (P(),) * 8 + (
            P(both, None, None), P(both, None), P(both, None, None), P(both, None, None), P(both),
            P("ty", "tx", None), P(both, None, None),
        ),
        out_specs=(P("ty", "tx", None), P(both, None, None)) + (P(),) * 8,
        check_vma=False,
    )
```

```python
import functools

import jax
import jax.numpy as jnp
from jax import lax
from jax.experimental import pallas as pl
from jax.experimental.pallas import tpu as pltpu
from jax.sharding import PartitionSpec as P

EPS = 1e-06
MESH = pl.DeviceIdType.MESH
F32, BF16, I32 = jnp.float32, jnp.bfloat16, jnp.int32
DEVICES = 128
MIX = 37
UNMIX = pow(MIX, -1, DEVICES)
ROWS = 64
GROUP = 8
GROUPS = DEVICES // GROUP
PIECE = 32
OWNERS = 89
AT_OUP, AT_ODOWN, AT_COUPLE, AT_SMALL, AT_DOWN, AT_UP = 0, 256, 512, 768, 800, 1824
PACKED = OWNERS * PIECE


def digits(tx, ty):
    return (tx // 4) * 2 + ty // 8, (ty // 2) % 4, tx % 4, ty % 2


def offset_device(me, step, sign):
    code = (step * MIX) % DEVICES
    x = (me[0] + 4 + sign * ((code // 2) % 4)) % 4
    y = (me[1] + 4 + sign * ((code // 8) % 4)) % 4
    z = (me[2] + 4 + sign * (code // 32)) % 4
    c = (me[3] + code) % 2
    return ((x // 2) * 4 + z, (x % 2) * 8 + y * 2 + c)


def owner_rank(tx, ty):
    return ((tx * 16 + ty) * MIX) % DEVICES


def sigmoid(v):
    return 0.5 * jnp.tanh(0.5 * v) + 0.5


def dot(a, b):
    return jnp.dot(a, b, preferred_element_type=F32)


def dot_t(a, b):
    return lax.dot_general(a, b, (((1,), (1,)), ((), ())), preferred_element_type=F32)


def t_dot(a, b):
    return lax.dot_general(a, b, (((0,), (0,)), ((), ())), preferred_element_type=F32)


def loop(n, f):
    lax.fori_loop(0, n, lambda i, c: (f(i), c)[1], 0)


def kernel(
    atm, taps, again, up, down, couple, ogain, oup, odown, mask, margin_cell, margin_area, owner, acot, ostate_hbm, ocot_hbm,
    anew, onew_hbm, inv_v, packed_hbm,
    ostate, ocot, wet, cells, shares, spread, flux_out, flux_in, back_out, back_in, onew_arr, slots_out, slots_in, slots_s,
    win, unit, inv_rms, normed, pre, act, gather, sgrad,
    gtaps, gagain, gup, gdown, gogain, goup, godown, small, partial, pieces, packed,
    edge_w, edge_e, halo_n, halo_s, halo_c,
    load_sem, halo_ssem, halo_rsem, slot_ssem, slot_rsem, flux_ssem, flux_rsem, back_ssem, back_rsem, misc_sem,
    part_ssem, part_rsem, sum_ssem, sum_rsem,
):
    tx, ty = lax.axis_index("tx"), lax.axis_index("ty")
    me = digits(tx, ty)
    height, breadth = atm.shape[0], atm.shape[1]
    n_cells = height * breadth

    barrier = pltpu.get_barrier_semaphore()
    loads = [
        pltpu.make_async_copy(ostate_hbm, ostate, load_sem.at[0]),
        pltpu.make_async_copy(ocot_hbm, ocot, load_sem.at[1]),
    ]
    for load in loads:
        load.start()

    def greet(i):
        pl.semaphore_signal(barrier, inc=1, device_id=offset_device(me, i + 1, 1), device_id_type=MESH)

    loop(DEVICES - 1, greet)

    edge_w[...] = jnp.zeros_like(edge_w)
    edge_e[...] = jnp.zeros_like(edge_e)

    def own_rows(y):
        win[y + 1, 8 : 8 + breadth, :] = atm[y].astype(F32)

    loop(height, own_rows)
    west = jnp.concatenate([win[y + 1, 8:9, :] for y in range(height)], axis=0)
    east = jnp.concatenate([win[y + 1, 7 + breadth : 8 + breadth, :] for y in range(height)], axis=0)
    nothing = jnp.zeros_like(west)
    edge_w[...] = jnp.concatenate([west, nothing], axis=0).astype(BF16)
    edge_e[...] = jnp.concatenate([east, nothing], axis=0).astype(BF16)

    slot = owner[...]
    t_tx, t_ty = slot >> 12, (slot >> 8) & 15
    theirs = ((t_tx >> 2) * 2 + (t_ty >> 3), (t_ty >> 1) & 3, t_tx & 3, t_ty & 1)
    dx, dy, dz, dc = [(t - m + n) & (n - 1) for t, m, n in zip(theirs, me, (4, 4, 4, 2))]
    step = ((((dz * 4 + dy) * 4 + dx) * 2 + dc) * UNMIX) & (DEVICES - 1)
    blocks = slot.shape[1]
    square = jnp.broadcast_to(step, (blocks, blocks))
    first = lax.broadcasted_iota(I32, square.shape, 0)
    second = lax.broadcasted_iota(I32, square.shape, 1)
    same = (square.astype(F32).T == square.astype(F32)) & (first < second)
    place = 2 * step + jnp.sum(same.astype(F32), axis=0, keepdims=True).astype(I32)

    steps = lax.broadcasted_iota(I32, (DEVICES, blocks), 0)
    local = jnp.broadcast_to(slot & (blocks - 1), (DEVICES, blocks))
    lanes = lax.broadcasted_iota(I32, (DEVICES, 128), 1)
    pair = [
        jnp.sum(jnp.where(place == 2 * steps + j, local, 0).astype(F32), axis=1, keepdims=True).astype(I32)
        for j in range(2)
    ]
    slots_out[...] = jnp.where(lanes == 0, pair[0], pair[1])

    area = margin_area[...]
    share = (area / jnp.sum(area, axis=0, keepdims=True)).reshape(128, blocks).astype(BF16)
    cell = margin_cell[...].reshape(128, blocks)
    high, low = (cell >> 4).astype(F32).astype(BF16), (cell & 15).astype(F32).astype(BF16)
    quads = lax.broadcasted_iota(I32, (blocks // 4, blocks), 0)
    lane_block = lax.broadcasted_iota(I32, (blocks // 4, 128), 1) // 32
    got_share = [jnp.zeros((blocks // 4, 128), F32)] * 4
    got_cell = [jnp.zeros((blocks // 4, 128), F32)] * 4
    for j in range(4):
        pick = (place == 4 * quads + j).astype(F32).astype(BF16)
        one_share = dot_t(pick, share)
        one_cell = 16.0 * dot_t(pick, high) + dot_t(pick, low)
        for k in range(4):
            turn = (32 * (j - k)) % 128
            here = lane_block == j
            got_share[k] = jnp.where(here, pltpu.roll(one_share, turn, 1) if turn else one_share, got_share[k])
            got_cell[k] = jnp.where(here, pltpu.roll(one_cell, turn, 1) if turn else one_cell, got_cell[k])
    for k in range(4):
        shares[k] = got_share[k]
        cells[k] = got_cell[k].astype(I32)

    ones = jnp.ones((32, 128), BF16)
    wet_rows_of = mask[...].astype(F32).astype(BF16)

    def wet_rows(i):
        rows = lax.broadcasted_iota(I32, (512, blocks), 0)
        cols = lax.broadcasted_iota(I32, (512, blocks), 1)
        pick = (rows // 32 + i * 16 == cols).astype(F32).astype(BF16)
        wide = dot_t(pick, wet_rows_of)
        r2 = lax.broadcasted_iota(I32, wide.shape, 0)
        c2 = lax.broadcasted_iota(I32, wide.shape, 1)
        wide = jnp.where(r2 % 32 == c2, wide, 0.0).astype(BF16)
        wet[pl.ds(pl.multiple_of(i * 16, 16), 16)] = dot(wide, ones).astype(BF16).reshape(16, 32, 128)

    def spread_columns(i):
        here = pl.ds(pl.multiple_of(i * 128, 128), 128)
        rows = lax.broadcasted_iota(I32, (n_cells, 128), 0)
        row = pl.ds(i, 1)
        total = jnp.where(rows == cells[0, row, :], shares[0, row, :], 0.0)
        for k in range(1, 4):
            total = total + jnp.where(rows == cells[k, row, :], shares[k, row, :], 0.0)
        spread[:, here] = total.astype(BF16)

    pl.semaphore_wait(barrier, DEVICES - 1)

    te, tw = (tx + 1) % 8, (tx + 7) % 8
    north, south = ty > 0, ty < 15

    def halo(i, src, dst, dx, dy):
        return pltpu.make_async_remote_copy(
            src, dst, halo_ssem.at[i], halo_rsem.at[i], device_id=(dx, dy), device_id_type=MESH
        )

    copies = [
        (south, halo(0, atm.at[height - 1], halo_n, tx, (ty + 1) % 16)),
        (north, halo(1, atm.at[0], halo_s, tx, (ty + 15) % 16)),
        (None, halo(2, edge_e, halo_c.at[0], te, ty)),
        (None, halo(3, edge_w, halo_c.at[1], tw, ty)),
        (south, halo(4, edge_e, halo_c.at[2], te, (ty + 1) % 16)),
        (south, halo(5, edge_w, halo_c.at[3], tw, (ty + 1) % 16)),
        (north, halo(6, edge_e, halo_c.at[4], te, (ty + 15) % 16)),
        (north, halo(7, edge_w, halo_c.at[5], tw, (ty + 15) % 16)),
    ]

    def when(cond, f):
        if cond is None:
            f()
        else:
            pl.when(cond)(f)

    for cond, copy in copies:
        when(cond, copy.start)

    def slot_copy(step, sign):
        return pltpu.make_async_remote_copy(
            slots_out.at[pl.ds(step, 1)], slots_in.at[pl.ds(step, 1)], slot_ssem, slot_rsem,
            device_id=offset_device(me, step, sign), device_id_type=MESH,
        )

    loop(DEVICES - 1, lambda i: slot_copy(i + 1, 1).start())
    slots_in[0:1, :] = slots_out[0:1, :]

    loop(64, spread_columns)
    loop(16, wet_rows)

    for cond, copy in copies:
        when(cond, copy.wait_send)
    receives = [north, south, None, None, north, north, south, south]
    for cond, (_, copy) in zip(receives, copies):
        when(cond, copy.wait_recv)

    @pl.when(north)
    def _():
        win[0, 8 : 8 + breadth, :] = halo_n[...].astype(F32)
        win[0, 7:8, :] = halo_c[2].astype(F32)[height - 1 : height]
        win[0, 8 + breadth : 9 + breadth, :] = halo_c[3].astype(F32)[height - 1 : height]

    @pl.when(jnp.logical_not(north))
    def _():
        win[0] = jnp.zeros(win.shape[1:], F32)

    @pl.when(south)
    def _():
        win[height + 1, 8 : 8 + breadth, :] = halo_s[...].astype(F32)
        win[height + 1, 7:8, :] = halo_c[4].astype(F32)[0:1]
        win[height + 1, 8 + breadth : 9 + breadth, :] = halo_c[5].astype(F32)[0:1]

    @pl.when(jnp.logical_not(south))
    def _():
        win[height + 1] = jnp.zeros(win.shape[1:], F32)

    west, east = halo_c[0].astype(F32), halo_c[1].astype(F32)
    for y in range(height):
        win[y + 1, 7:8, :] = west[y : y + 1]
        win[y + 1, 8 + breadth : 9 + breadth, :] = east[y : y + 1]

    def stencil_row(y):
        total = jnp.zeros((breadth, 256), F32)
        for a in range(3):
            for b in range(3):
                total = total + taps[a, b : b + 1, :] * win[y + a, 7 + b : 7 + b + breadth, :]
        inv = lax.rsqrt(jnp.mean(total * total, axis=-1, keepdims=True) + EPS)
        here = pl.ds(pl.multiple_of(y * breadth, breadth), breadth)
        u = total * inv
        unit[here, :] = u
        inv_rms[here, :] = jnp.broadcast_to(inv, (breadth, 128))
        normed[here, :] = (u * again[...]).astype(BF16)

    loop(height, stencil_row)

    def atm_mlp(i):
        here = pl.ds(pl.multiple_of(i * 128, 128), 128)
        v = dot(normed[here, :], up[...])
        pre[here, :] = v
        a = (v * sigmoid(v)).astype(BF16)
        act[here, :] = a
        old = atm[pl.ds(i * 2, 2)].reshape(128, 256).astype(F32)
        anew[pl.ds(i * 2, 2)] = (old + dot(a, down[...])).astype(BF16).reshape(2, breadth, 256)

    loop(4, atm_mlp)
    fresh = anew[...].reshape(n_cells, 256)
    coupled = dot(fresh, couple[...]).astype(BF16)
    gather[...] = coupled

    def flux_copy(step, sign):
        here = pl.ds(pl.multiple_of(step * ROWS, ROWS), ROWS)
        return pltpu.make_async_remote_copy(
            flux_out.at[here], flux_in.at[here], flux_ssem, flux_rsem.at[step // GROUP],
            device_id=offset_device(me, step, sign), device_id_type=MESH,
        )

    def flux_chunk(i):
        here = pl.ds(pl.multiple_of(i * 256, 256), 256)
        flux_out[here, :] = t_dot(spread[:, here], gather[...]).astype(BF16)
        for j in range(4):
            step = i * 4 + j
            if j == 0:
                pl.when(step > 0)(lambda: flux_copy(step, 1).start())
            else:
                flux_copy(step, 1).start()

    loop(DEVICES // 4, flux_chunk)
    flux_in[0:ROWS, :] = flux_out[0:ROWS, :]

    rest = slots_in.at[pl.ds(1, DEVICES - 1)]
    slots = pltpu.make_async_remote_copy(
        rest, rest, slot_ssem, slot_rsem, device_id=offset_device(me, 1, 1), device_id_type=MESH
    )
    slots.wait_recv()
    slots.wait_send()
    slot_rows = slots_in[...]
    lane = lax.broadcasted_iota(I32, (DEVICES, 256), 1)
    step_row = lax.broadcasted_iota(I32, (DEVICES, 256), 0)
    found = jnp.where(slot_rows[:, 0:1] == lane, 2 * step_row, 0) + jnp.where(
        slot_rows[:, 1:2] == lane, 2 * step_row + 1, 0
    )
    inv_v[...] = jnp.broadcast_to(jnp.max(found, axis=0, keepdims=True), inv_v.shape)
    to_scalar = pltpu.make_async_copy(slots_in, slots_s, misc_sem.at[0])
    to_scalar.start()
    to_scalar.wait()
    for load in loads:
        load.wait()

    goup[...] = jnp.zeros_like(goup)
    godown[...] = jnp.zeros_like(godown)
    gogain[...] = jnp.zeros_like(gogain)

    def back_copy(step, sign):
        here = pl.ds(pl.multiple_of(step * ROWS, ROWS), ROWS)
        return pltpu.make_async_remote_copy(
            back_out.at[here], back_in.at[here], back_ssem, back_rsem.at[step // GROUP],
            device_id=offset_device(me, step, sign), device_id_type=MESH,
        )

    def wait_group(g, buf, ssem, rsem):
        def first():
            some = buf.at[pl.ds(ROWS, (GROUP - 1) * ROWS)]
            pltpu.make_async_remote_copy(
                some, some, ssem, rsem.at[0], device_id=offset_device(me, 1, 1), device_id_type=MESH
            ).wait_recv()

        def later():
            some = buf.at[pl.ds(pl.multiple_of(g * (GROUP * ROWS), GROUP * ROWS), GROUP * ROWS)]
            pltpu.make_async_remote_copy(
                some, some, ssem, rsem.at[g], device_id=offset_device(me, 1, 1), device_id_type=MESH
            ).wait_recv()

        pl.when(g == 0)(first)
        pl.when(g > 0)(later)

    def ocean_group(g):
        wait_group(g, flux_in, flux_ssem, flux_rsem)
        here = pl.ds(pl.multiple_of(g * (GROUP * ROWS), GROUP * ROWS), GROUP * ROWS)
        slot = [slots_s[g * GROUP + j // 2, j % 2] & 255 for j in range(2 * GROUP)]
        state = jnp.concatenate([ostate[s] for s in slot], axis=0).astype(F32)
        wets = jnp.concatenate([wet[s] for s in slot], axis=0)
        out_grad = jnp.concatenate([ocot[s] for s in slot], axis=0) * wets
        total = state + flux_in[here, :].astype(F32)
        inv = lax.rsqrt(jnp.mean(total * total, axis=-1, keepdims=True) + EPS)
        u = total * inv
        nrm = (u * ogain[...]).astype(BF16)
        v = dot(nrm, oup[...])
        s = sigmoid(v)
        a = (v * s).astype(BF16)
        onew_arr[pl.ds(g * (2 * GROUP), 2 * GROUP)] = (
            (state + wets.astype(F32) * dot(a, odown[...])).astype(BF16).reshape(2 * GROUP, 32, 128)
        )
        godown[...] += t_dot(a, out_grad)
        pg = (dot_t(out_grad, odown[...]) * (s * (1.0 + v * (1.0 - s)))).astype(BF16)
        goup[...] += t_dot(nrm, pg)
        ng = dot_t(pg, oup[...])
        gogain[...] += jnp.sum(ng * u, axis=0, keepdims=True)
        gg = ng * ogain[...]
        tg = inv * (gg - u * jnp.mean(gg * u, axis=-1, keepdims=True))
        back_out[here, :] = tg.astype(BF16)

        def send(j):
            step = g * GROUP + j
            pl.when(step > 0)(lambda: back_copy(step, -1).start())

        loop(GROUP, send)

    loop(GROUPS, ocean_group)
    back_in[0:ROWS, :] = back_out[0:ROWS, :]

    store = pltpu.make_async_copy(onew_arr, onew_hbm, misc_sem.at[1])
    store.start()
    partial[AT_OUP : AT_OUP + 128, :] = goup[:, 0:128].astype(BF16)
    partial[AT_OUP + 128 : AT_OUP + 256, :] = goup[:, 128:256].astype(BF16)
    partial[AT_ODOWN : AT_ODOWN + 256, :] = godown[...].astype(BF16)

    sgrad[:, 0:128] = jnp.zeros((n_cells, 128), F32)

    def back_group(g):
        wait_group(g, back_in, back_ssem, back_rsem)
        here = pl.ds(pl.multiple_of(g * (GROUP * ROWS), GROUP * ROWS), GROUP * ROWS)
        sgrad[:, 0:128] += dot(spread[:, here], back_in[here, :])

    loop(GROUPS, back_group)
    gathered = sgrad[:, 0:128].astype(BF16)
    gather[...] = gathered
    partial[AT_COUPLE : AT_COUPLE + 256, :] = t_dot(anew[...].reshape(n_cells, 256), gathered).astype(BF16)

    gup[...] = jnp.zeros_like(gup)
    gdown[...] = jnp.zeros_like(gdown)
    gagain[...] = jnp.zeros_like(gagain)
    gtaps[...] = jnp.zeros_like(gtaps)

    def atm_back(i):
        here = pl.ds(pl.multiple_of(i * 128, 128), 128)
        cot = acot[pl.ds(i * 2, 2)].reshape(128, 256).astype(F32)
        out_grad = (cot + dot_t(gather[here, :], couple[...])).astype(BF16)
        gdown[...] += t_dot(act[here, :], out_grad)
        v = pre[here, :]
        s = sigmoid(v)
        pg = (dot_t(out_grad, down[...]) * (s * (1.0 + v * (1.0 - s)))).astype(BF16)
        gup[...] += t_dot(normed[here, :], pg)
        ng = dot_t(pg, up[...])
        u = unit[here, :]
        gagain[...] += jnp.sum(ng * u, axis=0, keepdims=True)
        gg = ng * again[...]
        sgrad[here, :] = inv_rms[here, 0:1] * (gg - u * jnp.mean(gg * u, axis=-1, keepdims=True))

    loop(4, atm_back)

    def taps_row(y):
        sg = sgrad[pl.ds(pl.multiple_of(y * breadth, breadth), breadth), :]
        for a in range(3):
            for b in range(3):
                gtaps[3 * a + b : 3 * a + b + 1, :] += jnp.sum(
                    sg * win[y + a, 7 + b : 7 + b + breadth, :], axis=0, keepdims=True
                )

    loop(height, taps_row)

    small[...] = jnp.zeros_like(small)
    small[0:9, :] = gtaps[0:9, 0:128]
    small[9:18, :] = gtaps[0:9, 128:256]
    small[18:19, :] = gagain[:, 0:128]
    small[19:20, :] = gagain[:, 128:256]
    small[20:21, :] = gogain[...]
    partial[AT_SMALL : AT_SMALL + 32, :] = small[...].astype(BF16)
    for i in range(2):
        partial[AT_DOWN + 512 * i : AT_DOWN + 512 * (i + 1), :] = gdown[:, 128 * i : 128 * (i + 1)].astype(BF16)
    for i in range(4):
        partial[AT_UP + 256 * i : AT_UP + 256 * (i + 1), :] = gup[:, 128 * i : 128 * (i + 1)].astype(BF16)

    def rows_of(rank):
        return pl.ds(pl.multiple_of(rank * PIECE, PIECE), PIECE)

    def part_copy(step):
        to = offset_device(me, step, 1)
        rank = owner_rank(*to)
        return rank, pltpu.make_async_remote_copy(
            partial.at[rows_of(rank)], pieces.at[step], part_ssem, part_rsem, device_id=to, device_id_type=MESH
        )

    def send_part(i):
        rank = owner_rank(*offset_device(me, i + 1, 1))
        pl.when(rank < OWNERS)(lambda: part_copy(i + 1)[1].start())

    loop(DEVICES - 1, send_part)
    rank = owner_rank(tx, ty)
    owns = rank < OWNERS

    def both_ends(ref, ssem, rsem):
        return pltpu.make_async_remote_copy(
            ref, ref, ssem, rsem, device_id=offset_device(me, 1, 1), device_id_type=MESH
        )

    @pl.when(owns)
    def _():
        both_ends(pieces.at[pl.ds(1, DEVICES - 1)], part_ssem, part_rsem).wait_recv()
        pieces[0] = partial[rows_of(rank), :]

        def add(i, total):
            return total + jnp.sum(pieces[pl.ds(i * 8, 8)].astype(F32), axis=0)

        total = lax.fori_loop(0, DEVICES // 8, add, jnp.zeros((PIECE, 128), F32))
        packed[rows_of(rank), :] = total.astype(BF16)

        def send_sum(i):
            pltpu.make_async_remote_copy(
                packed.at[rows_of(rank)], packed.at[rows_of(rank)], sum_ssem, sum_rsem,
                device_id=offset_device(me, i + 1, 1), device_id_type=MESH,
            ).start()

        loop(DEVICES - 1, send_sum)
        both_ends(packed.at[pl.ds(0, (OWNERS - 1) * PIECE)], sum_ssem, sum_rsem).wait_recv()
        both_ends(partial.at[pl.ds(0, (OWNERS - 1) * PIECE)], part_ssem, part_rsem).wait_send()
        both_ends(pieces.at[pl.ds(1, DEVICES - 1)], sum_ssem, sum_rsem).wait_send()

    @pl.when(jnp.logical_not(owns))
    def _():
        both_ends(packed.at[pl.ds(0, OWNERS * PIECE)], sum_ssem, sum_rsem).wait_recv()
        both_ends(partial.at[pl.ds(0, OWNERS * PIECE)], part_ssem, part_rsem).wait_send()

    result = pltpu.make_async_copy(packed, packed_hbm, misc_sem.at[0])
    result.start()

    sent = flux_out.at[pl.ds(ROWS, (DEVICES - 1) * ROWS)]
    pltpu.make_async_remote_copy(
        sent, sent, flux_ssem, flux_rsem.at[0], device_id=offset_device(me, 1, 1), device_id_type=MESH
    ).wait_send()
    sent = back_out.at[pl.ds(ROWS, (DEVICES - 1) * ROWS)]
    pltpu.make_async_remote_copy(
        sent, sent, back_ssem, back_rsem.at[0], device_id=offset_device(me, 1, 1), device_id_type=MESH
    ).wait_send()
    store.wait()
    result.wait()


def finish(
    inv, anew_in, onew_arr, packed, anew, onew, gtaps, gagain, gup, gdown, gcouple, gogain, goup, godown
):
    part = onew.shape[0]
    first = pl.program_id(0) * part

    def place(i):
        for j in range(8):
            onew[i * 8 + j] = onew_arr[inv[0, first + i * 8 + j] & 255]

    loop(part // 8, place)

    @pl.when(pl.program_id(0) == 0)
    def _():
        anew[...] = anew_in[...]
        goup[:, 0:128] = packed[AT_OUP : AT_OUP + 128, :].astype(F32)
        goup[:, 128:256] = packed[AT_OUP + 128 : AT_OUP + 256, :].astype(F32)
        godown[...] = packed[AT_ODOWN : AT_ODOWN + 256, :].astype(F32)
        gcouple[...] = packed[AT_COUPLE : AT_COUPLE + 256, :].astype(F32)
        small = packed[AT_SMALL : AT_SMALL + 32, :].astype(F32)
        for a in range(3):
            for i in range(2):
                gtaps[a, :, 128 * i : 128 * (i + 1)] = small[9 * i + 3 * a : 9 * i + 3 * a + 3]
        gagain[:, 0:128] = small[18:19]
        gagain[:, 128:256] = small[19:20]
        gogain[...] = small[20:21]
        for i in range(2):
            gdown[:, 128 * i : 128 * (i + 1)] = packed[AT_DOWN + 512 * i : AT_DOWN + 512 * (i + 1), :].astype(F32)
        for i in range(4):
            gup[:, 128 * i : 128 * (i + 1)] = packed[AT_UP + 256 * i : AT_UP + 256 * (i + 1), :].astype(F32)


def body(
    atm_state, kernel_taps, atm_gain, atm_up, atm_down, couple_weight, ocean_gain, ocean_up, ocean_down,
    ocean_state, land_mask, margin_cell, margin_area, owner_slot, atm_cotangent, ocean_cotangent,
):
    height, breadth, channels = atm_state.shape
    blocks = ocean_state.shape[0]
    n_rows = blocks * 32
    n_cells = height * breadth
    vmem, any_ = pl.BlockSpec(memory_space=pltpu.VMEM), pl.BlockSpec(memory_space=pl.ANY)
    block = lambda: pltpu.VMEM((blocks, 32, 128), BF16)
    flat = lambda: pltpu.VMEM((n_rows, 128), BF16)
    scratch = [
        block(), block(), block(),
        pltpu.VMEM((4, blocks // 4, 128), I32),
        pltpu.VMEM((4, blocks // 4, 128), F32),
        pltpu.VMEM((n_cells, n_rows), BF16),
        flat(), flat(), flat(), flat(),
        block(),
        pltpu.VMEM((DEVICES, 128), I32),
        pltpu.VMEM((DEVICES, 128), I32),
        pltpu.SMEM((DEVICES, 128), I32),
        pltpu.VMEM((height + 2, breadth + 16, channels), F32),
        pltpu.VMEM((n_cells, 256), F32),
        pltpu.VMEM((n_cells, 128), F32),
        pltpu.VMEM((n_cells, 256), BF16),
        pltpu.VMEM((n_cells, 512), F32),
        pltpu.VMEM((n_cells, 512), BF16),
        pltpu.VMEM((n_cells, 128), BF16),
        pltpu.VMEM((n_cells, 256), F32),
        pltpu.VMEM((16, 256), F32),
        pltpu.VMEM((1, 256), F32),
        pltpu.VMEM((256, 512), F32),
        pltpu.VMEM((512, 256), F32),
        pltpu.VMEM((1, 128), F32),
        pltpu.VMEM((128, 256), F32),
        pltpu.VMEM((256, 128), F32),
        pltpu.VMEM((32, 128), F32),
        pltpu.VMEM((PACKED, 128), BF16),
        pltpu.VMEM((DEVICES, PIECE, 128), BF16),
        pltpu.VMEM((PACKED, 128), BF16),
        pltpu.VMEM((16, channels), BF16),
        pltpu.VMEM((16, channels), BF16),
        pltpu.VMEM((breadth, channels), BF16),
        pltpu.VMEM((breadth, channels), BF16),
        pltpu.VMEM((6, 16, channels), BF16),
        pltpu.SemaphoreType.DMA((2,)),
        pltpu.SemaphoreType.DMA((8,)),
        pltpu.SemaphoreType.DMA((8,)),
        pltpu.SemaphoreType.DMA,
        pltpu.SemaphoreType.DMA,
        pltpu.SemaphoreType.DMA,
        pltpu.SemaphoreType.DMA((GROUPS,)),
        pltpu.SemaphoreType.DMA,
        pltpu.SemaphoreType.DMA((GROUPS,)),
        pltpu.SemaphoreType.DMA((2,)),
        pltpu.SemaphoreType.DMA,
        pltpu.SemaphoreType.DMA,
        pltpu.SemaphoreType.DMA,
        pltpu.SemaphoreType.DMA,
    ]
    anew, onew_arr, inv, packed = pl.pallas_call(
        kernel,
        out_shape=[
            jax.ShapeDtypeStruct((height, breadth, channels), BF16),
            jax.ShapeDtypeStruct((blocks, 32, 128), BF16),
            jax.ShapeDtypeStruct((8, 256), I32),
            jax.ShapeDtypeStruct((PACKED, 128), BF16),
        ],
        in_specs=[vmem] * 14 + [any_] * 2,
        out_specs=[vmem, any_, vmem, any_],
        scratch_shapes=scratch,
        compiler_params=pltpu.CompilerParams(
            collective_id=0, has_side_effects=True, vmem_limit_bytes=56 * 1024 * 1024
        ),
    )(
        atm_state, kernel_taps, atm_gain.reshape(1, -1), atm_up, atm_down, couple_weight,
        ocean_gain.reshape(1, -1), ocean_up, ocean_down, land_mask.T, margin_cell.transpose(1, 2, 0),
        margin_area.transpose(1, 2, 0), owner_slot.reshape(1, -1), atm_cotangent, ocean_state, ocean_cotangent,
    )
    part = blocks // 4
    whole = lambda *shape: pl.BlockSpec(shape, lambda i: (0,) * len(shape))
    anew, onew, gtaps, gagain, gup, gdown, gcouple, gogain, goup, godown = pl.pallas_call(
        finish,
        grid=(4,),
        out_shape=[
            jax.ShapeDtypeStruct((height, breadth, channels), BF16),
            jax.ShapeDtypeStruct((blocks, 32, 128), BF16),
            jax.ShapeDtypeStruct((3, 3, 256), F32),
            jax.ShapeDtypeStruct((1, 256), F32),
            jax.ShapeDtypeStruct((256, 512), F32),
            jax.ShapeDtypeStruct((512, 256), F32),
            jax.ShapeDtypeStruct((256, 128), F32),
            jax.ShapeDtypeStruct((1, 128), F32),
            jax.ShapeDtypeStruct((128, 256), F32),
            jax.ShapeDtypeStruct((256, 128), F32),
        ],
        in_specs=[
            pl.BlockSpec(memory_space=pltpu.SMEM),
            whole(height, breadth, channels), whole(blocks, 32, 128), whole(PACKED, 128),
        ],
        out_specs=[
            whole(height, breadth, channels), pl.BlockSpec((part, 32, 128), lambda i: (i, 0, 0)), whole(3, 3, 256),
            whole(1, 256), whole(256, 512), whole(512, 256), whole(256, 128), whole(1, 128), whole(128, 256),
            whole(256, 128),
        ],
        compiler_params=pltpu.CompilerParams(vmem_limit_bytes=40 * 1024 * 1024),
    )(inv, anew, onew_arr, packed)
    return (
        anew, onew, gtaps, gagain.reshape(-1), gup, gdown, gcouple, gogain.reshape(-1), goup, godown,
    )


def solution(mesh):
    both = ("tx", "ty")
    return jax.shard_map(
        body,
        mesh=mesh,
        in_specs=(P("ty", "tx", None),) + (P(),) * 8 + (
            P(both, None, None), P(both, None), P(both, None, None), P(both, None, None), P(both),
            P("ty", "tx", None), P(both, None, None),
        ),
        out_specs=(P("ty", "tx", None), P(both, None, None)) + (P(),) * 8,
        check_vma=False,
    )
```

```python
import functools

import jax
import jax.numpy as jnp
from jax import lax
from jax.experimental import pallas as pl
from jax.experimental.pallas import tpu as pltpu
from jax.sharding import PartitionSpec as P

EPS = 1e-06
MESH = pl.DeviceIdType.MESH
F32, BF16, I32 = jnp.float32, jnp.bfloat16, jnp.int32
DEVICES = 128
MIX = 37
UNMIX = pow(MIX, -1, DEVICES)
ROWS = 64
GROUP = 8
GROUPS = DEVICES // GROUP
PIECE = 16
LATE = DEVICES * PIECE
EARLY = 768
HALF, QUARTER = EARLY // 2, EARLY // 8


def digits(tx, ty):
    return (tx // 4) * 2 + ty // 8, (ty // 2) % 4, tx % 4, ty % 2


def rem(a, n):
    return lax.rem(a, jnp.int32(n))


def div(a, n):
    return lax.div(a, jnp.int32(n))


def device(x, y, z, c):
    return (div(x, 2) * 4 + z, rem(x, 2) * 8 + y * 2 + c)


def offset_device(me, step, sign):
    code = rem(step * MIX, DEVICES)
    x = rem(me[0] + 4 + sign * rem(div(code, 2), 4), 4)
    y = rem(me[1] + 4 + sign * rem(div(code, 8), 4), 4)
    z = rem(me[2] + 4 + sign * div(code, 32), 4)
    return device(x, y, z, rem(me[3] + code, 2))


def rank_of(tx, ty):
    return rem((tx * 16 + ty) * MIX, DEVICES)


def sigmoid(v):
    return 0.5 * jnp.tanh(0.5 * v) + 0.5


def dot(a, b):
    return jnp.dot(a, b, preferred_element_type=F32)


def dot_t(a, b):
    return lax.dot_general(a, b, (((1,), (1,)), ((), ())), preferred_element_type=F32)


def t_dot(a, b):
    return lax.dot_general(a, b, (((0,), (0,)), ((), ())), preferred_element_type=F32)


def loop(n, f):
    lax.fori_loop(0, n, lambda i, c: (f(i), c)[1], 0)


def kernel(
    atm, taps, again, up, down, couple, ogain, oup, odown, mask, margin_cell, margin_area, owner, acot, ostate_hbm, ocot_hbm,
    anew, onew_hbm, inv_v, late_hbm, early_hbm, small_hbm,
    ostate, ocot, wet, cells, shares, spread, flux_out, flux_in, back_out, back_in, onew_arr, owners, slots_v, slots_s,
    win, unit, inv_rms, normed, pre, act, gather, coupled_t, sgrad, up_t, down_t, couple_t, oup_t, odown_t,
    gtaps, gagain, gup, gdown_t, gogain, goup, godown_t, small, late, pieces, late_sum,
    early, early_core, early_mine, early_x, early_y, early_z, early_sum, small_core, small_x, small_y, small_z,
    edge_w, edge_e, halo_n, halo_s, halo_c,
    load_sem, halo_ssem, halo_rsem, own_ssem, own_rsem, flux_ssem, flux_rsem, back_ssem, back_rsem, misc_sem,
    late_ssem, late_rsem, sum_ssem, sum_rsem, early_ssem, early_rsem, small_ssem, small_rsem,
):
    tx, ty = lax.axis_index("tx"), lax.axis_index("ty")
    me = digits(tx, ty)
    height, breadth = atm.shape[0], atm.shape[1]
    n_cells = height * breadth

    barrier = pltpu.get_barrier_semaphore()
    loads = [
        pltpu.make_async_copy(ostate_hbm, ostate, load_sem.at[0]),
        pltpu.make_async_copy(ocot_hbm, ocot, load_sem.at[1]),
    ]
    for load in loads:
        load.start()

    xs = [rem(me[0] + i, 4) for i in range(4)]
    ys = [rem(me[1] + i, 4) for i in range(4)]
    zs = [rem(me[2] + i, 4) for i in range(4)]
    cs = [me[3], 1 - me[3]]
    for i in range(1, DEVICES):
        pl.semaphore_signal(
            barrier, inc=1, device_id=device(xs[i // 2 % 4], ys[i // 8 % 4], zs[i // 32], cs[i % 2]), device_id_type=MESH
        )
    partner = device(xs[0], ys[0], zs[0], cs[1])
    x_peers = [device(xs[i], ys[0], zs[0], cs[0]) for i in (1, 3, 2)]
    y_peers = [device(xs[0], ys[i], zs[0], cs[0]) for i in (1, 3, 2)]
    z_peers = [device(xs[0], ys[0], zs[i], cs[0]) for i in (1, 3, 2)]

    def remote(src, dst, ssem, rsem, to):
        return pltpu.make_async_remote_copy(src, dst, ssem, rsem, device_id=to, device_id_type=MESH)

    def both_ends(ref, ssem, rsem):
        return remote(ref, ref, ssem, rsem, partner)

    edge_w[...] = jnp.zeros_like(edge_w)
    edge_e[...] = jnp.zeros_like(edge_e)

    def own_rows(y):
        win[y + 1, 8 : 8 + breadth, :] = atm[y].astype(F32)

    loop(height, own_rows)
    west = jnp.concatenate([win[y + 1, 8:9, :] for y in range(height)], axis=0)
    east = jnp.concatenate([win[y + 1, 7 + breadth : 8 + breadth, :] for y in range(height)], axis=0)
    nothing = jnp.zeros_like(west)
    edge_w[...] = jnp.concatenate([west, nothing], axis=0).astype(BF16)
    edge_e[...] = jnp.concatenate([east, nothing], axis=0).astype(BF16)

    pl.semaphore_wait(barrier, DEVICES - 1)

    te, tw = (tx + 1) % 8, (tx + 7) % 8
    north, south = ty > 0, ty < 15

    def halo(i, src, dst, dx, dy):
        return pltpu.make_async_remote_copy(
            src, dst, halo_ssem.at[i], halo_rsem.at[i], device_id=(dx, dy), device_id_type=MESH
        )

    copies = [
        (south, halo(0, atm.at[height - 1], halo_n, tx, (ty + 1) % 16)),
        (north, halo(1, atm.at[0], halo_s, tx, (ty + 15) % 16)),
        (None, halo(2, edge_e, halo_c.at[0], te, ty)),
        (None, halo(3, edge_w, halo_c.at[1], tw, ty)),
        (south, halo(4, edge_e, halo_c.at[2], te, (ty + 1) % 16)),
        (south, halo(5, edge_w, halo_c.at[3], tw, (ty + 1) % 16)),
        (north, halo(6, edge_e, halo_c.at[4], te, (ty + 15) % 16)),
        (north, halo(7, edge_w, halo_c.at[5], tw, (ty + 15) % 16)),
    ]

    def when(cond, f):
        if cond is None:
            f()
        else:
            pl.when(cond)(f)

    for cond, copy in copies:
        when(cond, copy.start)

    owners[0:1, :] = owner[...]

    def own_phase(i, rows, peers):
        for n, to in zip((1, 3, 2), peers):
            remote(
                owners.at[pl.ds(0, rows)], owners.at[pl.ds(n * rows, rows)], own_ssem.at[i], own_rsem.at[i], to
            ).start()

    def own_wait(i, rows, peers):
        both_ends(owners.at[pl.ds(rows, rows * peers)], own_ssem.at[i], own_rsem.at[i]).wait_recv()

    own_phase(0, 1, [partner])

    slot = owner[...]
    t_tx, t_ty = slot >> 12, (slot >> 8) & 15
    theirs = ((t_tx >> 2) * 2 + (t_ty >> 3), (t_ty >> 1) & 3, t_tx & 3, t_ty & 1)
    dx, dy, dz, dc = [(t - m + n) & (n - 1) for t, m, n in zip(theirs, me, (4, 4, 4, 2))]
    step = ((((dz * 4 + dy) * 4 + dx) * 2 + dc) * UNMIX) & (DEVICES - 1)
    blocks = slot.shape[1]
    square = jnp.broadcast_to(step, (blocks, blocks))
    first = lax.broadcasted_iota(I32, square.shape, 0)
    second = lax.broadcasted_iota(I32, square.shape, 1)
    same = (square.astype(F32).T == square.astype(F32)) & (first < second)
    place = 2 * step + jnp.sum(same.astype(F32), axis=0, keepdims=True).astype(I32)

    area = margin_area[...]
    share = (area / jnp.sum(area, axis=0, keepdims=True)).reshape(128, blocks).astype(BF16)
    cell = margin_cell[...].reshape(128, blocks)
    high, low = (cell >> 4).astype(F32).astype(BF16), (cell & 15).astype(F32).astype(BF16)
    quads = lax.broadcasted_iota(I32, (blocks // 4, blocks), 0)
    lane_block = lax.broadcasted_iota(I32, (blocks // 4, 128), 1) // 32
    got_share = [jnp.zeros((blocks // 4, 128), F32)] * 4
    got_cell = [jnp.zeros((blocks // 4, 128), F32)] * 4
    for j in range(4):
        pick = (place == 4 * quads + j).astype(F32).astype(BF16)
        one_share = dot_t(pick, share)
        one_cell = 16.0 * dot_t(pick, high) + dot_t(pick, low)
        for k in range(4):
            turn = (32 * (j - k)) % 128
            here = lane_block == j
            got_share[k] = jnp.where(here, pltpu.roll(one_share, turn, 1) if turn else one_share, got_share[k])
            got_cell[k] = jnp.where(here, pltpu.roll(one_cell, turn, 1) if turn else one_cell, got_cell[k])
    for k in range(4):
        shares[k] = got_share[k]
        cells[k] = got_cell[k].astype(I32)

    for weight, turned in ((up, up_t), (down, down_t), (couple, couple_t), (oup, oup_t), (odown, odown_t)):
        turned[...] = weight[...].astype(F32).T.astype(BF16)

    own_wait(0, 1, 1)
    own_phase(1, 2, x_peers)

    for cond, copy in copies:
        when(cond, copy.wait_send)
    receives = [north, south, None, None, north, north, south, south]
    for cond, (_, copy) in zip(receives, copies):
        when(cond, copy.wait_recv)

    @pl.when(north)
    def _():
        win[0, 8 : 8 + breadth, :] = halo_n[...].astype(F32)
        win[0, 7:8, :] = halo_c[2].astype(F32)[height - 1 : height]
        win[0, 8 + breadth : 9 + breadth, :] = halo_c[3].astype(F32)[height - 1 : height]

    @pl.when(jnp.logical_not(north))
    def _():
        win[0] = jnp.zeros(win.shape[1:], F32)

    @pl.when(south)
    def _():
        win[height + 1, 8 : 8 + breadth, :] = halo_s[...].astype(F32)
        win[height + 1, 7:8, :] = halo_c[4].astype(F32)[0:1]
        win[height + 1, 8 + breadth : 9 + breadth, :] = halo_c[5].astype(F32)[0:1]

    @pl.when(jnp.logical_not(south))
    def _():
        win[height + 1] = jnp.zeros(win.shape[1:], F32)

    west, east = halo_c[0].astype(F32), halo_c[1].astype(F32)
    for y in range(height):
        win[y + 1, 7:8, :] = west[y : y + 1]
        win[y + 1, 8 + breadth : 9 + breadth, :] = east[y : y + 1]

    def stencil_row(y):
        total = jnp.zeros((breadth, 256), F32)
        for a in range(3):
            for b in range(3):
                total = total + taps[a, b : b + 1, :] * win[y + a, 7 + b : 7 + b + breadth, :]
        inv = lax.rsqrt(jnp.mean(total * total, axis=-1, keepdims=True) + EPS)
        here = pl.ds(pl.multiple_of(y * breadth, breadth), breadth)
        u = total * inv
        unit[here, :] = u
        inv_rms[here, :] = jnp.broadcast_to(inv, (breadth, 128))
        normed[here, :] = (u * again[...]).astype(BF16)

    loop(height, stencil_row)
    own_wait(1, 2, 3)
    own_phase(2, 8, y_peers)

    def atm_mlp(i):
        here = pl.ds(pl.multiple_of(i * 128, 128), 128)
        v = dot(normed[here, :], up[...])
        pre[here, :] = v
        a = (v * sigmoid(v)).astype(BF16)
        act[here, :] = a
        old = atm[pl.ds(i * 2, 2)].reshape(128, 256).astype(F32)
        anew[pl.ds(i * 2, 2)] = (old + dot(a, down[...])).astype(BF16).reshape(2, breadth, 256)

    loop(4, atm_mlp)
    coupled_t[...] = dot_t(couple_t[...], anew[...].reshape(n_cells, 256)).astype(BF16)
    own_wait(2, 8, 3)
    own_phase(3, 32, z_peers)

    def spread_columns(i):
        here = pl.ds(pl.multiple_of(i * 128, 128), 128)
        rows = lax.broadcasted_iota(I32, (n_cells, 128), 0)
        row = pl.ds(i, 1)
        total = jnp.where(rows == cells[0, row, :], shares[0, row, :], 0.0)
        for k in range(1, 4):
            total = total + jnp.where(rows == cells[k, row, :], shares[k, row, :], 0.0)
        spread[:, here] = total.astype(BF16)

    def flux_copy(step, sign):
        here = pl.ds(pl.multiple_of(step * ROWS, ROWS), ROWS)
        return pltpu.make_async_remote_copy(
            flux_out.at[here], flux_in.at[here], flux_ssem, flux_rsem.at[step // GROUP],
            device_id=offset_device(me, step, sign), device_id_type=MESH,
        )

    def flux_group(g):
        for j in range(GROUP // 2):
            spread_columns(g * (GROUP // 2) + j)
        here = pl.ds(pl.multiple_of(g * (GROUP * ROWS), GROUP * ROWS), GROUP * ROWS)
        flux_out[here, :] = dot(coupled_t[...], spread[:, here]).astype(BF16).T
        pl.when(g > 0)(lambda: flux_copy(g * GROUP, 1).start())
        for j in range(1, GROUP):
            flux_copy(g * GROUP + j, 1).start()

    loop(GROUPS, flux_group)
    flux_in[0:ROWS, :] = flux_out[0:ROWS, :]

    ones = jnp.ones((32, 128), BF16)
    wet_rows_of = mask[...].astype(F32).astype(BF16)

    def wet_rows(i):
        rows = lax.broadcasted_iota(I32, (512, blocks), 0)
        cols = lax.broadcasted_iota(I32, (512, blocks), 1)
        pick = (rows // 32 + i * 16 == cols).astype(F32).astype(BF16)
        wide = dot_t(pick, wet_rows_of)
        r2 = lax.broadcasted_iota(I32, wide.shape, 0)
        c2 = lax.broadcasted_iota(I32, wide.shape, 1)
        wide = jnp.where(r2 % 32 == c2, wide, 0.0).astype(BF16)
        wet[pl.ds(pl.multiple_of(i * 16, 16), 16)] = dot(wide, ones).astype(BF16).reshape(16, 32, 128)

    loop(16, wet_rows)

    own_wait(3, 32, 3)
    owned = owners[...]
    lane = lax.broadcasted_iota(I32, owned.shape, 1)
    hit = (owned >> 8) == tx * 16 + ty
    lane_f = lane.astype(F32)
    local = (owned & (blocks - 1)).astype(F32)
    one = jnp.min(jnp.where(hit, lane_f, 1e4), axis=1, keepdims=True)
    two = jnp.max(jnp.where(hit, lane_f, -1.0), axis=1, keepdims=True)
    one = jnp.sum(jnp.where(lane_f == one, local, 0.0), axis=1, keepdims=True).astype(I32)
    two = jnp.sum(jnp.where(lane_f == two, local, 0.0), axis=1, keepdims=True).astype(I32)
    position = 2 * ((lax.broadcasted_iota(I32, owned.shape, 0) * UNMIX) & (DEVICES - 1))
    found = jnp.where(one == lane, position, 0) + jnp.where(two == lane, position + 1, 0)
    inv_v[...] = jnp.broadcast_to(
        jnp.max(found.astype(F32), axis=0, keepdims=True).astype(I32), inv_v.shape
    )
    slots_v[...] = jnp.where(lane[:, 0:128] == 0, one, two)
    to_scalar = pltpu.make_async_copy(slots_v, slots_s, misc_sem.at[0])
    to_scalar.start()
    to_scalar.wait()
    for load in loads:
        load.wait()

    goup[...] = jnp.zeros_like(goup)
    godown_t[...] = jnp.zeros_like(godown_t)
    gogain[...] = jnp.zeros_like(gogain)

    def back_copy(step, sign):
        here = pl.ds(pl.multiple_of(step * ROWS, ROWS), ROWS)
        return pltpu.make_async_remote_copy(
            back_out.at[here], back_in.at[here], back_ssem, back_rsem.at[step // GROUP],
            device_id=offset_device(me, step, sign), device_id_type=MESH,
        )

    def wait_group(g, buf, ssem, rsem):
        def first():
            some = buf.at[pl.ds(ROWS, (GROUP - 1) * ROWS)]
            pltpu.make_async_remote_copy(
                some, some, ssem, rsem.at[0], device_id=offset_device(me, 1, 1), device_id_type=MESH
            ).wait_recv()

        def later():
            some = buf.at[pl.ds(pl.multiple_of(g * (GROUP * ROWS), GROUP * ROWS), GROUP * ROWS)]
            pltpu.make_async_remote_copy(
                some, some, ssem, rsem.at[g], device_id=offset_device(me, 1, 1), device_id_type=MESH
            ).wait_recv()

        pl.when(g == 0)(first)
        pl.when(g > 0)(later)

    def ocean_group(g):
        wait_group(g, flux_in, flux_ssem, flux_rsem)
        here = pl.ds(pl.multiple_of(g * (GROUP * ROWS), GROUP * ROWS), GROUP * ROWS)
        codes = [rem((g * GROUP + j) * MIX, DEVICES) for j in range(GROUP)]
        slot = [slots_s[codes[j // 2], j % 2] & 255 for j in range(2 * GROUP)]
        state = jnp.concatenate([ostate[s] for s in slot], axis=0).astype(F32)
        wets = jnp.concatenate([wet[s] for s in slot], axis=0)
        out_grad = jnp.concatenate([ocot[s] for s in slot], axis=0) * wets
        total = state + flux_in[here, :].astype(F32)
        inv = lax.rsqrt(jnp.mean(total * total, axis=-1, keepdims=True) + EPS)
        u = total * inv
        nrm = (u * ogain[...]).astype(BF16)
        v = dot(nrm, oup[...])
        s = sigmoid(v)
        a = (v * s).astype(BF16)
        onew_arr[pl.ds(g * (2 * GROUP), 2 * GROUP)] = (
            (state + wets.astype(F32) * dot(a, odown[...])).astype(BF16).reshape(2 * GROUP, 32, 128)
        )
        godown_t[...] += t_dot(out_grad, a)
        pg = (dot(out_grad, odown_t[...]) * (s * (1.0 + v * (1.0 - s)))).astype(BF16)
        goup[...] += t_dot(nrm, pg)
        ng = dot(pg, oup_t[...])
        gogain[...] += jnp.sum(ng * u, axis=0, keepdims=True)
        gg = ng * ogain[...]
        tg = inv * (gg - u * jnp.mean(gg * u, axis=-1, keepdims=True))
        back_out[here, :] = tg.astype(BF16)

        pl.when(g > 0)(lambda: back_copy(g * GROUP, -1).start())
        for j in range(1, GROUP):
            back_copy(g * GROUP + j, -1).start()

    loop(GROUPS, ocean_group)
    back_in[0:ROWS, :] = back_out[0:ROWS, :]

    store = pltpu.make_async_copy(onew_arr, onew_hbm, misc_sem.at[1])
    store.start()
    for i in range(2):
        early[128 * i : 128 * (i + 1), :] = goup[:, 128 * i : 128 * (i + 1)].astype(BF16)
        early[256 + 128 * i : 256 + 128 * (i + 1), :] = godown_t[:, 128 * i : 128 * (i + 1)].astype(BF16)

    sgrad[:, 0:128] = jnp.zeros((n_cells, 128), F32)

    def back_group(g):
        wait_group(g, back_in, back_ssem, back_rsem)
        here = pl.ds(pl.multiple_of(g * (GROUP * ROWS), GROUP * ROWS), GROUP * ROWS)
        sgrad[:, 0:128] += dot(spread[:, here], back_in[here, :])

    loop(GROUPS, back_group)
    gathered = sgrad[:, 0:128].astype(BF16)
    gather[...] = gathered
    gcouple_t = t_dot(gathered, anew[...].reshape(n_cells, 256)).astype(BF16)
    for i in range(2):
        early[512 + 128 * i : 512 + 128 * (i + 1), :] = gcouple_t[:, 128 * i : 128 * (i + 1)]

    x, y, z, c = me

    def span(i, n):
        return pl.ds(pl.multiple_of(i * n, n), n)

    def early_copy(i, src, dst, to):
        remote(src, dst, early_ssem.at[i], early_rsem.at[i], to).start()

    def early_wait(i, ref):
        both_ends(ref, early_ssem.at[i], early_rsem.at[i]).wait_recv()

    def add_four(ref):
        rows = ref.shape[0] // 4
        total = ref[0:rows, :]
        for i in range(1, 4):
            total = total + ref[i * rows : (i + 1) * rows, :]
        return total

    def early_0():
        early_copy(0, early.at[span(1 - c, HALF)], early_core, partner)

    def early_1():
        early_wait(0, early_core)
        early_mine[...] = early[span(c, HALF), :].astype(F32) + early_core[...].astype(F32)
        early_x[span(x, QUARTER), :] = early_mine[span(x, QUARTER), :]
        for n, to in zip((1, 3, 2), x_peers):
            early_copy(1, early_mine.at[span(xs[n], QUARTER)], early_x.at[span(x, QUARTER)], to)

    def early_2():
        early_wait(1, early_x.at[pl.ds(0, 3 * QUARTER)])
        early_y[span(y, QUARTER), :] = add_four(early_x)
        for to in y_peers:
            early_copy(2, early_y.at[span(y, QUARTER)], early_y.at[span(y, QUARTER)], to)

    def early_3():
        early_wait(2, early_y.at[pl.ds(0, 3 * QUARTER)])
        early_z[span(z, QUARTER), :] = add_four(early_y)
        for to in z_peers:
            early_copy(3, early_z.at[span(z, QUARTER)], early_z.at[span(z, QUARTER)], to)

    def early_4():
        early_wait(3, early_z.at[pl.ds(0, 3 * QUARTER)])
        here = span(c * 4 + x, QUARTER)
        early_sum[here, :] = add_four(early_z).astype(BF16)
        for to in x_peers:
            early_copy(4, early_sum.at[here], early_sum.at[here], to)

    def early_5():
        early_wait(4, early_sum.at[pl.ds(0, 3 * QUARTER)])
        here = span(c, HALF)
        early_copy(5, early_sum.at[here], early_sum.at[here], partner)

    def early_6():
        early_wait(5, early_sum.at[pl.ds(0, HALF)])

    early_0()
    gup[...] = jnp.zeros_like(gup)
    gdown_t[...] = jnp.zeros_like(gdown_t)
    gagain[...] = jnp.zeros_like(gagain)
    gtaps[...] = jnp.zeros_like(gtaps)

    def atm_back(i):
        here = pl.ds(pl.multiple_of(i * 128, 128), 128)
        cot = acot[pl.ds(i * 2, 2)].reshape(128, 256).astype(F32)
        out_grad = (cot + dot(gather[here, :], couple_t[...])).astype(BF16)
        gdown_t[...] += t_dot(out_grad, act[here, :])
        v = pre[here, :]
        s = sigmoid(v)
        pg = (dot(out_grad, down_t[...]) * (s * (1.0 + v * (1.0 - s)))).astype(BF16)
        gup[...] += t_dot(normed[here, :], pg)
        ng = dot(pg, up_t[...])
        u = unit[here, :]
        gagain[...] += jnp.sum(ng * u, axis=0, keepdims=True)
        gg = ng * again[...]
        sgrad[here, :] = inv_rms[here, 0:1] * (gg - u * jnp.mean(gg * u, axis=-1, keepdims=True))

    loop(2, atm_back)
    early_1()
    loop(2, lambda i: atm_back(i + 2))
    early_2()

    def taps_row(y):
        sg = sgrad[pl.ds(pl.multiple_of(y * breadth, breadth), breadth), :]
        for a in range(3):
            for b in range(3):
                gtaps[3 * a + b : 3 * a + b + 1, :] += jnp.sum(
                    sg * win[y + a, 7 + b : 7 + b + breadth, :], axis=0, keepdims=True
                )

    loop(height, taps_row)

    small[...] = jnp.zeros_like(small)
    small[0:9, :] = gtaps[0:9, 0:128]
    small[9:18, :] = gtaps[0:9, 128:256]
    small[18:19, :] = gagain[:, 0:128]
    small[19:20, :] = gagain[:, 128:256]
    small[20:21, :] = gogain[...]

    def small_phase(i, value, buf, at, peers):
        buf[at] = value
        for to in peers:
            remote(buf.at[at], buf.at[at], small_ssem.at[i], small_rsem.at[i], to).start()

    def small_wait(i, buf):
        rest = buf.shape[0] - 1
        both_ends(buf.at[pl.ds(0, rest)], small_ssem.at[i], small_rsem.at[i]).wait_recv()
        total = buf[0]
        for n in range(rest):
            total = total + buf[n + 1]
        return total

    small_phase(0, small[...], small_core, c, [partner])
    for i in range(4):
        late[256 * i : 256 * (i + 1), :] = gup[:, 128 * i : 128 * (i + 1)].astype(BF16)
        late[1024 + 256 * i : 1024 + 256 * (i + 1), :] = gdown_t[:, 128 * i : 128 * (i + 1)].astype(BF16)

    def send_late(i):
        to = offset_device(me, i + 1, 1)
        remote(late.at[span(rank_of(*to), PIECE)], pieces.at[i + 1], late_ssem, late_rsem, to).start()

    loop(DEVICES - 1, send_late)
    small_phase(1, small_wait(0, small_core), small_x, x, x_peers)
    early_3()
    mine = span(rank_of(tx, ty), PIECE)
    pieces[0] = late[mine, :]
    both_ends(pieces.at[pl.ds(1, DEVICES - 1)], late_ssem, late_rsem).wait_recv()

    def add(i, total):
        return total + jnp.sum(pieces[pl.ds(i * 8, 8)].astype(F32), axis=0)

    late_sum[mine, :] = lax.fori_loop(0, DEVICES // 8, add, jnp.zeros((PIECE, 128), F32)).astype(BF16)

    def send_sum(i):
        remote(late_sum.at[mine], late_sum.at[mine], sum_ssem, sum_rsem, offset_device(me, i + 1, 1)).start()

    small_phase(2, small_wait(1, small_x), small_y, y, y_peers)
    early_4()
    loop(DEVICES - 1, send_sum)
    small_phase(3, small_wait(2, small_y), small_z, z, z_peers)
    early_5()
    early_6()
    small[...] = small_wait(3, small_z)
    results = [
        pltpu.make_async_copy(early_sum, early_hbm, misc_sem.at[0]),
        pltpu.make_async_copy(small, small_hbm, misc_sem.at[2]),
        pltpu.make_async_copy(late_sum, late_hbm, misc_sem.at[3]),
    ]
    results[0].start()
    results[1].start()
    others = pl.ds(0, LATE - PIECE)
    both_ends(late_sum.at[others], sum_ssem, sum_rsem).wait_recv()
    results[2].start()
    both_ends(late.at[others], late_ssem, late_rsem).wait_send()
    both_ends(late.at[others], sum_ssem, sum_rsem).wait_send()
    for i, rows in ((0, 1), (1, 6), (2, 24), (3, 96)):
        both_ends(owners.at[pl.ds(0, rows)], own_ssem.at[i], own_rsem.at[i]).wait_send()
    for i, rows in enumerate((HALF, 3 * QUARTER, 3 * QUARTER, 3 * QUARTER, 3 * QUARTER, HALF)):
        sent = early_x if 0 < i < 4 else early
        both_ends(sent.at[pl.ds(0, rows)], early_ssem.at[i], early_rsem.at[i]).wait_send()
    for i, n in enumerate((1, 3, 3, 3)):
        both_ends(small_z.at[pl.ds(0, n)], small_ssem.at[i], small_rsem.at[i]).wait_send()

    sent = flux_out.at[pl.ds(ROWS, (DEVICES - 1) * ROWS)]
    pltpu.make_async_remote_copy(
        sent, sent, flux_ssem, flux_rsem.at[0], device_id=offset_device(me, 1, 1), device_id_type=MESH
    ).wait_send()
    sent = back_out.at[pl.ds(ROWS, (DEVICES - 1) * ROWS)]
    pltpu.make_async_remote_copy(
        sent, sent, back_ssem, back_rsem.at[0], device_id=offset_device(me, 1, 1), device_id_type=MESH
    ).wait_send()
    store.wait()
    for result in results:
        result.wait()


def finish(
    inv, anew_in, onew_arr, late, early, small, anew, onew, gtaps, gagain, gup, gdown, gcouple, gogain, goup, godown
):
    part = onew.shape[0]
    first = pl.program_id(0) * part

    def place(i):
        for j in range(8):
            onew[i * 8 + j] = onew_arr[inv[0, first + i * 8 + j] & 255]

    loop(part // 8, place)

    @pl.when(pl.program_id(0) == 0)
    def _():
        anew[...] = anew_in[...]
        for i in range(2):
            here = slice(128 * i, 128 * (i + 1))
            goup[:, here] = early[128 * i : 128 * (i + 1), :].astype(F32)
            godown[here, :] = early[256 + 128 * i : 256 + 128 * (i + 1), :].astype(F32).T
            gcouple[here, :] = early[512 + 128 * i : 512 + 128 * (i + 1), :].astype(F32).T
        for a in range(3):
            for i in range(2):
                gtaps[a, :, 128 * i : 128 * (i + 1)] = small[9 * i + 3 * a : 9 * i + 3 * a + 3, :]
        gagain[:, 0:128] = small[18:19, :]
        gagain[:, 128:256] = small[19:20, :]
        gogain[...] = small[20:21, :]
        for i in range(4):
            here = slice(128 * i, 128 * (i + 1))
            gup[:, here] = late[256 * i : 256 * (i + 1), :].astype(F32)
            gdown[here, :] = late[1024 + 256 * i : 1024 + 256 * (i + 1), :].astype(F32).T


def body(
    atm_state, kernel_taps, atm_gain, atm_up, atm_down, couple_weight, ocean_gain, ocean_up, ocean_down,
    ocean_state, land_mask, margin_cell, margin_area, owner_slot, atm_cotangent, ocean_cotangent,
):
    height, breadth, channels = atm_state.shape
    blocks = ocean_state.shape[0]
    n_rows = blocks * 32
    n_cells = height * breadth
    vmem, any_ = pl.BlockSpec(memory_space=pltpu.VMEM), pl.BlockSpec(memory_space=pl.ANY)
    block = lambda: pltpu.VMEM((blocks, 32, 128), BF16)
    flat = lambda: pltpu.VMEM((n_rows, 128), BF16)
    scratch = [
        block(), block(), block(),
        pltpu.VMEM((4, blocks // 4, 128), I32),
        pltpu.VMEM((4, blocks // 4, 128), F32),
        pltpu.VMEM((n_cells, n_rows), BF16),
        flat(), flat(), flat(), flat(),
        block(),
        pltpu.VMEM((DEVICES, blocks), I32),
        pltpu.VMEM((DEVICES, 128), I32),
        pltpu.SMEM((DEVICES, 128), I32),
        pltpu.VMEM((height + 2, breadth + 16, channels), F32),
        pltpu.VMEM((n_cells, 256), F32),
        pltpu.VMEM((n_cells, 128), F32),
        pltpu.VMEM((n_cells, 256), BF16),
        pltpu.VMEM((n_cells, 512), F32),
        pltpu.VMEM((n_cells, 512), BF16),
        pltpu.VMEM((n_cells, 128), BF16),
        pltpu.VMEM((128, n_cells), BF16),
        pltpu.VMEM((n_cells, 256), F32),
        pltpu.VMEM((512, 256), BF16),
        pltpu.VMEM((256, 512), BF16),
        pltpu.VMEM((128, 256), BF16),
        pltpu.VMEM((256, 128), BF16),
        pltpu.VMEM((128, 256), BF16),
        pltpu.VMEM((16, 256), F32),
        pltpu.VMEM((1, 256), F32),
        pltpu.VMEM((256, 512), F32),
        pltpu.VMEM((256, 512), F32),
        pltpu.VMEM((1, 128), F32),
        pltpu.VMEM((128, 256), F32),
        pltpu.VMEM((128, 256), F32),
        pltpu.VMEM((32, 128), F32),
        pltpu.VMEM((LATE, 128), BF16),
        pltpu.VMEM((DEVICES, PIECE, 128), BF16),
        pltpu.VMEM((LATE, 128), BF16),
        pltpu.VMEM((EARLY, 128), BF16),
        pltpu.VMEM((HALF, 128), BF16),
        pltpu.VMEM((HALF, 128), F32),
        pltpu.VMEM((HALF, 128), F32),
        pltpu.VMEM((HALF, 128), F32),
        pltpu.VMEM((HALF, 128), F32),
        pltpu.VMEM((EARLY, 128), BF16),
        pltpu.VMEM((2, 32, 128), F32),
        pltpu.VMEM((4, 32, 128), F32),
        pltpu.VMEM((4, 32, 128), F32),
        pltpu.VMEM((4, 32, 128), F32),
        pltpu.VMEM((16, channels), BF16),
        pltpu.VMEM((16, channels), BF16),
        pltpu.VMEM((breadth, channels), BF16),
        pltpu.VMEM((breadth, channels), BF16),
        pltpu.VMEM((6, 16, channels), BF16),
        pltpu.SemaphoreType.DMA((2,)),
        pltpu.SemaphoreType.DMA((8,)),
        pltpu.SemaphoreType.DMA((8,)),
        pltpu.SemaphoreType.DMA((4,)),
        pltpu.SemaphoreType.DMA((4,)),
        pltpu.SemaphoreType.DMA,
        pltpu.SemaphoreType.DMA((GROUPS,)),
        pltpu.SemaphoreType.DMA,
        pltpu.SemaphoreType.DMA((GROUPS,)),
        pltpu.SemaphoreType.DMA((4,)),
        pltpu.SemaphoreType.DMA,
        pltpu.SemaphoreType.DMA,
        pltpu.SemaphoreType.DMA,
        pltpu.SemaphoreType.DMA,
        pltpu.SemaphoreType.DMA((6,)),
        pltpu.SemaphoreType.DMA((6,)),
        pltpu.SemaphoreType.DMA((4,)),
        pltpu.SemaphoreType.DMA((4,)),
    ]
    anew, onew_arr, inv, late, early, small = pl.pallas_call(
        kernel,
        out_shape=[
            jax.ShapeDtypeStruct((height, breadth, channels), BF16),
            jax.ShapeDtypeStruct((blocks, 32, 128), BF16),
            jax.ShapeDtypeStruct((8, 256), I32),
            jax.ShapeDtypeStruct((LATE, 128), BF16),
            jax.ShapeDtypeStruct((EARLY, 128), BF16),
            jax.ShapeDtypeStruct((32, 128), F32),
        ],
        in_specs=[vmem] * 14 + [any_] * 2,
        out_specs=[vmem, any_, vmem, any_, any_, any_],
        scratch_shapes=scratch,
        compiler_params=pltpu.CompilerParams(
            collective_id=0, has_side_effects=True, vmem_limit_bytes=56 * 1024 * 1024
        ),
    )(
        atm_state, kernel_taps, atm_gain.reshape(1, -1), atm_up, atm_down, couple_weight,
        ocean_gain.reshape(1, -1), ocean_up, ocean_down, land_mask.T, margin_cell.transpose(1, 2, 0),
        margin_area.transpose(1, 2, 0), owner_slot.reshape(1, -1), atm_cotangent, ocean_state, ocean_cotangent,
    )
    part = blocks // 4
    whole = lambda *shape: pl.BlockSpec(shape, lambda i: (0,) * len(shape))
    anew, onew, gtaps, gagain, gup, gdown, gcouple, gogain, goup, godown = pl.pallas_call(
        finish,
        grid=(4,),
        out_shape=[
            jax.ShapeDtypeStruct((height, breadth, channels), BF16),
            jax.ShapeDtypeStruct((blocks, 32, 128), BF16),
            jax.ShapeDtypeStruct((3, 3, 256), F32),
            jax.ShapeDtypeStruct((1, 256), F32),
            jax.ShapeDtypeStruct((256, 512), F32),
            jax.ShapeDtypeStruct((512, 256), F32),
            jax.ShapeDtypeStruct((256, 128), F32),
            jax.ShapeDtypeStruct((1, 128), F32),
            jax.ShapeDtypeStruct((128, 256), F32),
            jax.ShapeDtypeStruct((256, 128), F32),
        ],
        in_specs=[
            pl.BlockSpec(memory_space=pltpu.SMEM),
            whole(height, breadth, channels), whole(blocks, 32, 128),
            whole(LATE, 128), whole(EARLY, 128), whole(32, 128),
        ],
        out_specs=[
            whole(height, breadth, channels), pl.BlockSpec((part, 32, 128), lambda i: (i, 0, 0)), whole(3, 3, 256),
            whole(1, 256), whole(256, 512), whole(512, 256), whole(256, 128), whole(1, 128), whole(128, 256),
            whole(256, 128),
        ],
        compiler_params=pltpu.CompilerParams(vmem_limit_bytes=60 * 1024 * 1024),
    )(inv, anew, onew_arr, late, early, small)
    return (
        anew, onew, gtaps, gagain.reshape(-1), gup, gdown, gcouple, gogain.reshape(-1), goup, godown,
    )


def solution(mesh):
    both = ("tx", "ty")
    return jax.shard_map(
        body,
        mesh=mesh,
        in_specs=(P("ty", "tx", None),) + (P(),) * 8 + (
            P(both, None, None), P(both, None), P(both, None, None), P(both, None, None), P(both),
            P("ty", "tx", None), P(both, None, None),
        ),
        out_specs=(P("ty", "tx", None), P(both, None, None)) + (P(),) * 8,
        check_vma=False,
    )
```

```python
import functools

import jax
import jax.numpy as jnp
from jax import lax
from jax.experimental import pallas as pl
from jax.experimental.pallas import tpu as pltpu
from jax.sharding import PartitionSpec as P

EPS = 1e-06
MESH = pl.DeviceIdType.MESH
F32, BF16, I32 = jnp.float32, jnp.bfloat16, jnp.int32
DEVICES = 128
ROWS = 64
GROUP = 8
GROUPS = DEVICES // GROUP
PIECE = 16
LATE = DEVICES * PIECE
EARLY = 768
HALF, QUARTER = EARLY // 2, EARLY // 8


def digits(tx, ty):
    return (tx // 4) * 2 + ty // 8, (ty // 2) % 4, tx % 4, ty % 2


def rem(a, n):
    return lax.rem(a, jnp.int32(n))


def div(a, n):
    return lax.div(a, jnp.int32(n))


def device(x, y, z, c):
    return (div(x, 2) * 4 + z, rem(x, 2) * 8 + y * 2 + c)


def group_devices(me, sign, low, turn, cores):
    found = []
    for j in range(GROUP):
        dx, two = j % 4, j // 4 * 2
        x = rem(me[0] + 4 + sign * dx, 4)
        y = rem(me[1] + 8 + sign * (turn + dx), 4)
        z = rem(me[2] + 8 + sign * (low + two + dx), 4)
        found.append(device(x, y, z, cores))
    return found


def step_devices(me, g, sign):
    return group_devices(me, sign, rem(div(g, 2), 2), div(g, 4), rem(me[3] + g, 2))


def step_codes(g):
    low, turn, dc = rem(div(g, 2), 2), div(g, 4), rem(g, 2)
    return [
        ((rem(low + j // 4 * 2 + j % 4, 4) * 4 + rem(turn + j % 4, 4)) * 4 + j % 4) * 2 + dc for j in range(GROUP)
    ]


def step_of(dx, dy, dz, dc):
    t, turn = (dz - dx) & 3, (dy - dx) & 3
    return (dc + 2 * (t & 1) + 4 * turn) * GROUP + dx + 4 * (t >> 1)


def rank_of(tx, ty):
    return rem(ty, 2) * (DEVICES // 2) + tx * 8 + div(ty, 2)


def sigmoid(v):
    return 0.5 * jnp.tanh(0.5 * v) + 0.5


def dot(a, b):
    return jnp.dot(a, b, preferred_element_type=F32)


def dot_t(a, b):
    return lax.dot_general(a, b, (((1,), (1,)), ((), ())), preferred_element_type=F32)


def t_dot(a, b):
    return lax.dot_general(a, b, (((0,), (0,)), ((), ())), preferred_element_type=F32)


def loop(n, f):
    lax.fori_loop(0, n, lambda i, c: (f(i), c)[1], 0)


def kernel(
    atm, taps, again, up, down, couple, ogain, oup, odown, mask, margin_cell, margin_area, owner, acot, ostate_hbm, ocot_hbm,
    anew, onew_hbm, late_hbm, early_hbm, small_hbm,
    ostate, ocot, wet, cells, shares, spread, flux_out, flux_in, back_out, back_in, onew, onew_arr, owners, slots_v, slots_s, inv_v, inv_s,
    win, unit, inv_rms, normed, pre, act, gather, coupled_t, out_grad, pre_grad, act_t, normed_t, anew_t, sgrad, up_t, down_t, couple_t, oup_t, odown_t,
    gtaps, gagain, gogain, goup, godown_t, small, late, pieces, late_sum,
    early, early_core, early_mine, early_x, early_y, early_z, early_sum, small_core, small_x, small_y, small_z,
    edge_w, edge_e, halo_n, halo_s, halo_c,
    load_sem, halo_ssem, halo_rsem, own_ssem, own_rsem, flux_ssem, flux_rsem, back_ssem, back_rsem, misc_sem,
    met, late_ssem, late_rsem, sum_ssem, sum_rsem, early_ssem, early_rsem, small_ssem, small_rsem,
):
    tx, ty = lax.axis_index("tx"), lax.axis_index("ty")
    me = digits(tx, ty)
    height, breadth = atm.shape[0], atm.shape[1]
    n_cells = height * breadth

    barrier = pltpu.get_barrier_semaphore()
    loads = [
        pltpu.make_async_copy(ostate_hbm, ostate, load_sem.at[0]),
        pltpu.make_async_copy(ocot_hbm, ocot, load_sem.at[1]),
    ]
    for load in loads:
        load.start()

    xs = [rem(me[0] + i, 4) for i in range(4)]
    ys = [rem(me[1] + i, 4) for i in range(4)]
    zs = [rem(me[2] + i, 4) for i in range(4)]
    cs = [me[3], 1 - me[3]]
    partner = device(xs[0], ys[0], zs[0], cs[1])
    x_peers = [device(xs[i], ys[0], zs[0], cs[0]) for i in (1, 3, 2)]
    y_peers = [device(xs[0], ys[i], zs[0], cs[0]) for i in (1, 3, 2)]
    z_peers = [device(xs[0], ys[0], zs[i], cs[0]) for i in (1, 3, 2)]

    te, tw, ts, tn = rem(tx + 1, 8), rem(tx + 7, 8), rem(ty + 1, 16), rem(ty + 15, 16)
    around = [(tx, tn), (tx, ts)] + [(side, row) for side in (te, tw) for row in (tn, ty, ts)]
    greeted = [partner] + x_peers + y_peers + z_peers + around
    for to in greeted:
        pl.semaphore_signal(barrier, inc=1, device_id=to, device_id_type=MESH)

    def meet(i, peers):
        for to in peers:
            pl.semaphore_signal(met.at[i], inc=1, device_id=to, device_id_type=MESH)

    def remote(src, dst, ssem, rsem, to):
        return pltpu.make_async_remote_copy(src, dst, ssem, rsem, device_id=to, device_id_type=MESH)

    def both_ends(ref, ssem, rsem):
        return remote(ref, ref, ssem, rsem, partner)

    edge_w[...] = jnp.zeros_like(edge_w)
    edge_e[...] = jnp.zeros_like(edge_e)

    def own_rows(y):
        win[y + 1, 8 : 8 + breadth, :] = atm[y].astype(F32)

    loop(height, own_rows)
    west = jnp.concatenate([win[y + 1, 8:9, :] for y in range(height)], axis=0)
    east = jnp.concatenate([win[y + 1, 7 + breadth : 8 + breadth, :] for y in range(height)], axis=0)
    nothing = jnp.zeros_like(west)
    edge_w[...] = jnp.concatenate([west, nothing], axis=0).astype(BF16)
    edge_e[...] = jnp.concatenate([east, nothing], axis=0).astype(BF16)

    pl.semaphore_wait(barrier, len(greeted))
    meet(0, y_peers)

    north, south = ty > 0, ty < 15

    def halo(i, src, dst, dx, dy):
        return pltpu.make_async_remote_copy(
            src, dst, halo_ssem.at[i], halo_rsem.at[i], device_id=(dx, dy), device_id_type=MESH
        )

    copies = [
        (south, halo(0, atm.at[height - 1], halo_n, tx, ts)),
        (north, halo(1, atm.at[0], halo_s, tx, tn)),
        (None, halo(2, edge_e, halo_c.at[0], te, ty)),
        (None, halo(3, edge_w, halo_c.at[1], tw, ty)),
        (south, halo(4, edge_e, halo_c.at[2], te, ts)),
        (south, halo(5, edge_w, halo_c.at[3], tw, ts)),
        (north, halo(6, edge_e, halo_c.at[4], te, tn)),
        (north, halo(7, edge_w, halo_c.at[5], tw, tn)),
    ]

    def when(cond, f):
        if cond is None:
            f()
        else:
            pl.when(cond)(f)

    for cond, copy in copies:
        when(cond, copy.start)

    owners[0:1, :] = owner[...]

    def own_phase(i, rows, peers):
        for n, to in zip((1, 3, 2), peers):
            remote(
                owners.at[pl.ds(0, rows)], owners.at[pl.ds(n * rows, rows)], own_ssem.at[i], own_rsem.at[i], to
            ).start()

    def own_wait(i, rows, peers):
        both_ends(owners.at[pl.ds(rows, rows * peers)], own_ssem.at[i], own_rsem.at[i]).wait_recv()

    own_phase(0, 1, [partner])

    slot = owner[...]
    t_tx, t_ty = slot >> 12, (slot >> 8) & 15
    theirs = ((t_tx >> 2) * 2 + (t_ty >> 3), (t_ty >> 1) & 3, t_tx & 3, t_ty & 1)
    dx, dy, dz, dc = [(t - m + n) & (n - 1) for t, m, n in zip(theirs, me, (4, 4, 4, 2))]
    step = step_of(dx, dy, dz, dc)
    blocks = slot.shape[1]
    square = jnp.broadcast_to(step, (blocks, blocks))
    first = lax.broadcasted_iota(I32, square.shape, 0)
    second = lax.broadcasted_iota(I32, square.shape, 1)
    same = (square.astype(F32).T == square.astype(F32)) & (first < second)
    place = 2 * step + jnp.sum(same.astype(F32), axis=0, keepdims=True).astype(I32)

    area = margin_area[...]
    share = (area / jnp.sum(area, axis=0, keepdims=True)).reshape(128, blocks).astype(BF16)
    cell = margin_cell[...].reshape(128, blocks)
    high, low = (cell >> 4).astype(F32).astype(BF16), (cell & 15).astype(F32).astype(BF16)
    quads = lax.broadcasted_iota(I32, (blocks // 4, blocks), 0)
    lane_block = lax.broadcasted_iota(I32, (blocks // 4, 128), 1) // 32
    got_share = [jnp.zeros((blocks // 4, 128), F32)] * 4
    got_cell = [jnp.zeros((blocks // 4, 128), F32)] * 4
    for j in range(4):
        pick = (place == 4 * quads + j).astype(F32).astype(BF16)
        one_share = dot_t(pick, share)
        one_cell = 16.0 * dot_t(pick, high) + dot_t(pick, low)
        for k in range(4):
            turn = (32 * (j - k)) % 128
            here = lane_block == j
            got_share[k] = jnp.where(here, pltpu.roll(one_share, turn, 1) if turn else one_share, got_share[k])
            got_cell[k] = jnp.where(here, pltpu.roll(one_cell, turn, 1) if turn else one_cell, got_cell[k])
    for k in range(4):
        shares[k] = got_share[k]
        cells[k] = got_cell[k].astype(I32)

    pl.semaphore_wait(met.at[0], 3)
    meet(1, z_peers)
    own_wait(0, 1, 1)
    own_phase(1, 2, x_peers)
    def spread_columns(i):
        here = pl.ds(pl.multiple_of(i * 128, 128), 128)
        row = pl.ds(i, 1)
        rows = lax.broadcasted_iota(I32, (n_cells // 16, 16, 128), 0) * 16 + lax.broadcasted_iota(
            I32, (n_cells // 16, 16, 128), 1
        )
        rows = rows.astype(jnp.int16)
        total = None
        for k in range(4):
            cell_k = jnp.broadcast_to(cells[k, row, :], (16, 128)).astype(jnp.int16)
            share_k = jnp.broadcast_to(shares[k, row, :], (16, 128)).astype(BF16)
            part = jnp.where(rows == cell_k[None], share_k[None], jnp.zeros((), BF16))
            total = part if total is None else total + part
        spread[:, here] = total.reshape(n_cells, 128)

    couple_t[...] = couple[...].astype(F32).T.astype(BF16)
    pl.semaphore_wait(met.at[1], 3)
    meet(2, [partner])

    for cond, copy in copies:
        when(cond, copy.wait_send)
    receives = [north, south, None, None, north, north, south, south]
    for cond, (_, copy) in zip(receives, copies):
        when(cond, copy.wait_recv)

    @pl.when(north)
    def _():
        win[0, 8 : 8 + breadth, :] = halo_n[...].astype(F32)
        win[0, 7:8, :] = halo_c[2].astype(F32)[height - 1 : height]
        win[0, 8 + breadth : 9 + breadth, :] = halo_c[3].astype(F32)[height - 1 : height]

    @pl.when(jnp.logical_not(north))
    def _():
        win[0] = jnp.zeros(win.shape[1:], F32)

    @pl.when(south)
    def _():
        win[height + 1, 8 : 8 + breadth, :] = halo_s[...].astype(F32)
        win[height + 1, 7:8, :] = halo_c[4].astype(F32)[0:1]
        win[height + 1, 8 + breadth : 9 + breadth, :] = halo_c[5].astype(F32)[0:1]

    @pl.when(jnp.logical_not(south))
    def _():
        win[height + 1] = jnp.zeros(win.shape[1:], F32)

    west, east = halo_c[0].astype(F32), halo_c[1].astype(F32)
    for y in range(height):
        win[y + 1, 7:8, :] = west[y : y + 1]
        win[y + 1, 8 + breadth : 9 + breadth, :] = east[y : y + 1]

    def stencil_row(y):
        total = jnp.zeros((breadth, 256), F32)
        for a in range(3):
            for b in range(3):
                total = total + taps[a, b : b + 1, :] * win[y + a, 7 + b : 7 + b + breadth, :]
        inv = lax.rsqrt(jnp.mean(total * total, axis=-1, keepdims=True) + EPS)
        here = pl.ds(pl.multiple_of(y * breadth, breadth), breadth)
        u = total * inv
        unit[here, :] = u
        inv_rms[here, :] = jnp.broadcast_to(inv, (breadth, 128))
        normed[here, :] = (u * again[...]).astype(BF16)

    loop(height, stencil_row)

    def atm_mlp(i):
        here = pl.ds(pl.multiple_of(i * 128, 128), 128)
        v = dot(normed[here, :], up[...])
        pre[here, :] = v
        a = (v * sigmoid(v)).astype(BF16)
        act[here, :] = a
        old = atm[pl.ds(i * 2, 2)].reshape(128, 256).astype(F32)
        anew[pl.ds(i * 2, 2)] = (old + dot(a, down[...])).astype(BF16).reshape(2, breadth, 256)

    loop(4, atm_mlp)
    coupled_t[...] = dot_t(couple_t[...], anew[...].reshape(n_cells, 256)).astype(BF16)
    own_wait(1, 2, 3)
    own_phase(2, 8, y_peers)
    pl.semaphore_wait(met.at[2], 1)

    def send_group(g, sign, src, dst, ssem, rsem):
        for j, to in enumerate(step_devices(me, g, sign)):
            here = pl.ds(pl.multiple_of((g * GROUP + j) * ROWS, ROWS), ROWS)
            copy = remote(src.at[here], dst.at[here], ssem, rsem.at[g], to)
            when(g > 0 if j == 0 else None, copy.start)

    def flux_group(g):
        for j in range(GROUP // 2):
            spread_columns(g * (GROUP // 2) + j)
        here = pl.ds(pl.multiple_of(g * (GROUP * ROWS), GROUP * ROWS), GROUP * ROWS)
        flux_out[here, :] = dot(coupled_t[...], spread[:, here]).astype(BF16).T
        send_group(g, 1, flux_out, flux_in, flux_ssem, flux_rsem)

    loop(GROUPS // 2, flux_group)
    own_wait(2, 8, 3)
    own_phase(3, 32, z_peers)
    loop(GROUPS // 2, lambda g: flux_group(g + GROUPS // 2))
    flux_in[0:ROWS, :] = flux_out[0:ROWS, :]

    ones = jnp.ones((32, 128), BF16)
    wet_rows_of = mask[...].astype(F32).astype(BF16)

    def wet_rows(i):
        rows = lax.broadcasted_iota(I32, (512, blocks), 0)
        cols = lax.broadcasted_iota(I32, (512, blocks), 1)
        pick = (rows // 32 + i * 16 == cols).astype(F32).astype(BF16)
        wide = dot_t(pick, wet_rows_of)
        r2 = lax.broadcasted_iota(I32, wide.shape, 0)
        c2 = lax.broadcasted_iota(I32, wide.shape, 1)
        wide = jnp.where(r2 % 32 == c2, wide, 0.0).astype(BF16)
        wet[pl.ds(pl.multiple_of(i * 16, 16), 16)] = dot(wide, ones).astype(BF16).reshape(16, 32, 128)

    loop(16, wet_rows)

    loop(16, wet_rows)

    for weight, turned in ((oup, oup_t), (odown, odown_t)):
        turned[...] = weight[...].astype(F32).T.astype(BF16)

    own_wait(3, 32, 3)
    owned = owners[...]
    lane = lax.broadcasted_iota(I32, owned.shape, 1)
    hit = (owned >> 8) == tx * 16 + ty
    lane_f = lane.astype(F32)
    local = (owned & (blocks - 1)).astype(F32)
    one = jnp.min(jnp.where(hit, lane_f, 1e4), axis=1, keepdims=True)
    two = jnp.max(jnp.where(hit, lane_f, -1.0), axis=1, keepdims=True)
    one = jnp.sum(jnp.where(lane_f == one, local, 0.0), axis=1, keepdims=True).astype(I32)
    two = jnp.sum(jnp.where(lane_f == two, local, 0.0), axis=1, keepdims=True).astype(I32)
    code = lax.broadcasted_iota(I32, owned.shape, 0)
    position = 2 * step_of((code >> 1) & 3, (code >> 3) & 3, code >> 5, code & 1)
    found = jnp.where(one == lane, position, 0) + jnp.where(two == lane, position + 1, 0)
    inv_v[...] = jnp.broadcast_to(
        jnp.max(found.astype(F32), axis=0, keepdims=True).astype(I32), inv_v.shape
    )
    slots_v[...] = jnp.where(lane[:, 0:128] == 0, one, two)
    to_scalar = [
        pltpu.make_async_copy(slots_v, slots_s, misc_sem.at[0]),
        pltpu.make_async_copy(inv_v, inv_s, misc_sem.at[4]),
    ]
    for copy in to_scalar:
        copy.start()
    for copy in to_scalar:
        copy.wait()
    for load in loads:
        load.wait()

    goup[...] = jnp.zeros_like(goup)
    godown_t[...] = jnp.zeros_like(godown_t)
    gogain[...] = jnp.zeros_like(gogain)

    def wait_group(g, buf, ssem, rsem):
        def first():
            both_ends(buf.at[pl.ds(ROWS, (GROUP - 1) * ROWS)], ssem, rsem.at[0]).wait_recv()

        def later():
            here = pl.ds(pl.multiple_of(g * (GROUP * ROWS), GROUP * ROWS), GROUP * ROWS)
            both_ends(buf.at[here], ssem, rsem.at[g]).wait_recv()

        pl.when(g == 0)(first)
        pl.when(g > 0)(later)

    def ocean_group(g):
        wait_group(g, flux_in, flux_ssem, flux_rsem)
        here = pl.ds(pl.multiple_of(g * (GROUP * ROWS), GROUP * ROWS), GROUP * ROWS)
        codes = step_codes(g)
        slot = [slots_s[codes[j // 2], j % 2] & 255 for j in range(2 * GROUP)]
        state = jnp.concatenate([ostate[s] for s in slot], axis=0).astype(F32)
        wets = jnp.concatenate([wet[s] for s in slot], axis=0)
        wet_cot = jnp.concatenate([ocot[s] for s in slot], axis=0) * wets
        total = state + flux_in[here, :].astype(F32)
        inv = lax.rsqrt(jnp.mean(total * total, axis=-1, keepdims=True) + EPS)
        u = total * inv
        nrm = (u * ogain[...]).astype(BF16)
        v = dot(nrm, oup[...])
        s = sigmoid(v)
        a = (v * s).astype(BF16)
        onew_arr[pl.ds(g * (2 * GROUP), 2 * GROUP)] = (
            (state + wets.astype(F32) * dot(a, odown[...])).astype(BF16).reshape(2 * GROUP, 32, 128)
        )
        godown_t[...] += t_dot(wet_cot, a)
        pg = (dot(wet_cot, odown_t[...]) * (s * (1.0 + v * (1.0 - s)))).astype(BF16)
        goup[...] += t_dot(nrm, pg)
        ng = dot(pg, oup_t[...])
        gogain[...] += jnp.sum(ng * u, axis=0, keepdims=True)
        gg = ng * ogain[...]
        tg = inv * (gg - u * jnp.mean(gg * u, axis=-1, keepdims=True))
        back_out[here, :] = tg.astype(BF16)

        send_group(g, -1, back_out, back_in, back_ssem, back_rsem)

    loop(GROUPS, ocean_group)
    back_in[0:ROWS, :] = back_out[0:ROWS, :]

    for i in range(2):
        early[128 * i : 128 * (i + 1), :] = goup[:, 128 * i : 128 * (i + 1)].astype(BF16)
        early[256 + 128 * i : 256 + 128 * (i + 1), :] = godown_t[:, 128 * i : 128 * (i + 1)].T.astype(BF16)

    for weight, turned in ((up, up_t), (down, down_t)):
        turned[...] = weight[...].astype(F32).T.astype(BF16)
    for i in range(4):
        here = slice(128 * i, 128 * (i + 1))
        act_t[:, here] = act[here, :].T
        normed_t[:, here] = normed[here, :].T
        anew_t[:, here] = anew[2 * i : 2 * i + 2].reshape(128, 256).T

    sgrad[:, 0:128] = jnp.zeros((n_cells, 128), F32)

    def back_group(g):
        wait_group(g, back_in, back_ssem, back_rsem)
        here = pl.ds(pl.multiple_of(g * (GROUP * ROWS), GROUP * ROWS), GROUP * ROWS)
        sgrad[:, 0:128] += dot(spread[:, here], back_in[here, :])

    loop(GROUPS, back_group)
    gathered = sgrad[:, 0:128].astype(BF16)
    gather[...] = gathered
    early[512:768, :] = dot(anew_t[...], gathered).astype(BF16)

    x, y, z, c = me

    def span(i, n):
        return pl.ds(pl.multiple_of(i * n, n), n)

    def early_copy(i, src, dst, to):
        remote(src, dst, early_ssem.at[i], early_rsem.at[i], to).start()

    def early_wait(i, ref):
        both_ends(ref, early_ssem.at[i], early_rsem.at[i]).wait_recv()

    def add_four(ref):
        rows = ref.shape[0] // 4
        total = ref[0:rows, :]
        for i in range(1, 4):
            total = total + ref[i * rows : (i + 1) * rows, :]
        return total

    def early_0():
        early_copy(0, early.at[span(1 - c, HALF)], early_core, partner)

    def early_1():
        early_wait(0, early_core)
        early_mine[...] = early[span(c, HALF), :].astype(F32) + early_core[...].astype(F32)
        early_x[span(x, QUARTER), :] = early_mine[span(x, QUARTER), :]
        for n, to in zip((1, 3, 2), x_peers):
            early_copy(1, early_mine.at[span(xs[n], QUARTER)], early_x.at[span(x, QUARTER)], to)

    def early_2():
        early_wait(1, early_x.at[pl.ds(0, 3 * QUARTER)])
        early_y[span(y, QUARTER), :] = add_four(early_x)
        for to in y_peers:
            early_copy(2, early_y.at[span(y, QUARTER)], early_y.at[span(y, QUARTER)], to)

    def early_3():
        early_wait(2, early_y.at[pl.ds(0, 3 * QUARTER)])
        early_z[span(z, QUARTER), :] = add_four(early_y)
        for to in z_peers:
            early_copy(3, early_z.at[span(z, QUARTER)], early_z.at[span(z, QUARTER)], to)

    def early_4():
        early_wait(3, early_z.at[pl.ds(0, 3 * QUARTER)])
        here = span(c * 4 + x, QUARTER)
        early_sum[here, :] = add_four(early_z).astype(BF16)
        for to in x_peers:
            early_copy(4, early_sum.at[here], early_sum.at[here], to)

    def early_5():
        early_wait(4, early_sum.at[pl.ds(0, 3 * QUARTER)])
        here = span(c, HALF)
        early_copy(5, early_sum.at[here], early_sum.at[here], partner)

    def early_6():
        early_wait(5, early_sum.at[pl.ds(0, HALF)])

    early_0()
    def send_late(low):
        def group(g):
            for j, to in enumerate(group_devices(me, 1, rem(g, 2), div(g, 2), low)):
                copy = remote(
                    late.at[span(rank_of(*to), PIECE)], pieces.at[(g * GROUP + j) * 2 + c], late_ssem, late_rsem, to
                )
                when(jnp.logical_or(g > 0, c != low) if j == 0 else None, copy.start)

        loop(GROUPS // 2, group)

    def atm_out_grad(i):
        here = pl.ds(pl.multiple_of(i * 128, 128), 128)
        cot = acot[pl.ds(i * 2, 2)].reshape(128, 256).astype(F32)
        out_grad[here, :] = (cot + dot(gather[here, :], couple_t[...])).astype(BF16)

    loop(4, atm_out_grad)
    for i in range(2):
        half = dot(act_t[...], out_grad[:, 128 * i : 128 * (i + 1)])
        late[1024 + 512 * i : 1024 + 512 * (i + 1), :] = half.astype(BF16)
    send_late(1)

    def atm_back(i):
        here = pl.ds(pl.multiple_of(i * 128, 128), 128)
        v = pre[here, :]
        s = sigmoid(v)
        pre_grad[here, :] = (dot(out_grad[here, :], down_t[...]) * (s * (1.0 + v * (1.0 - s)))).astype(BF16)

    loop(4, atm_back)
    for i in range(4):
        late[256 * i : 256 * (i + 1), :] = dot(normed_t[...], pre_grad[:, 128 * i : 128 * (i + 1)]).astype(BF16)
    send_late(0)

    gagain[...] = jnp.zeros_like(gagain)
    gtaps[...] = jnp.zeros_like(gtaps)

    def atm_norm_back(i):
        here = pl.ds(pl.multiple_of(i * 128, 128), 128)
        ng = dot(pre_grad[here, :], up_t[...])
        u = unit[here, :]
        gagain[...] += jnp.sum(ng * u, axis=0, keepdims=True)
        gg = ng * again[...]
        sgrad[here, :] = inv_rms[here, 0:1] * (gg - u * jnp.mean(gg * u, axis=-1, keepdims=True))

    loop(4, atm_norm_back)
    early_1()

    def taps_row(y):
        sg = sgrad[pl.ds(pl.multiple_of(y * breadth, breadth), breadth), :]
        for a in range(3):
            for b in range(3):
                gtaps[3 * a + b : 3 * a + b + 1, :] += jnp.sum(
                    sg * win[y + a, 7 + b : 7 + b + breadth, :], axis=0, keepdims=True
                )

    loop(height, taps_row)

    small[...] = jnp.zeros_like(small)
    small[0:9, :] = gtaps[0:9, 0:128]
    small[9:18, :] = gtaps[0:9, 128:256]
    small[18:19, :] = gagain[:, 0:128]
    small[19:20, :] = gagain[:, 128:256]
    small[20:21, :] = gogain[...]

    def small_phase(i, value, buf, at, peers):
        buf[at] = value
        for to in peers:
            remote(buf.at[at], buf.at[at], small_ssem.at[i], small_rsem.at[i], to).start()

    def small_wait(i, buf):
        rest = buf.shape[0] - 1
        both_ends(buf.at[pl.ds(0, rest)], small_ssem.at[i], small_rsem.at[i]).wait_recv()
        total = buf[0]
        for n in range(rest):
            total = total + buf[n + 1]
        return total

    small_phase(0, small[...], small_core, c, [partner])
    small_phase(1, small_wait(0, small_core), small_x, x, x_peers)
    early_2()

    def place_blocks(i):
        for j in range(8):
            onew[i * 8 + j] = onew_arr[inv_s[0, i * 8 + j] & 255]

    loop(blocks // 8, place_blocks)
    store = pltpu.make_async_copy(onew, onew_hbm, misc_sem.at[1])
    store.start()
    early_3()
    mine = span(rank_of(tx, ty), PIECE)
    pieces[c] = late[mine, :]
    both_ends(pieces.at[pl.ds(1, DEVICES - 1)], late_ssem, late_rsem).wait_recv()

    def add(i, total):
        return total + jnp.sum(pieces[pl.ds(i * 8, 8)].astype(F32), axis=0)

    late_sum[mine, :] = lax.fori_loop(0, DEVICES // 8, add, jnp.zeros((PIECE, 128), F32)).astype(BF16)

    def send_sum(g):
        for j, to in enumerate(step_devices(me, g, 1)):
            copy = remote(late_sum.at[mine], late_sum.at[mine], sum_ssem, sum_rsem, to)
            when(g > 0 if j == 0 else None, copy.start)

    small_phase(2, small_wait(1, small_x), small_y, y, y_peers)
    early_4()
    loop(GROUPS, send_sum)
    small_phase(3, small_wait(2, small_y), small_z, z, z_peers)
    early_5()
    early_6()
    small[...] = small_wait(3, small_z)
    results = [
        pltpu.make_async_copy(early_sum, early_hbm, misc_sem.at[0]),
        pltpu.make_async_copy(small, small_hbm, misc_sem.at[2]),
        pltpu.make_async_copy(late_sum, late_hbm, misc_sem.at[3]),
    ]
    results[0].start()
    results[1].start()
    others = pl.ds(0, LATE - PIECE)
    both_ends(late_sum.at[others], sum_ssem, sum_rsem).wait_recv()
    results[2].start()
    both_ends(late.at[others], late_ssem, late_rsem).wait_send()
    both_ends(late.at[others], sum_ssem, sum_rsem).wait_send()
    for i, rows in ((0, 1), (1, 6), (2, 24), (3, 96)):
        both_ends(owners.at[pl.ds(0, rows)], own_ssem.at[i], own_rsem.at[i]).wait_send()
    for i, rows in enumerate((HALF, 3 * QUARTER, 3 * QUARTER, 3 * QUARTER, 3 * QUARTER, HALF)):
        sent = early_x if 0 < i < 4 else early
        both_ends(sent.at[pl.ds(0, rows)], early_ssem.at[i], early_rsem.at[i]).wait_send()
    for i, n in enumerate((1, 3, 3, 3)):
        both_ends(small_z.at[pl.ds(0, n)], small_ssem.at[i], small_rsem.at[i]).wait_send()

    both_ends(flux_out.at[pl.ds(ROWS, (DEVICES - 1) * ROWS)], flux_ssem, flux_rsem.at[0]).wait_send()
    both_ends(back_out.at[pl.ds(ROWS, (DEVICES - 1) * ROWS)], back_ssem, back_rsem.at[0]).wait_send()
    store.wait()
    for result in results:
        result.wait()


def finish(anew_in, onew_in, late_in, early_in, small_in, *refs):
    outs, (anew, onew, late, early, small), (gtaps, gagain, gup, gdown, gcouple, gogain, goup, godown), sem, osem = (
        refs[:10], refs[10:15], refs[15:23], refs[23], refs[24]
    )
    o_anew, o_onew, *o_grads = outs
    n = onew.shape[0] // 4
    parts = [pl.ds(i * n, n) for i in range(4)]
    loads = [
        pltpu.make_async_copy(src, dst, sem.at[i])
        for i, (src, dst) in enumerate(
            [(late_in, late), (early_in, early), (small_in, small), (anew_in, anew)]
            + [(onew_in.at[p], onew.at[p]) for p in parts]
        )
    ]
    for load in loads:
        load.start()
    stores = []

    def put(src, dst):
        stores.append(pltpu.make_async_copy(src, dst, osem.at[len(stores)]))
        stores[-1].start()

    loads[0].wait()
    for i in range(4):
        gup[:, 128 * i : 128 * (i + 1)] = late[256 * i : 256 * (i + 1), :].astype(F32)
    put(gup, o_grads[2])
    for i in range(2):
        gdown[:, 128 * i : 128 * (i + 1)] = late[1024 + 512 * i : 1024 + 512 * (i + 1), :].astype(F32)
    put(gdown, o_grads[3])
    for load in loads[1:4]:
        load.wait()
    put(anew, o_anew)
    for i in range(2):
        goup[:, 128 * i : 128 * (i + 1)] = early[128 * i : 128 * (i + 1), :].astype(F32)
    godown[...] = early[256:512, :].astype(F32)
    gcouple[...] = early[512:768, :].astype(F32)
    for a in range(3):
        for i in range(2):
            gtaps[a, :, 128 * i : 128 * (i + 1)] = small[9 * i + 3 * a : 9 * i + 3 * a + 3, :]
    gagain[:, 0:128] = small[18:19, :]
    gagain[:, 128:256] = small[19:20, :]
    gogain[...] = small[20:21, :]
    for i in (0, 1, 4, 5, 6, 7):
        put((gtaps, gagain, gup, gdown, gcouple, gogain, goup, godown)[i], o_grads[i])
    for load, p in zip(loads[4:], parts):
        load.wait()
        put(onew.at[p], o_onew.at[p])
    for store in stores:
        store.wait()


def body(
    atm_state, kernel_taps, atm_gain, atm_up, atm_down, couple_weight, ocean_gain, ocean_up, ocean_down,
    ocean_state, land_mask, margin_cell, margin_area, owner_slot, atm_cotangent, ocean_cotangent,
):
    height, breadth, channels = atm_state.shape
    blocks = ocean_state.shape[0]
    n_rows = blocks * 32
    n_cells = height * breadth
    vmem, any_ = pl.BlockSpec(memory_space=pltpu.VMEM), pl.BlockSpec(memory_space=pl.ANY)
    block = lambda: pltpu.VMEM((blocks, 32, 128), BF16)
    flat = lambda: pltpu.VMEM((n_rows, 128), BF16)
    scratch = [
        block(), block(), block(),
        pltpu.VMEM((4, blocks // 4, 128), I32),
        pltpu.VMEM((4, blocks // 4, 128), F32),
        pltpu.VMEM((n_cells, n_rows), BF16),
        flat(), flat(), flat(), flat(),
        block(), block(),
        pltpu.VMEM((DEVICES, blocks), I32),
        pltpu.VMEM((DEVICES, 128), I32),
        pltpu.SMEM((DEVICES, 128), I32),
        pltpu.VMEM((8, blocks), I32),
        pltpu.SMEM((8, blocks), I32),
        pltpu.VMEM((height + 2, breadth + 16, channels), F32),
        pltpu.VMEM((n_cells, 256), F32),
        pltpu.VMEM((n_cells, 128), F32),
        pltpu.VMEM((n_cells, 256), BF16),
        pltpu.VMEM((n_cells, 512), F32),
        pltpu.VMEM((n_cells, 512), BF16),
        pltpu.VMEM((n_cells, 128), BF16),
        pltpu.VMEM((128, n_cells), BF16),
        pltpu.VMEM((n_cells, 256), BF16),
        pltpu.VMEM((n_cells, 512), BF16),
        pltpu.VMEM((512, n_cells), BF16),
        pltpu.VMEM((256, n_cells), BF16),
        pltpu.VMEM((256, n_cells), BF16),
        pltpu.VMEM((n_cells, 256), F32),
        pltpu.VMEM((512, 256), BF16),
        pltpu.VMEM((256, 512), BF16),
        pltpu.VMEM((128, 256), BF16),
        pltpu.VMEM((256, 128), BF16),
        pltpu.VMEM((128, 256), BF16),
        pltpu.VMEM((16, 256), F32),
        pltpu.VMEM((1, 256), F32),
        pltpu.VMEM((1, 128), F32),
        pltpu.VMEM((128, 256), F32),
        pltpu.VMEM((128, 256), F32),
        pltpu.VMEM((32, 128), F32),
        pltpu.VMEM((LATE, 128), BF16),
        pltpu.VMEM((DEVICES, PIECE, 128), BF16),
        pltpu.VMEM((LATE, 128), BF16),
        pltpu.VMEM((EARLY, 128), BF16),
        pltpu.VMEM((HALF, 128), BF16),
        pltpu.VMEM((HALF, 128), F32),
        pltpu.VMEM((HALF, 128), F32),
        pltpu.VMEM((HALF, 128), F32),
        pltpu.VMEM((HALF, 128), F32),
        pltpu.VMEM((EARLY, 128), BF16),
        pltpu.VMEM((2, 32, 128), F32),
        pltpu.VMEM((4, 32, 128), F32),
        pltpu.VMEM((4, 32, 128), F32),
        pltpu.VMEM((4, 32, 128), F32),
        pltpu.VMEM((16, channels), BF16),
        pltpu.VMEM((16, channels), BF16),
        pltpu.VMEM((breadth, channels), BF16),
        pltpu.VMEM((breadth, channels), BF16),
        pltpu.VMEM((6, 16, channels), BF16),
        pltpu.SemaphoreType.DMA((2,)),
        pltpu.SemaphoreType.DMA((8,)),
        pltpu.SemaphoreType.DMA((8,)),
        pltpu.SemaphoreType.DMA((4,)),
        pltpu.SemaphoreType.DMA((4,)),
        pltpu.SemaphoreType.DMA,
        pltpu.SemaphoreType.DMA((GROUPS,)),
        pltpu.SemaphoreType.DMA,
        pltpu.SemaphoreType.DMA((GROUPS,)),
        pltpu.SemaphoreType.DMA((5,)),
        pltpu.SemaphoreType.REGULAR((3,)),
        pltpu.SemaphoreType.DMA,
        pltpu.SemaphoreType.DMA,
        pltpu.SemaphoreType.DMA,
        pltpu.SemaphoreType.DMA,
        pltpu.SemaphoreType.DMA((6,)),
        pltpu.SemaphoreType.DMA((6,)),
        pltpu.SemaphoreType.DMA((4,)),
        pltpu.SemaphoreType.DMA((4,)),
    ]
    anew, onew, late, early, small = pl.pallas_call(
        kernel,
        out_shape=[
            jax.ShapeDtypeStruct((height, breadth, channels), BF16),
            jax.ShapeDtypeStruct((blocks, 32, 128), BF16),
            jax.ShapeDtypeStruct((LATE, 128), BF16),
            jax.ShapeDtypeStruct((EARLY, 128), BF16),
            jax.ShapeDtypeStruct((32, 128), F32),
        ],
        in_specs=[vmem] * 14 + [any_] * 2,
        out_specs=[vmem, any_, any_, any_, any_],
        scratch_shapes=scratch,
        compiler_params=pltpu.CompilerParams(
            collective_id=0, has_side_effects=True, vmem_limit_bytes=56 * 1024 * 1024
        ),
    )(
        atm_state, kernel_taps, atm_gain.reshape(1, -1), atm_up, atm_down, couple_weight,
        ocean_gain.reshape(1, -1), ocean_up, ocean_down, land_mask.T, margin_cell.transpose(1, 2, 0),
        margin_area.transpose(1, 2, 0), owner_slot.reshape(1, -1), atm_cotangent, ocean_state, ocean_cotangent,
    )
    anew, onew, gtaps, gagain, gup, gdown, gcouple, gogain, goup, godown = pl.pallas_call(
        finish,
        out_shape=[
            jax.ShapeDtypeStruct((height, breadth, channels), BF16),
            jax.ShapeDtypeStruct((blocks, 32, 128), BF16),
            jax.ShapeDtypeStruct((3, 3, 256), F32),
            jax.ShapeDtypeStruct((1, 256), F32),
            jax.ShapeDtypeStruct((256, 512), F32),
            jax.ShapeDtypeStruct((512, 256), F32),
            jax.ShapeDtypeStruct((256, 128), F32),
            jax.ShapeDtypeStruct((1, 128), F32),
            jax.ShapeDtypeStruct((128, 256), F32),
            jax.ShapeDtypeStruct((256, 128), F32),
        ],
        in_specs=[any_] * 5,
        out_specs=[any_] * 10,
        scratch_shapes=[
            pltpu.VMEM((height, breadth, channels), BF16), block(), pltpu.VMEM((LATE, 128), BF16),
            pltpu.VMEM((EARLY, 128), BF16), pltpu.VMEM((32, 128), F32),
            pltpu.VMEM((3, 3, 256), F32), pltpu.VMEM((1, 256), F32), pltpu.VMEM((256, 512), F32),
            pltpu.VMEM((512, 256), F32), pltpu.VMEM((256, 128), F32), pltpu.VMEM((1, 128), F32),
            pltpu.VMEM((128, 256), F32), pltpu.VMEM((256, 128), F32),
            pltpu.SemaphoreType.DMA((8,)), pltpu.SemaphoreType.DMA((13,)),
        ],
        compiler_params=pltpu.CompilerParams(vmem_limit_bytes=60 * 1024 * 1024),
    )(anew, onew, late, early, small)
    return (
        anew, onew, gtaps, gagain.reshape(-1), gup, gdown, gcouple, gogain.reshape(-1), goup, godown,
    )


def solution(mesh):
    both = ("tx", "ty")
    return jax.shard_map(
        body,
        mesh=mesh,
        in_specs=(P("ty", "tx", None),) + (P(),) * 8 + (
            P(both, None, None), P(both, None), P(both, None, None), P(both, None, None), P(both),
            P("ty", "tx", None), P(both, None, None),
        ),
        out_specs=(P("ty", "tx", None), P(both, None, None)) + (P(),) * 8,
        check_vma=False,
    )
```

```python
import functools

import jax
import jax.numpy as jnp
from jax import lax
from jax.experimental import pallas as pl
from jax.experimental.pallas import tpu as pltpu
from jax.sharding import PartitionSpec as P

EPS = 1e-06
MESH = pl.DeviceIdType.MESH
F32, BF16, I32 = jnp.float32, jnp.bfloat16, jnp.int32
DEVICES = 128
ROWS = 64
GROUP = 8
GROUPS = DEVICES // GROUP
AHEAD = 9
PIECE = 16
LATE = DEVICES * PIECE
EARLY = 768
HALF, QUARTER = EARLY // 2, EARLY // 8


def digits(tx, ty):
    return (tx // 4) * 2 + ty // 8, (ty // 2) % 4, tx % 4, ty % 2


def rem(a, n):
    return lax.rem(a, jnp.int32(n))


def div(a, n):
    return lax.div(a, jnp.int32(n))


def device(x, y, z, c):
    return (div(x, 2) * 4 + z, rem(x, 2) * 8 + y * 2 + c)


def group_devices(me, sign, low, turn, cores):
    found = []
    for j in range(GROUP):
        dx, two = j % 4, j // 4 * 2
        x = rem(me[0] + 4 + sign * dx, 4)
        y = rem(me[1] + 8 + sign * (turn + dx), 4)
        z = rem(me[2] + 8 + sign * (low + two + dx), 4)
        found.append(device(x, y, z, cores))
    return found


def step_devices(me, g, sign):
    return group_devices(me, sign, rem(div(g, 2), 2), div(g, 4), rem(me[3] + g, 2))


def step_codes(g):
    low, turn, dc = rem(div(g, 2), 2), div(g, 4), rem(g, 2)
    return [
        ((rem(low + j // 4 * 2 + j % 4, 4) * 4 + rem(turn + j % 4, 4)) * 4 + j % 4) * 2 + dc for j in range(GROUP)
    ]


def step_of(dx, dy, dz, dc):
    t, turn = (dz - dx) & 3, (dy - dx) & 3
    return (dc + 2 * (t & 1) + 4 * turn) * GROUP + dx + 4 * (t >> 1)


def rank_of(tx, ty):
    return rem(ty, 2) * (DEVICES // 2) + tx * 8 + div(ty, 2)


def sigmoid(v):
    return 0.5 * jnp.tanh(0.5 * v) + 0.5


def dot(a, b):
    return jnp.dot(a, b, preferred_element_type=F32)


def dot_t(a, b):
    return lax.dot_general(a, b, (((1,), (1,)), ((), ())), preferred_element_type=F32)


def t_dot(a, b):
    return lax.dot_general(a, b, (((0,), (0,)), ((), ())), preferred_element_type=F32)


def loop(n, f):
    lax.fori_loop(0, n, lambda i, c: (f(i), c)[1], 0)


def kernel(
    atm, taps, again, up, down, couple, ogain, oup, odown, mask, margin_cell, margin_area, owner, acot, ostate_hbm, ocot_hbm,
    anew, onew_hbm, late_hbm, early_hbm, small_hbm,
    ostate, ocot, wet, cells, shares, spread, flux_out, flux_in, back_out, back_in, onew, onew_arr, owners, slots_v, slots_s, inv_v, inv_s,
    win, unit, inv_rms, normed, pre, act, gather, coupled_t, out_grad, pre_grad, act_t, normed_t, anew_t, sgrad, up_t, down_t, couple_t, oup_t, odown_t,
    gtaps, gagain, gogain, goup, godown_t, small, late, pieces, late_sum,
    early, early_core, early_mine, early_x, early_y, early_z, early_sum, small_core, small_x, small_y, small_z,
    edge_w, edge_e, halo_n, halo_s, halo_c,
    load_sem, halo_ssem, halo_rsem, own_ssem, own_rsem, flux_ssem, flux_rsem, back_ssem, back_rsem, misc_sem,
    met, late_ssem, late_rsem, sum_ssem, sum_rsem, early_ssem, early_rsem, small_ssem, small_rsem,
):
    tx, ty = lax.axis_index("tx"), lax.axis_index("ty")
    me = digits(tx, ty)
    height, breadth = atm.shape[0], atm.shape[1]
    n_cells = height * breadth

    barrier = pltpu.get_barrier_semaphore()
    loads = [
        pltpu.make_async_copy(ostate_hbm, ostate, load_sem.at[0]),
        pltpu.make_async_copy(ocot_hbm, ocot, load_sem.at[1]),
    ]
    for load in loads:
        load.start()

    xs = [rem(me[0] + i, 4) for i in range(4)]
    ys = [rem(me[1] + i, 4) for i in range(4)]
    zs = [rem(me[2] + i, 4) for i in range(4)]
    cs = [me[3], 1 - me[3]]
    partner = device(xs[0], ys[0], zs[0], cs[1])
    x_peers = [device(xs[i], ys[0], zs[0], cs[0]) for i in (1, 3, 2)]
    y_peers = [device(xs[0], ys[i], zs[0], cs[0]) for i in (1, 3, 2)]
    z_peers = [device(xs[0], ys[0], zs[i], cs[0]) for i in (1, 3, 2)]

    te, tw, ts, tn = rem(tx + 1, 8), rem(tx + 7, 8), rem(ty + 1, 16), rem(ty + 15, 16)
    around = [(tx, tn), (tx, ts)] + [(side, row) for side in (te, tw) for row in (tn, ty, ts)]
    greeted = [partner] + x_peers + y_peers + z_peers + around
    for to in greeted:
        pl.semaphore_signal(barrier, inc=1, device_id=to, device_id_type=MESH)

    def meet(i, peers):
        for to in peers:
            pl.semaphore_signal(met.at[i], inc=1, device_id=to, device_id_type=MESH)

    def remote(src, dst, ssem, rsem, to):
        return pltpu.make_async_remote_copy(src, dst, ssem, rsem, device_id=to, device_id_type=MESH)

    def both_ends(ref, ssem, rsem):
        return remote(ref, ref, ssem, rsem, partner)

    edge_w[...] = jnp.zeros_like(edge_w)
    edge_e[...] = jnp.zeros_like(edge_e)

    def own_rows(y):
        win[y + 1, 8 : 8 + breadth, :] = atm[y].astype(F32)

    loop(height, own_rows)
    west = jnp.concatenate([win[y + 1, 8:9, :] for y in range(height)], axis=0)
    east = jnp.concatenate([win[y + 1, 7 + breadth : 8 + breadth, :] for y in range(height)], axis=0)
    nothing = jnp.zeros_like(west)
    edge_w[...] = jnp.concatenate([west, nothing], axis=0).astype(BF16)
    edge_e[...] = jnp.concatenate([east, nothing], axis=0).astype(BF16)

    pl.semaphore_wait(barrier, len(greeted))
    meet(0, y_peers)

    north, south = ty > 0, ty < 15

    def halo(i, src, dst, dx, dy):
        return pltpu.make_async_remote_copy(
            src, dst, halo_ssem.at[i], halo_rsem.at[i], device_id=(dx, dy), device_id_type=MESH
        )

    copies = [
        (south, halo(0, atm.at[height - 1], halo_n, tx, ts)),
        (north, halo(1, atm.at[0], halo_s, tx, tn)),
        (None, halo(2, edge_e, halo_c.at[0], te, ty)),
        (None, halo(3, edge_w, halo_c.at[1], tw, ty)),
        (south, halo(4, edge_e, halo_c.at[2], te, ts)),
        (south, halo(5, edge_w, halo_c.at[3], tw, ts)),
        (north, halo(6, edge_e, halo_c.at[4], te, tn)),
        (north, halo(7, edge_w, halo_c.at[5], tw, tn)),
    ]

    def when(cond, f):
        if cond is None:
            f()
        else:
            pl.when(cond)(f)

    for cond, copy in copies:
        when(cond, copy.start)

    owners[0:1, :] = owner[...]

    def own_phase(i, rows, peers):
        for n, to in zip((1, 3, 2), peers):
            remote(
                owners.at[pl.ds(0, rows)], owners.at[pl.ds(n * rows, rows)], own_ssem.at[i], own_rsem.at[i], to
            ).start()

    def own_wait(i, rows, peers):
        both_ends(owners.at[pl.ds(rows, rows * peers)], own_ssem.at[i], own_rsem.at[i]).wait_recv()

    own_phase(0, 1, [partner])

    slot = owner[...]
    t_tx, t_ty = slot >> 12, (slot >> 8) & 15
    theirs = ((t_tx >> 2) * 2 + (t_ty >> 3), (t_ty >> 1) & 3, t_tx & 3, t_ty & 1)
    dx, dy, dz, dc = [(t - m + n) & (n - 1) for t, m, n in zip(theirs, me, (4, 4, 4, 2))]
    step = step_of(dx, dy, dz, dc)
    blocks = slot.shape[1]
    square = jnp.broadcast_to(step, (blocks, blocks))
    first = lax.broadcasted_iota(I32, square.shape, 0)
    second = lax.broadcasted_iota(I32, square.shape, 1)
    same = (square.astype(F32).T == square.astype(F32)) & (first < second)
    place = 2 * step + jnp.sum(same.astype(F32), axis=0, keepdims=True).astype(I32)

    area = margin_area[...]
    share = (area / jnp.sum(area, axis=0, keepdims=True)).reshape(128, blocks).astype(BF16)
    cell = margin_cell[...].reshape(128, blocks)
    high, low = (cell >> 4).astype(F32).astype(BF16), (cell & 15).astype(F32).astype(BF16)
    quads = lax.broadcasted_iota(I32, (blocks // 4, blocks), 0)
    lane_block = lax.broadcasted_iota(I32, (blocks // 4, 128), 1) // 32
    got_share = [jnp.zeros((blocks // 4, 128), F32)] * 4
    got_cell = [jnp.zeros((blocks // 4, 128), F32)] * 4
    for j in range(4):
        pick = (place == 4 * quads + j).astype(F32).astype(BF16)
        one_share = dot_t(pick, share)
        one_cell = 16.0 * dot_t(pick, high) + dot_t(pick, low)
        for k in range(4):
            turn = (32 * (j - k)) % 128
            here = lane_block == j
            got_share[k] = jnp.where(here, pltpu.roll(one_share, turn, 1) if turn else one_share, got_share[k])
            got_cell[k] = jnp.where(here, pltpu.roll(one_cell, turn, 1) if turn else one_cell, got_cell[k])
    for k in range(4):
        shares[k] = got_share[k]
        cells[k] = got_cell[k].astype(I32)

    pl.semaphore_wait(met.at[0], 3)
    meet(1, z_peers)
    own_wait(0, 1, 1)
    own_phase(1, 2, x_peers)
    def spread_columns(i):
        here = pl.ds(pl.multiple_of(i * 128, 128), 128)
        row = pl.ds(i, 1)
        rows = lax.broadcasted_iota(I32, (n_cells // 16, 16, 128), 0) * 16 + lax.broadcasted_iota(
            I32, (n_cells // 16, 16, 128), 1
        )
        rows = rows.astype(jnp.int16)
        total = None
        for k in range(4):
            cell_k = jnp.broadcast_to(cells[k, row, :], (16, 128)).astype(jnp.int16)
            share_k = jnp.broadcast_to(shares[k, row, :], (16, 128)).astype(BF16)
            part = jnp.where(rows == cell_k[None], share_k[None], jnp.zeros((), BF16))
            total = part if total is None else total + part
        spread[:, here] = total.reshape(n_cells, 128)

    couple_t[...] = couple[...].astype(F32).T.astype(BF16)
    pl.semaphore_wait(met.at[1], 3)
    meet(2, [partner])

    for cond, copy in copies:
        when(cond, copy.wait_send)
    receives = [north, south, None, None, north, north, south, south]
    for cond, (_, copy) in zip(receives, copies):
        when(cond, copy.wait_recv)

    @pl.when(north)
    def _():
        win[0, 8 : 8 + breadth, :] = halo_n[...].astype(F32)
        win[0, 7:8, :] = halo_c[2].astype(F32)[height - 1 : height]
        win[0, 8 + breadth : 9 + breadth, :] = halo_c[3].astype(F32)[height - 1 : height]

    @pl.when(jnp.logical_not(north))
    def _():
        win[0] = jnp.zeros(win.shape[1:], F32)

    @pl.when(south)
    def _():
        win[height + 1, 8 : 8 + breadth, :] = halo_s[...].astype(F32)
        win[height + 1, 7:8, :] = halo_c[4].astype(F32)[0:1]
        win[height + 1, 8 + breadth : 9 + breadth, :] = halo_c[5].astype(F32)[0:1]

    @pl.when(jnp.logical_not(south))
    def _():
        win[height + 1] = jnp.zeros(win.shape[1:], F32)

    west, east = halo_c[0].astype(F32), halo_c[1].astype(F32)
    for y in range(height):
        win[y + 1, 7:8, :] = west[y : y + 1]
        win[y + 1, 8 + breadth : 9 + breadth, :] = east[y : y + 1]

    def stencil_row(y):
        total = jnp.zeros((breadth, 256), F32)
        for a in range(3):
            for b in range(3):
                total = total + taps[a, b : b + 1, :] * win[y + a, 7 + b : 7 + b + breadth, :]
        inv = lax.rsqrt(jnp.mean(total * total, axis=-1, keepdims=True) + EPS)
        here = pl.ds(pl.multiple_of(y * breadth, breadth), breadth)
        u = total * inv
        unit[here, :] = u
        inv_rms[here, :] = jnp.broadcast_to(inv, (breadth, 128))
        normed[here, :] = (u * again[...]).astype(BF16)

    loop(height, stencil_row)

    def atm_mlp(i):
        here = pl.ds(pl.multiple_of(i * 128, 128), 128)
        v = dot(normed[here, :], up[...])
        pre[here, :] = v
        a = (v * sigmoid(v)).astype(BF16)
        act[here, :] = a
        old = atm[pl.ds(i * 2, 2)].reshape(128, 256).astype(F32)
        anew[pl.ds(i * 2, 2)] = (old + dot(a, down[...])).astype(BF16).reshape(2, breadth, 256)

    loop(4, atm_mlp)
    coupled_t[...] = dot_t(couple_t[...], anew[...].reshape(n_cells, 256)).astype(BF16)
    own_wait(1, 2, 3)
    own_phase(2, 8, y_peers)
    pl.semaphore_wait(met.at[2], 1)

    def send_group(g, sign, src, dst, ssem, rsem):
        for j, to in enumerate(step_devices(me, g, sign)):
            here = pl.ds(pl.multiple_of((g * GROUP + j) * ROWS, ROWS), ROWS)
            copy = remote(src.at[here], dst.at[here], ssem, rsem.at[g], to)
            when(g > 0 if j == 0 else None, copy.start)

    def flux_group(g):
        for j in range(GROUP // 2):
            spread_columns(g * (GROUP // 2) + j)
        here = pl.ds(pl.multiple_of(g * (GROUP * ROWS), GROUP * ROWS), GROUP * ROWS)
        flux_out[here, :] = dot(coupled_t[...], spread[:, here]).astype(BF16).T
        send_group(g, 1, flux_out, flux_in, flux_ssem, flux_rsem)

    loop(4, flux_group)
    own_wait(2, 8, 3)
    own_phase(3, 32, z_peers)
    loop(AHEAD - 4, lambda g: flux_group(g + 4))
    flux_in[0:ROWS, :] = flux_out[0:ROWS, :]

    wet[...] = mask[...].astype(F32).T
    for weight, turned in ((oup, oup_t), (odown, odown_t)):
        turned[...] = weight[...].astype(F32).T.astype(BF16)

    own_wait(3, 32, 3)
    owned = owners[...]
    lane = lax.broadcasted_iota(I32, owned.shape, 1)
    hit = (owned >> 8) == tx * 16 + ty
    lane_f = lane.astype(F32)
    local = (owned & (blocks - 1)).astype(F32)
    one = jnp.min(jnp.where(hit, lane_f, 1e4), axis=1, keepdims=True)
    two = jnp.max(jnp.where(hit, lane_f, -1.0), axis=1, keepdims=True)
    one = jnp.sum(jnp.where(lane_f == one, local, 0.0), axis=1, keepdims=True).astype(I32)
    two = jnp.sum(jnp.where(lane_f == two, local, 0.0), axis=1, keepdims=True).astype(I32)
    code = lax.broadcasted_iota(I32, owned.shape, 0)
    position = 2 * step_of((code >> 1) & 3, (code >> 3) & 3, code >> 5, code & 1)
    found = jnp.where(one == lane, position, 0) + jnp.where(two == lane, position + 1, 0)
    inv_v[...] = jnp.broadcast_to(
        jnp.max(found.astype(F32), axis=0, keepdims=True).astype(I32), inv_v.shape
    )
    slots_v[...] = jnp.where(lane[:, 0:128] == 0, one, two)
    to_scalar = [
        pltpu.make_async_copy(slots_v, slots_s, misc_sem.at[0]),
        pltpu.make_async_copy(inv_v, inv_s, misc_sem.at[4]),
    ]
    for copy in to_scalar:
        copy.start()
    for copy in to_scalar:
        copy.wait()
    for load in loads:
        load.wait()

    goup[...] = jnp.zeros_like(goup)
    godown_t[...] = jnp.zeros_like(godown_t)
    gogain[...] = jnp.zeros_like(gogain)

    def wait_group(g, buf, ssem, rsem):
        def first():
            both_ends(buf.at[pl.ds(ROWS, (GROUP - 1) * ROWS)], ssem, rsem.at[0]).wait_recv()

        def later():
            here = pl.ds(pl.multiple_of(g * (GROUP * ROWS), GROUP * ROWS), GROUP * ROWS)
            both_ends(buf.at[here], ssem, rsem.at[g]).wait_recv()

        pl.when(g == 0)(first)
        pl.when(g > 0)(later)

    def ocean_group(g):
        wait_group(g, flux_in, flux_ssem, flux_rsem)
        here = pl.ds(pl.multiple_of(g * (GROUP * ROWS), GROUP * ROWS), GROUP * ROWS)
        codes = step_codes(g)
        slot = [slots_s[codes[j // 2], j % 2] & 255 for j in range(2 * GROUP)]
        state = jnp.concatenate([ostate[s] for s in slot], axis=0).astype(F32)
        eye = lax.broadcasted_iota(I32, (32, 32), 0) == lax.broadcasted_iota(I32, (32, 32), 1)
        wets = jnp.concatenate([jnp.where(eye, wet[pl.ds(s, 1), :], 0.0) for s in slot], axis=0).astype(BF16)
        wets = dot(wets, jnp.ones((32, 128), BF16))
        wet_cot = jnp.concatenate([ocot[s] for s in slot], axis=0) * wets.astype(BF16)
        total = state + flux_in[here, :].astype(F32)
        inv = lax.rsqrt(jnp.mean(total * total, axis=-1, keepdims=True) + EPS)
        u = total * inv
        nrm = (u * ogain[...]).astype(BF16)
        v = dot(nrm, oup[...])
        s = sigmoid(v)
        a = (v * s).astype(BF16)
        onew_arr[pl.ds(g * (2 * GROUP), 2 * GROUP)] = (
            (state + wets * dot(a, odown[...])).astype(BF16).reshape(2 * GROUP, 32, 128)
        )
        godown_t[...] += t_dot(wet_cot, a)
        pg = (dot(wet_cot, odown_t[...]) * (s * (1.0 + v * (1.0 - s)))).astype(BF16)
        goup[...] += t_dot(nrm, pg)
        ng = dot(pg, oup_t[...])
        gogain[...] += jnp.sum(ng * u, axis=0, keepdims=True)
        gg = ng * ogain[...]
        tg = inv * (gg - u * jnp.mean(gg * u, axis=-1, keepdims=True))
        back_out[here, :] = tg.astype(BF16)

        send_group(g, -1, back_out, back_in, back_ssem, back_rsem)

    def both_groups(g):
        flux_group(g + AHEAD)
        ocean_group(g)

    loop(GROUPS - AHEAD, both_groups)
    loop(AHEAD, lambda g: ocean_group(g + GROUPS - AHEAD))
    back_in[0:ROWS, :] = back_out[0:ROWS, :]

    for i in range(2):
        early[128 * i : 128 * (i + 1), :] = goup[:, 128 * i : 128 * (i + 1)].astype(BF16)
        early[256 + 128 * i : 256 + 128 * (i + 1), :] = godown_t[:, 128 * i : 128 * (i + 1)].T.astype(BF16)

    for weight, turned in ((up, up_t), (down, down_t)):
        turned[...] = weight[...].astype(F32).T.astype(BF16)
    for i in range(4):
        here = slice(128 * i, 128 * (i + 1))
        act_t[:, here] = act[here, :].T
        normed_t[:, here] = normed[here, :].T
        anew_t[:, here] = anew[2 * i : 2 * i + 2].reshape(128, 256).T

    sgrad[:, 0:128] = jnp.zeros((n_cells, 128), F32)

    def back_group(g):
        wait_group(g, back_in, back_ssem, back_rsem)
        here = pl.ds(pl.multiple_of(g * (GROUP * ROWS), GROUP * ROWS), GROUP * ROWS)
        sgrad[:, 0:128] += dot(spread[:, here], back_in[here, :])

    loop(GROUPS, back_group)
    gathered = sgrad[:, 0:128].astype(BF16)
    gather[...] = gathered
    early[512:768, :] = dot(anew_t[...], gathered).astype(BF16)

    x, y, z, c = me

    def span(i, n):
        return pl.ds(pl.multiple_of(i * n, n), n)

    def early_copy(i, src, dst, to):
        remote(src, dst, early_ssem.at[i], early_rsem.at[i], to).start()

    def early_wait(i, ref):
        both_ends(ref, early_ssem.at[i], early_rsem.at[i]).wait_recv()

    def add_four(ref):
        rows = ref.shape[0] // 4
        total = ref[0:rows, :]
        for i in range(1, 4):
            total = total + ref[i * rows : (i + 1) * rows, :]
        return total

    def early_0():
        early_copy(0, early.at[span(1 - c, HALF)], early_core, partner)

    def early_1():
        early_wait(0, early_core)
        early_mine[...] = early[span(c, HALF), :].astype(F32) + early_core[...].astype(F32)
        early_x[span(x, QUARTER), :] = early_mine[span(x, QUARTER), :]
        for n, to in zip((1, 3, 2), x_peers):
            early_copy(1, early_mine.at[span(xs[n], QUARTER)], early_x.at[span(x, QUARTER)], to)

    def early_2():
        early_wait(1, early_x.at[pl.ds(0, 3 * QUARTER)])
        early_y[span(y, QUARTER), :] = add_four(early_x)
        for to in y_peers:
            early_copy(2, early_y.at[span(y, QUARTER)], early_y.at[span(y, QUARTER)], to)

    def early_3():
        early_wait(2, early_y.at[pl.ds(0, 3 * QUARTER)])
        early_z[span(z, QUARTER), :] = add_four(early_y)
        for to in z_peers:
            early_copy(3, early_z.at[span(z, QUARTER)], early_z.at[span(z, QUARTER)], to)

    def early_4():
        early_wait(3, early_z.at[pl.ds(0, 3 * QUARTER)])
        here = span(c * 4 + x, QUARTER)
        early_sum[here, :] = add_four(early_z).astype(BF16)
        for to in x_peers:
            early_copy(4, early_sum.at[here], early_sum.at[here], to)

    def early_5():
        early_wait(4, early_sum.at[pl.ds(0, 3 * QUARTER)])
        here = span(c, HALF)
        early_copy(5, early_sum.at[here], early_sum.at[here], partner)

    def early_6():
        early_wait(5, early_sum.at[pl.ds(0, HALF)])

    early_0()
    def send_late(low):
        def group(g):
            for j, to in enumerate(group_devices(me, 1, rem(g, 2), div(g, 2), low)):
                copy = remote(
                    late.at[span(rank_of(*to), PIECE)], pieces.at[(g * GROUP + j) * 2 + c], late_ssem, late_rsem, to
                )
                when(jnp.logical_or(g > 0, c != low) if j == 0 else None, copy.start)

        loop(GROUPS // 2, group)

    def atm_out_grad(i):
        here = pl.ds(pl.multiple_of(i * 128, 128), 128)
        cot = acot[pl.ds(i * 2, 2)].reshape(128, 256).astype(F32)
        out_grad[here, :] = (cot + dot(gather[here, :], couple_t[...])).astype(BF16)

    loop(4, atm_out_grad)
    for i in range(2):
        half = dot(act_t[...], out_grad[:, 128 * i : 128 * (i + 1)])
        late[1024 + 512 * i : 1024 + 512 * (i + 1), :] = half.astype(BF16)
    send_late(1)
    early_1()

    def atm_back(i):
        here = pl.ds(pl.multiple_of(i * 128, 128), 128)
        v = pre[here, :]
        s = sigmoid(v)
        pre_grad[here, :] = (dot(out_grad[here, :], down_t[...]) * (s * (1.0 + v * (1.0 - s)))).astype(BF16)

    loop(4, atm_back)
    for i in range(4):
        late[256 * i : 256 * (i + 1), :] = dot(normed_t[...], pre_grad[:, 128 * i : 128 * (i + 1)]).astype(BF16)
    send_late(0)

    gagain[...] = jnp.zeros_like(gagain)
    gtaps[...] = jnp.zeros_like(gtaps)

    def atm_norm_back(i):
        here = pl.ds(pl.multiple_of(i * 128, 128), 128)
        ng = dot(pre_grad[here, :], up_t[...])
        u = unit[here, :]
        gagain[...] += jnp.sum(ng * u, axis=0, keepdims=True)
        gg = ng * again[...]
        sgrad[here, :] = inv_rms[here, 0:1] * (gg - u * jnp.mean(gg * u, axis=-1, keepdims=True))

    loop(4, atm_norm_back)
    early_2()

    def taps_row(y):
        sg = sgrad[pl.ds(pl.multiple_of(y * breadth, breadth), breadth), :]
        for a in range(3):
            for b in range(3):
                gtaps[3 * a + b : 3 * a + b + 1, :] += jnp.sum(
                    sg * win[y + a, 7 + b : 7 + b + breadth, :], axis=0, keepdims=True
                )

    loop(height, taps_row)

    small[...] = jnp.zeros_like(small)
    small[0:9, :] = gtaps[0:9, 0:128]
    small[9:18, :] = gtaps[0:9, 128:256]
    small[18:19, :] = gagain[:, 0:128]
    small[19:20, :] = gagain[:, 128:256]
    small[20:21, :] = gogain[...]

    def small_phase(i, value, buf, at, peers):
        buf[at] = value
        for to in peers:
            remote(buf.at[at], buf.at[at], small_ssem.at[i], small_rsem.at[i], to).start()

    def small_wait(i, buf):
        rest = buf.shape[0] - 1
        both_ends(buf.at[pl.ds(0, rest)], small_ssem.at[i], small_rsem.at[i]).wait_recv()
        total = buf[0]
        for n in range(rest):
            total = total + buf[n + 1]
        return total

    small_phase(0, small[...], small_core, c, [partner])
    early_3()
    small_phase(1, small_wait(0, small_core), small_x, x, x_peers)

    mine = span(rank_of(tx, ty), PIECE)
    pieces[c] = late[mine, :]
    both_ends(pieces.at[pl.ds(1, DEVICES - 1)], late_ssem, late_rsem).wait_recv()

    def add(i, total):
        return total + jnp.sum(pieces[pl.ds(i * 8, 8)].astype(F32), axis=0)

    late_sum[mine, :] = lax.fori_loop(0, DEVICES // 8, add, jnp.zeros((PIECE, 128), F32)).astype(BF16)

    def send_sum(g):
        for j, to in enumerate(step_devices(me, g, 1)):
            copy = remote(late_sum.at[mine], late_sum.at[mine], sum_ssem, sum_rsem, to)
            when(g > 0 if j == 0 else None, copy.start)

    loop(GROUPS // 2, send_sum)
    early_4()
    small_phase(2, small_wait(1, small_x), small_y, y, y_peers)
    loop(GROUPS // 2, lambda g: send_sum(g + GROUPS // 2))

    def place_blocks(i):
        for j in range(8):
            onew[i * 8 + j] = onew_arr[inv_s[0, i * 8 + j] & 255]

    loop(blocks // 8, place_blocks)
    store = pltpu.make_async_copy(onew, onew_hbm, misc_sem.at[1])
    store.start()
    early_5()
    small_phase(3, small_wait(2, small_y), small_z, z, z_peers)
    early_6()
    small[...] = small_wait(3, small_z)
    results = [
        pltpu.make_async_copy(early_sum, early_hbm, misc_sem.at[0]),
        pltpu.make_async_copy(small, small_hbm, misc_sem.at[2]),
        pltpu.make_async_copy(late_sum, late_hbm, misc_sem.at[3]),
    ]
    results[0].start()
    results[1].start()
    others = pl.ds(0, LATE - PIECE)
    both_ends(late_sum.at[others], sum_ssem, sum_rsem).wait_recv()
    results[2].start()
    both_ends(late.at[others], late_ssem, late_rsem).wait_send()
    both_ends(late.at[others], sum_ssem, sum_rsem).wait_send()
    for i, rows in ((0, 1), (1, 6), (2, 24), (3, 96)):
        both_ends(owners.at[pl.ds(0, rows)], own_ssem.at[i], own_rsem.at[i]).wait_send()
    for i, rows in enumerate((HALF, 3 * QUARTER, 3 * QUARTER, 3 * QUARTER, 3 * QUARTER, HALF)):
        sent = early_x if 0 < i < 4 else early
        both_ends(sent.at[pl.ds(0, rows)], early_ssem.at[i], early_rsem.at[i]).wait_send()
    for i, n in enumerate((1, 3, 3, 3)):
        both_ends(small_z.at[pl.ds(0, n)], small_ssem.at[i], small_rsem.at[i]).wait_send()

    both_ends(flux_out.at[pl.ds(ROWS, (DEVICES - 1) * ROWS)], flux_ssem, flux_rsem.at[0]).wait_send()
    both_ends(back_out.at[pl.ds(ROWS, (DEVICES - 1) * ROWS)], back_ssem, back_rsem.at[0]).wait_send()
    store.wait()
    for result in results:
        result.wait()


def finish(anew_in, onew_in, late_in, early_in, small_in, *refs):
    outs, (anew, onew, late, early, small), (gtaps, gagain, gup, gdown, gcouple, gogain, goup, godown), sem, osem = (
        refs[:10], refs[10:15], refs[15:23], refs[23], refs[24]
    )
    o_anew, o_onew, *o_grads = outs
    n = onew.shape[0] // 4
    parts = [pl.ds(i * n, n) for i in range(4)]
    loads = [
        pltpu.make_async_copy(src, dst, sem.at[i])
        for i, (src, dst) in enumerate(
            [(late_in, late), (early_in, early), (small_in, small), (anew_in, anew)]
            + [(onew_in.at[p], onew.at[p]) for p in parts]
        )
    ]
    for load in loads:
        load.start()
    stores = []

    def put(src, dst):
        stores.append(pltpu.make_async_copy(src, dst, osem.at[len(stores)]))
        stores[-1].start()

    loads[0].wait()
    for i in range(4):
        gup[:, 128 * i : 128 * (i + 1)] = late[256 * i : 256 * (i + 1), :].astype(F32)
    put(gup, o_grads[2])
    for i in range(2):
        gdown[:, 128 * i : 128 * (i + 1)] = late[1024 + 512 * i : 1024 + 512 * (i + 1), :].astype(F32)
    put(gdown, o_grads[3])
    for load in loads[1:4]:
        load.wait()
    put(anew, o_anew)
    for i in range(2):
        goup[:, 128 * i : 128 * (i + 1)] = early[128 * i : 128 * (i + 1), :].astype(F32)
    godown[...] = early[256:512, :].astype(F32)
    gcouple[...] = early[512:768, :].astype(F32)
    for a in range(3):
        for i in range(2):
            gtaps[a, :, 128 * i : 128 * (i + 1)] = small[9 * i + 3 * a : 9 * i + 3 * a + 3, :]
    gagain[:, 0:128] = small[18:19, :]
    gagain[:, 128:256] = small[19:20, :]
    gogain[...] = small[20:21, :]
    for i in (0, 1, 4, 5, 6, 7):
        put((gtaps, gagain, gup, gdown, gcouple, gogain, goup, godown)[i], o_grads[i])
    for load, p in zip(loads[4:], parts):
        load.wait()
        put(onew.at[p], o_onew.at[p])
    for store in stores:
        store.wait()


def body(
    atm_state, kernel_taps, atm_gain, atm_up, atm_down, couple_weight, ocean_gain, ocean_up, ocean_down,
    ocean_state, land_mask, margin_cell, margin_area, owner_slot, atm_cotangent, ocean_cotangent,
):
    height, breadth, channels = atm_state.shape
    blocks = ocean_state.shape[0]
    n_rows = blocks * 32
    n_cells = height * breadth
    vmem, any_ = pl.BlockSpec(memory_space=pltpu.VMEM), pl.BlockSpec(memory_space=pl.ANY)
    block = lambda: pltpu.VMEM((blocks, 32, 128), BF16)
    flat = lambda: pltpu.VMEM((n_rows, 128), BF16)
    scratch = [
        block(), block(),
        pltpu.VMEM((blocks, 32), F32),
        pltpu.VMEM((4, blocks // 4, 128), I32),
        pltpu.VMEM((4, blocks // 4, 128), F32),
        pltpu.VMEM((n_cells, n_rows), BF16),
        flat(), flat(), flat(), flat(),
        block(), block(),
        pltpu.VMEM((DEVICES, blocks), I32),
        pltpu.VMEM((DEVICES, 128), I32),
        pltpu.SMEM((DEVICES, 128), I32),
        pltpu.VMEM((8, blocks), I32),
        pltpu.SMEM((8, blocks), I32),
        pltpu.VMEM((height + 2, breadth + 16, channels), F32),
        pltpu.VMEM((n_cells, 256), F32),
        pltpu.VMEM((n_cells, 128), F32),
        pltpu.VMEM((n_cells, 256), BF16),
        pltpu.VMEM((n_cells, 512), F32),
        pltpu.VMEM((n_cells, 512), BF16),
        pltpu.VMEM((n_cells, 128), BF16),
        pltpu.VMEM((128, n_cells), BF16),
        pltpu.VMEM((n_cells, 256), BF16),
        pltpu.VMEM((n_cells, 512), BF16),
        pltpu.VMEM((512, n_cells), BF16),
        pltpu.VMEM((256, n_cells), BF16),
        pltpu.VMEM((256, n_cells), BF16),
        pltpu.VMEM((n_cells, 256), F32),
        pltpu.VMEM((512, 256), BF16),
        pltpu.VMEM((256, 512), BF16),
        pltpu.VMEM((128, 256), BF16),
        pltpu.VMEM((256, 128), BF16),
        pltpu.VMEM((128, 256), BF16),
        pltpu.VMEM((16, 256), F32),
        pltpu.VMEM((1, 256), F32),
        pltpu.VMEM((1, 128), F32),
        pltpu.VMEM((128, 256), F32),
        pltpu.VMEM((128, 256), F32),
        pltpu.VMEM((32, 128), F32),
        pltpu.VMEM((LATE, 128), BF16),
        pltpu.VMEM((DEVICES, PIECE, 128), BF16),
        pltpu.VMEM((LATE, 128), BF16),
        pltpu.VMEM((EARLY, 128), BF16),
        pltpu.VMEM((HALF, 128), BF16),
        pltpu.VMEM((HALF, 128), F32),
        pltpu.VMEM((HALF, 128), F32),
        pltpu.VMEM((HALF, 128), F32),
        pltpu.VMEM((HALF, 128), F32),
        pltpu.VMEM((EARLY, 128), BF16),
        pltpu.VMEM((2, 32, 128), F32),
        pltpu.VMEM((4, 32, 128), F32),
        pltpu.VMEM((4, 32, 128), F32),
        pltpu.VMEM((4, 32, 128), F32),
        pltpu.VMEM((16, channels), BF16),
        pltpu.VMEM((16, channels), BF16),
        pltpu.VMEM((breadth, channels), BF16),
        pltpu.VMEM((breadth, channels), BF16),
        pltpu.VMEM((6, 16, channels), BF16),
        pltpu.SemaphoreType.DMA((2,)),
        pltpu.SemaphoreType.DMA((8,)),
        pltpu.SemaphoreType.DMA((8,)),
        pltpu.SemaphoreType.DMA((4,)),
        pltpu.SemaphoreType.DMA((4,)),
        pltpu.SemaphoreType.DMA,
        pltpu.SemaphoreType.DMA((GROUPS,)),
        pltpu.SemaphoreType.DMA,
        pltpu.SemaphoreType.DMA((GROUPS,)),
        pltpu.SemaphoreType.DMA((5,)),
        pltpu.SemaphoreType.REGULAR((3,)),
        pltpu.SemaphoreType.DMA,
        pltpu.SemaphoreType.DMA,
        pltpu.SemaphoreType.DMA,
        pltpu.SemaphoreType.DMA,
        pltpu.SemaphoreType.DMA((6,)),
        pltpu.SemaphoreType.DMA((6,)),
        pltpu.SemaphoreType.DMA((4,)),
        pltpu.SemaphoreType.DMA((4,)),
    ]
    anew, onew, late, early, small = pl.pallas_call(
        kernel,
        out_shape=[
            jax.ShapeDtypeStruct((height, breadth, channels), BF16),
            jax.ShapeDtypeStruct((blocks, 32, 128), BF16),
            jax.ShapeDtypeStruct((LATE, 128), BF16),
            jax.ShapeDtypeStruct((EARLY, 128), BF16),
            jax.ShapeDtypeStruct((32, 128), F32),
        ],
        in_specs=[vmem] * 14 + [any_] * 2,
        out_specs=[vmem, any_, any_, any_, any_],
        scratch_shapes=scratch,
        compiler_params=pltpu.CompilerParams(
            collective_id=0, has_side_effects=True, vmem_limit_bytes=56 * 1024 * 1024
        ),
    )(
        atm_state, kernel_taps, atm_gain.reshape(1, -1), atm_up, atm_down, couple_weight,
        ocean_gain.reshape(1, -1), ocean_up, ocean_down, land_mask.T, margin_cell.transpose(1, 2, 0),
        margin_area.transpose(1, 2, 0), owner_slot.reshape(1, -1), atm_cotangent, ocean_state, ocean_cotangent,
    )
    anew, onew, gtaps, gagain, gup, gdown, gcouple, gogain, goup, godown = pl.pallas_call(
        finish,
        out_shape=[
            jax.ShapeDtypeStruct((height, breadth, channels), BF16),
            jax.ShapeDtypeStruct((blocks, 32, 128), BF16),
            jax.ShapeDtypeStruct((3, 3, 256), F32),
            jax.ShapeDtypeStruct((1, 256), F32),
            jax.ShapeDtypeStruct((256, 512), F32),
            jax.ShapeDtypeStruct((512, 256), F32),
            jax.ShapeDtypeStruct((256, 128), F32),
            jax.ShapeDtypeStruct((1, 128), F32),
            jax.ShapeDtypeStruct((128, 256), F32),
            jax.ShapeDtypeStruct((256, 128), F32),
        ],
        in_specs=[any_] * 5,
        out_specs=[any_] * 10,
        scratch_shapes=[
            pltpu.VMEM((height, breadth, channels), BF16), block(), pltpu.VMEM((LATE, 128), BF16),
            pltpu.VMEM((EARLY, 128), BF16), pltpu.VMEM((32, 128), F32),
            pltpu.VMEM((3, 3, 256), F32), pltpu.VMEM((1, 256), F32), pltpu.VMEM((256, 512), F32),
            pltpu.VMEM((512, 256), F32), pltpu.VMEM((256, 128), F32), pltpu.VMEM((1, 128), F32),
            pltpu.VMEM((128, 256), F32), pltpu.VMEM((256, 128), F32),
            pltpu.SemaphoreType.DMA((8,)), pltpu.SemaphoreType.DMA((13,)),
        ],
        compiler_params=pltpu.CompilerParams(vmem_limit_bytes=60 * 1024 * 1024),
    )(anew, onew, late, early, small)
    return (
        anew, onew, gtaps, gagain.reshape(-1), gup, gdown, gcouple, gogain.reshape(-1), goup, godown,
    )


def solution(mesh):
    both = ("tx", "ty")
    return jax.shard_map(
        body,
        mesh=mesh,
        in_specs=(P("ty", "tx", None),) + (P(),) * 8 + (
            P(both, None, None), P(both, None), P(both, None, None), P(both, None, None), P(both),
            P("ty", "tx", None), P(both, None, None),
        ),
        out_specs=(P("ty", "tx", None), P(both, None, None)) + (P(),) * 8,
        check_vma=False,
    )
```

```python
import functools

import jax
import jax.numpy as jnp
from jax import lax
from jax.experimental import pallas as pl
from jax.experimental.pallas import tpu as pltpu
from jax.sharding import PartitionSpec as P

EPS = 1e-06
MESH = pl.DeviceIdType.MESH
F32, BF16, I32 = jnp.float32, jnp.bfloat16, jnp.int32
DEVICES = 128
ROWS = 64
GROUP = 8
GROUPS = DEVICES // GROUP
AHEAD = 9
PIECE = 16
LATE = DEVICES * PIECE
EARLY = 768
HALF, QUARTER = EARLY // 2, EARLY // 8


def digits(tx, ty):
    return (tx // 4) * 2 + ty // 8, (ty // 2) % 4, tx % 4, ty % 2


def rem(a, n):
    return lax.rem(a, jnp.int32(n))


def div(a, n):
    return lax.div(a, jnp.int32(n))


def device(x, y, z, c):
    return (div(x, 2) * 4 + z, rem(x, 2) * 8 + y * 2 + c)


def group_devices(me, sign, low, turn, cores):
    found = []
    for j in range(GROUP):
        dx, two = j % 4, j // 4 * 2
        x = rem(me[0] + 4 + sign * dx, 4)
        y = rem(me[1] + 8 + sign * (turn + dx), 4)
        z = rem(me[2] + 8 + sign * (low + two + dx), 4)
        found.append(device(x, y, z, cores))
    return found


def step_devices(me, g, sign):
    return group_devices(me, sign, rem(div(g, 2), 2), div(g, 4), rem(me[3] + g, 2))


def step_codes(g):
    low, turn, dc = rem(div(g, 2), 2), div(g, 4), rem(g, 2)
    return [
        ((rem(low + j // 4 * 2 + j % 4, 4) * 4 + rem(turn + j % 4, 4)) * 4 + j % 4) * 2 + dc for j in range(GROUP)
    ]


def step_of(dx, dy, dz, dc):
    t, turn = (dz - dx) & 3, (dy - dx) & 3
    return (dc + 2 * (t & 1) + 4 * turn) * GROUP + dx + 4 * (t >> 1)


def rank_of(tx, ty):
    return rem(ty, 2) * (DEVICES // 2) + tx * 8 + div(ty, 2)


def sigmoid(v):
    return 0.5 * jnp.tanh(0.5 * v) + 0.5


def dot(a, b):
    return jnp.dot(a, b, preferred_element_type=F32)


def dot_t(a, b):
    return lax.dot_general(a, b, (((1,), (1,)), ((), ())), preferred_element_type=F32)


def t_dot(a, b):
    return lax.dot_general(a, b, (((0,), (0,)), ((), ())), preferred_element_type=F32)


def loop(n, f):
    lax.fori_loop(0, n, lambda i, c: (f(i), c)[1], 0)


def kernel(
    atm, taps, again, up, down, couple, ogain, oup, odown, mask, margin_cell, margin_area, owner, acot, ostate_hbm, ocot_hbm,
    anew, onew_hbm, late_hbm, early_hbm, small_hbm,
    ostate, ocot, wet, cells, shares, spread, flux_out, flux_in, back_out, back_in, onew, onew_arr, owners, slots_v, slots_s, inv_v, inv_s,
    win, unit, inv_rms, normed, pre, act, gather, coupled_t, out_grad, pre_grad, act_t, normed_t, anew_t, sgrad, up_t, down_t, couple_t, oup_t, odown_t,
    gtaps, gagain, gogain, goup, godown_t, small, late, pieces, late_sum,
    early, early_core, early_mine, early_x, early_y, early_z, early_sum, small_core, small_x, small_y, small_z,
    edge_w, edge_e, halo_n, halo_s, halo_c,
    load_sem, halo_ssem, halo_rsem, own_ssem, own_rsem, flux_ssem, flux_rsem, back_ssem, back_rsem, misc_sem,
    met, late_ssem, late_rsem, sum_ssem, sum_rsem, early_ssem, early_rsem, small_ssem, small_rsem,
):
    tx, ty = lax.axis_index("tx"), lax.axis_index("ty")
    me = digits(tx, ty)
    height, breadth = atm.shape[0], atm.shape[1]
    n_cells = height * breadth

    barrier = pltpu.get_barrier_semaphore()
    loads = [
        pltpu.make_async_copy(ostate_hbm, ostate, load_sem.at[0]),
        pltpu.make_async_copy(ocot_hbm, ocot, load_sem.at[1]),
    ]
    for load in loads:
        load.start()

    xs = [rem(me[0] + i, 4) for i in range(4)]
    ys = [rem(me[1] + i, 4) for i in range(4)]
    zs = [rem(me[2] + i, 4) for i in range(4)]
    cs = [me[3], 1 - me[3]]
    partner = device(xs[0], ys[0], zs[0], cs[1])
    x_peers = [device(xs[i], ys[0], zs[0], cs[0]) for i in (1, 3, 2)]
    y_peers = [device(xs[0], ys[i], zs[0], cs[0]) for i in (1, 3, 2)]
    z_peers = [device(xs[0], ys[0], zs[i], cs[0]) for i in (1, 3, 2)]

    te, tw, ts, tn = rem(tx + 1, 8), rem(tx + 7, 8), rem(ty + 1, 16), rem(ty + 15, 16)
    around = [(tx, tn), (tx, ts)] + [(side, row) for side in (te, tw) for row in (tn, ty, ts)]
    greeted = [partner] + x_peers + y_peers + z_peers + around
    for to in greeted:
        pl.semaphore_signal(barrier, inc=1, device_id=to, device_id_type=MESH)

    def meet(i, peers):
        for to in peers:
            pl.semaphore_signal(met.at[i], inc=1, device_id=to, device_id_type=MESH)

    def remote(src, dst, ssem, rsem, to):
        return pltpu.make_async_remote_copy(src, dst, ssem, rsem, device_id=to, device_id_type=MESH)

    def both_ends(ref, ssem, rsem):
        return remote(ref, ref, ssem, rsem, partner)

    edge_w[...] = jnp.zeros_like(edge_w)
    edge_e[...] = jnp.zeros_like(edge_e)

    def own_rows(y):
        win[y + 1, 8 : 8 + breadth, :] = atm[y].astype(F32)

    loop(height, own_rows)
    west = jnp.concatenate([win[y + 1, 8:9, :] for y in range(height)], axis=0)
    east = jnp.concatenate([win[y + 1, 7 + breadth : 8 + breadth, :] for y in range(height)], axis=0)
    nothing = jnp.zeros_like(west)
    edge_w[...] = jnp.concatenate([west, nothing], axis=0).astype(BF16)
    edge_e[...] = jnp.concatenate([east, nothing], axis=0).astype(BF16)

    pl.semaphore_wait(barrier, len(greeted))
    meet(0, y_peers)

    north, south = ty > 0, ty < 15

    def halo(i, src, dst, dx, dy):
        return pltpu.make_async_remote_copy(
            src, dst, halo_ssem.at[i], halo_rsem.at[i], device_id=(dx, dy), device_id_type=MESH
        )

    copies = [
        (south, halo(0, atm.at[height - 1], halo_n, tx, ts)),
        (north, halo(1, atm.at[0], halo_s, tx, tn)),
        (None, halo(2, edge_e, halo_c.at[0], te, ty)),
        (None, halo(3, edge_w, halo_c.at[1], tw, ty)),
        (south, halo(4, edge_e, halo_c.at[2], te, ts)),
        (south, halo(5, edge_w, halo_c.at[3], tw, ts)),
        (north, halo(6, edge_e, halo_c.at[4], te, tn)),
        (north, halo(7, edge_w, halo_c.at[5], tw, tn)),
    ]

    def when(cond, f):
        if cond is None:
            f()
        else:
            pl.when(cond)(f)

    for cond, copy in copies:
        when(cond, copy.start)

    owners[0:1, :] = owner[...]

    def own_phase(i, rows, peers):
        for n, to in zip((1, 3, 2), peers):
            remote(
                owners.at[pl.ds(0, rows)], owners.at[pl.ds(n * rows, rows)], own_ssem.at[i], own_rsem.at[i], to
            ).start()

    def own_wait(i, rows, peers):
        both_ends(owners.at[pl.ds(rows, rows * peers)], own_ssem.at[i], own_rsem.at[i]).wait_recv()

    own_phase(0, 1, [partner])

    slot = owner[...]
    t_tx, t_ty = slot >> 12, (slot >> 8) & 15
    theirs = ((t_tx >> 2) * 2 + (t_ty >> 3), (t_ty >> 1) & 3, t_tx & 3, t_ty & 1)
    dx, dy, dz, dc = [(t - m + n) & (n - 1) for t, m, n in zip(theirs, me, (4, 4, 4, 2))]
    step = step_of(dx, dy, dz, dc)
    blocks = slot.shape[1]
    square = jnp.broadcast_to(step, (blocks, blocks))
    first = lax.broadcasted_iota(I32, square.shape, 0)
    second = lax.broadcasted_iota(I32, square.shape, 1)
    same = (square.astype(F32).T == square.astype(F32)) & (first < second)
    place = 2 * step + jnp.sum(same.astype(F32), axis=0, keepdims=True).astype(I32)

    area = margin_area[...]
    share = (area / jnp.sum(area, axis=0, keepdims=True)).reshape(128, blocks).astype(BF16)
    cell = margin_cell[...].reshape(128, blocks)
    high, low = (cell >> 4).astype(F32).astype(BF16), (cell & 15).astype(F32).astype(BF16)
    quads = lax.broadcasted_iota(I32, (blocks // 4, blocks), 0)
    lane_block = lax.broadcasted_iota(I32, (blocks // 4, 128), 1) // 32
    got_share = [jnp.zeros((blocks // 4, 128), F32)] * 4
    got_cell = [jnp.zeros((blocks // 4, 128), F32)] * 4
    for j in range(4):
        pick = (place == 4 * quads + j).astype(F32).astype(BF16)
        one_share = dot_t(pick, share)
        one_cell = 16.0 * dot_t(pick, high) + dot_t(pick, low)
        for k in range(4):
            turn = (32 * (j - k)) % 128
            here = lane_block == j
            got_share[k] = jnp.where(here, pltpu.roll(one_share, turn, 1) if turn else one_share, got_share[k])
            got_cell[k] = jnp.where(here, pltpu.roll(one_cell, turn, 1) if turn else one_cell, got_cell[k])
    for k in range(4):
        shares[k] = got_share[k]
        cells[k] = got_cell[k].astype(I32)

    pl.semaphore_wait(met.at[0], 3)
    meet(1, z_peers)
    own_wait(0, 1, 1)
    own_phase(1, 2, x_peers)
    def spread_columns(i):
        here = pl.ds(pl.multiple_of(i * 128, 128), 128)
        row = pl.ds(i, 1)
        rows = lax.broadcasted_iota(I32, (n_cells // 16, 16, 128), 0) * 16 + lax.broadcasted_iota(
            I32, (n_cells // 16, 16, 128), 1
        )
        rows = rows.astype(jnp.int16)
        total = None
        for k in range(4):
            cell_k = jnp.broadcast_to(cells[k, row, :], (16, 128)).astype(jnp.int16)
            share_k = jnp.broadcast_to(shares[k, row, :], (16, 128)).astype(BF16)
            part = jnp.where(rows == cell_k[None], share_k[None], jnp.zeros((), BF16))
            total = part if total is None else total + part
        spread[:, here] = total.reshape(n_cells, 128)

    couple_t[...] = couple[...].astype(F32).T.astype(BF16)
    pl.semaphore_wait(met.at[1], 3)
    meet(2, [partner])

    for cond, copy in copies:
        when(cond, copy.wait_send)
    receives = [north, south, None, None, north, north, south, south]
    for cond, (_, copy) in zip(receives, copies):
        when(cond, copy.wait_recv)

    @pl.when(north)
    def _():
        win[0, 8 : 8 + breadth, :] = halo_n[...].astype(F32)
        win[0, 7:8, :] = halo_c[2].astype(F32)[height - 1 : height]
        win[0, 8 + breadth : 9 + breadth, :] = halo_c[3].astype(F32)[height - 1 : height]

    @pl.when(jnp.logical_not(north))
    def _():
        win[0] = jnp.zeros(win.shape[1:], F32)

    @pl.when(south)
    def _():
        win[height + 1, 8 : 8 + breadth, :] = halo_s[...].astype(F32)
        win[height + 1, 7:8, :] = halo_c[4].astype(F32)[0:1]
        win[height + 1, 8 + breadth : 9 + breadth, :] = halo_c[5].astype(F32)[0:1]

    @pl.when(jnp.logical_not(south))
    def _():
        win[height + 1] = jnp.zeros(win.shape[1:], F32)

    west, east = halo_c[0].astype(F32), halo_c[1].astype(F32)
    for y in range(height):
        win[y + 1, 7:8, :] = west[y : y + 1]
        win[y + 1, 8 + breadth : 9 + breadth, :] = east[y : y + 1]

    def stencil_row(y):
        total = jnp.zeros((breadth, 256), F32)
        for a in range(3):
            for b in range(3):
                total = total + taps[a, b : b + 1, :] * win[y + a, 7 + b : 7 + b + breadth, :]
        inv = lax.rsqrt(jnp.mean(total * total, axis=-1, keepdims=True) + EPS)
        here = pl.ds(pl.multiple_of(y * breadth, breadth), breadth)
        u = total * inv
        unit[here, :] = u
        inv_rms[here, :] = jnp.broadcast_to(inv, (breadth, 128))
        normed[here, :] = (u * again[...]).astype(BF16)

    loop(height, stencil_row)

    def atm_mlp(i):
        here = pl.ds(pl.multiple_of(i * 128, 128), 128)
        v = dot(normed[here, :], up[...])
        pre[here, :] = v
        a = (v * sigmoid(v)).astype(BF16)
        act[here, :] = a
        old = atm[pl.ds(i * 2, 2)].reshape(128, 256).astype(F32)
        anew[pl.ds(i * 2, 2)] = (old + dot(a, down[...])).astype(BF16).reshape(2, breadth, 256)

    loop(4, atm_mlp)
    coupled_t[...] = dot_t(couple_t[...], anew[...].reshape(n_cells, 256)).astype(BF16)
    own_wait(1, 2, 3)
    own_phase(2, 8, y_peers)
    pl.semaphore_wait(met.at[2], 1)

    def send_group(g, sign, src, dst, ssem, rsem):
        for j, to in enumerate(step_devices(me, g, sign)):
            here = pl.ds(pl.multiple_of((g * GROUP + j) * ROWS, ROWS), ROWS)
            copy = remote(src.at[here], dst.at[here], ssem, rsem.at[g], to)
            when(g > 0 if j == 0 else None, copy.start)

    def flux_group(g):
        for j in range(GROUP // 2):
            spread_columns(g * (GROUP // 2) + j)
        here = pl.ds(pl.multiple_of(g * (GROUP * ROWS), GROUP * ROWS), GROUP * ROWS)
        flux_out[here, :] = dot(coupled_t[...], spread[:, here]).astype(BF16).T
        send_group(g, 1, flux_out, flux_in, flux_ssem, flux_rsem)

    loop(4, flux_group)
    own_wait(2, 8, 3)
    own_phase(3, 32, z_peers)
    loop(AHEAD - 4, lambda g: flux_group(g + 4))
    flux_in[0:ROWS, :] = flux_out[0:ROWS, :]

    wet[...] = mask[...].astype(F32).T
    for weight, turned in ((oup, oup_t), (odown, odown_t)):
        turned[...] = weight[...].astype(F32).T.astype(BF16)

    own_wait(3, 32, 3)
    owned = owners[...]
    lane = lax.broadcasted_iota(I32, owned.shape, 1)
    hit = (owned >> 8) == tx * 16 + ty
    lane_f = lane.astype(F32)
    local = (owned & (blocks - 1)).astype(F32)
    one = jnp.min(jnp.where(hit, lane_f, 1e4), axis=1, keepdims=True)
    two = jnp.max(jnp.where(hit, lane_f, -1.0), axis=1, keepdims=True)
    one = jnp.sum(jnp.where(lane_f == one, local, 0.0), axis=1, keepdims=True).astype(I32)
    two = jnp.sum(jnp.where(lane_f == two, local, 0.0), axis=1, keepdims=True).astype(I32)
    code = lax.broadcasted_iota(I32, owned.shape, 0)
    position = 2 * step_of((code >> 1) & 3, (code >> 3) & 3, code >> 5, code & 1)
    found = jnp.where(one == lane, position, 0) + jnp.where(two == lane, position + 1, 0)
    inv_v[...] = jnp.broadcast_to(
        jnp.max(found.astype(F32), axis=0, keepdims=True).astype(I32), inv_v.shape
    )
    slots_v[...] = jnp.where(lane[:, 0:128] == 0, one, two)
    to_scalar = [
        pltpu.make_async_copy(slots_v, slots_s, misc_sem.at[0]),
        pltpu.make_async_copy(inv_v, inv_s, misc_sem.at[4]),
    ]
    for copy in to_scalar:
        copy.start()
    for copy in to_scalar:
        copy.wait()
    for load in loads:
        load.wait()

    goup[...] = jnp.zeros_like(goup)
    godown_t[...] = jnp.zeros_like(godown_t)
    gogain[...] = jnp.zeros_like(gogain)

    def wait_group(g, buf, ssem, rsem):
        def first():
            both_ends(buf.at[pl.ds(ROWS, (GROUP - 1) * ROWS)], ssem, rsem.at[0]).wait_recv()

        def later():
            here = pl.ds(pl.multiple_of(g * (GROUP * ROWS), GROUP * ROWS), GROUP * ROWS)
            both_ends(buf.at[here], ssem, rsem.at[g]).wait_recv()

        pl.when(g == 0)(first)
        pl.when(g > 0)(later)

    def ocean_group(g):
        wait_group(g, flux_in, flux_ssem, flux_rsem)
        here = pl.ds(pl.multiple_of(g * (GROUP * ROWS), GROUP * ROWS), GROUP * ROWS)
        codes = step_codes(g)
        slot = [slots_s[codes[j // 2], j % 2] & 255 for j in range(2 * GROUP)]
        state = jnp.concatenate([ostate[s] for s in slot], axis=0).astype(F32)
        eye = lax.broadcasted_iota(I32, (32, 32), 0) == lax.broadcasted_iota(I32, (32, 32), 1)
        wets = jnp.concatenate([jnp.where(eye, wet[pl.ds(s, 1), :], 0.0) for s in slot], axis=0).astype(BF16)
        wets = dot(wets, jnp.ones((32, 128), BF16))
        wet_cot = jnp.concatenate([ocot[s] for s in slot], axis=0) * wets.astype(BF16)
        total = state + flux_in[here, :].astype(F32)
        inv = lax.rsqrt(jnp.mean(total * total, axis=-1, keepdims=True) + EPS)
        u = total * inv
        nrm = (u * ogain[...]).astype(BF16)
        v = dot(nrm, oup[...])
        s = sigmoid(v)
        a = (v * s).astype(BF16)
        onew_arr[pl.ds(g * (2 * GROUP), 2 * GROUP)] = (
            (state + wets * dot(a, odown[...])).astype(BF16).reshape(2 * GROUP, 32, 128)
        )
        godown_t[...] += t_dot(wet_cot, a)
        pg = (dot(wet_cot, odown_t[...]) * (s * (1.0 + v * (1.0 - s)))).astype(BF16)
        goup[...] += t_dot(nrm, pg)
        ng = dot(pg, oup_t[...])
        gogain[...] += jnp.sum(ng * u, axis=0, keepdims=True)
        gg = ng * ogain[...]
        tg = inv * (gg - u * jnp.mean(gg * u, axis=-1, keepdims=True))
        back_out[here, :] = tg.astype(BF16)

        send_group(g, -1, back_out, back_in, back_ssem, back_rsem)

    def both_groups(g):
        flux_group(g + AHEAD)
        ocean_group(g)

    loop(GROUPS - AHEAD, both_groups)
    loop(AHEAD, lambda g: ocean_group(g + GROUPS - AHEAD))
    back_in[0:ROWS, :] = back_out[0:ROWS, :]

    for i in range(2):
        early[128 * i : 128 * (i + 1), :] = goup[:, 128 * i : 128 * (i + 1)].astype(BF16)
        early[256 + 128 * i : 256 + 128 * (i + 1), :] = godown_t[:, 128 * i : 128 * (i + 1)].T.astype(BF16)

    for weight, turned in ((up, up_t), (down, down_t)):
        turned[...] = weight[...].astype(F32).T.astype(BF16)
    for i in range(4):
        here = slice(128 * i, 128 * (i + 1))
        act_t[:, here] = act[here, :].T
        normed_t[:, here] = normed[here, :].T
        anew_t[:, here] = anew[2 * i : 2 * i + 2].reshape(128, 256).T

    sgrad[:, 0:128] = jnp.zeros((n_cells, 128), F32)

    def back_group(g):
        wait_group(g, back_in, back_ssem, back_rsem)
        here = pl.ds(pl.multiple_of(g * (GROUP * ROWS), GROUP * ROWS), GROUP * ROWS)
        sgrad[:, 0:128] += dot(spread[:, here], back_in[here, :])

    loop(GROUPS, back_group)
    gathered = sgrad[:, 0:128].astype(BF16)
    gather[...] = gathered
    early[512:768, :] = dot(anew_t[...], gathered).astype(BF16)

    x, y, z, c = me

    def span(i, n):
        return pl.ds(pl.multiple_of(i * n, n), n)

    def early_copy(i, src, dst, to):
        remote(src, dst, early_ssem.at[i], early_rsem.at[i], to).start()

    def early_wait(i, ref):
        both_ends(ref, early_ssem.at[i], early_rsem.at[i]).wait_recv()

    def add_four(ref):
        rows = ref.shape[0] // 4
        total = ref[0:rows, :]
        for i in range(1, 4):
            total = total + ref[i * rows : (i + 1) * rows, :]
        return total

    def early_0():
        early_copy(0, early.at[span(1 - c, HALF)], early_core, partner)

    def early_1():
        early_wait(0, early_core)
        early_mine[...] = early[span(c, HALF), :].astype(F32) + early_core[...].astype(F32)
        early_x[span(x, QUARTER), :] = early_mine[span(x, QUARTER), :]
        for n, to in zip((1, 3, 2), x_peers):
            early_copy(1, early_mine.at[span(xs[n], QUARTER)], early_x.at[span(x, QUARTER)], to)

    def early_2():
        early_wait(1, early_x.at[pl.ds(0, 3 * QUARTER)])
        early_y[span(y, QUARTER), :] = add_four(early_x)
        for to in y_peers:
            early_copy(2, early_y.at[span(y, QUARTER)], early_y.at[span(y, QUARTER)], to)

    def early_3():
        early_wait(2, early_y.at[pl.ds(0, 3 * QUARTER)])
        early_z[span(z, QUARTER), :] = add_four(early_y)
        for to in z_peers:
            early_copy(3, early_z.at[span(z, QUARTER)], early_z.at[span(z, QUARTER)], to)

    def early_4():
        early_wait(3, early_z.at[pl.ds(0, 3 * QUARTER)])
        here = span(c * 4 + x, QUARTER)
        early_sum[here, :] = add_four(early_z).astype(BF16)
        for to in x_peers:
            early_copy(4, early_sum.at[here], early_sum.at[here], to)

    def early_5():
        early_wait(4, early_sum.at[pl.ds(0, 3 * QUARTER)])
        here = span(c, HALF)
        early_copy(5, early_sum.at[here], early_sum.at[here], partner)

    def early_6():
        early_wait(5, early_sum.at[pl.ds(0, HALF)])

    early_0()
    def send_late(low):
        def group(g):
            for j, to in enumerate(group_devices(me, 1, rem(g, 2), div(g, 2), low)):
                copy = remote(
                    late.at[span(rank_of(*to), PIECE)], pieces.at[(g * GROUP + j) * 2 + c], late_ssem, late_rsem, to
                )
                when(jnp.logical_or(g > 0, c != low) if j == 0 else None, copy.start)

        loop(GROUPS // 2, group)

    def atm_out_grad(i):
        here = pl.ds(pl.multiple_of(i * 128, 128), 128)
        cot = acot[pl.ds(i * 2, 2)].reshape(128, 256).astype(F32)
        out_grad[here, :] = (cot + dot(gather[here, :], couple_t[...])).astype(BF16)

    loop(4, atm_out_grad)
    for i in range(2):
        half = dot(act_t[...], out_grad[:, 128 * i : 128 * (i + 1)])
        late[1024 + 512 * i : 1024 + 512 * (i + 1), :] = half.astype(BF16)
    send_late(1)
    early_1()

    def atm_back(i):
        here = pl.ds(pl.multiple_of(i * 128, 128), 128)
        v = pre[here, :]
        s = sigmoid(v)
        pre_grad[here, :] = (dot(out_grad[here, :], down_t[...]) * (s * (1.0 + v * (1.0 - s)))).astype(BF16)

    loop(4, atm_back)
    for i in range(4):
        late[256 * i : 256 * (i + 1), :] = dot(normed_t[...], pre_grad[:, 128 * i : 128 * (i + 1)]).astype(BF16)
    send_late(0)

    gagain[...] = jnp.zeros_like(gagain)
    gtaps[...] = jnp.zeros_like(gtaps)

    def atm_norm_back(i):
        here = pl.ds(pl.multiple_of(i * 128, 128), 128)
        ng = dot(pre_grad[here, :], up_t[...])
        u = unit[here, :]
        gagain[...] += jnp.sum(ng * u, axis=0, keepdims=True)
        gg = ng * again[...]
        sgrad[here, :] = inv_rms[here, 0:1] * (gg - u * jnp.mean(gg * u, axis=-1, keepdims=True))

    loop(4, atm_norm_back)
    early_2()

    def taps_row(y):
        sg = sgrad[pl.ds(pl.multiple_of(y * breadth, breadth), breadth), :]
        for a in range(3):
            for b in range(3):
                gtaps[3 * a + b : 3 * a + b + 1, :] += jnp.sum(
                    sg * win[y + a, 7 + b : 7 + b + breadth, :], axis=0, keepdims=True
                )

    loop(height, taps_row)

    small[...] = jnp.zeros_like(small)
    small[0:9, :] = gtaps[0:9, 0:128]
    small[9:18, :] = gtaps[0:9, 128:256]
    small[18:19, :] = gagain[:, 0:128]
    small[19:20, :] = gagain[:, 128:256]
    small[20:21, :] = gogain[...]

    def small_phase(i, value, buf, at, peers):
        buf[at] = value
        for to in peers:
            remote(buf.at[at], buf.at[at], small_ssem.at[i], small_rsem.at[i], to).start()

    def small_wait(i, buf):
        rest = buf.shape[0] - 1
        both_ends(buf.at[pl.ds(0, rest)], small_ssem.at[i], small_rsem.at[i]).wait_recv()
        total = buf[0]
        for n in range(rest):
            total = total + buf[n + 1]
        return total

    small_phase(0, small[...], small_core, c, [partner])
    small_phase(1, small_wait(0, small_core), small_x, x, x_peers)
    early_3()

    mine = span(rank_of(tx, ty), PIECE)
    pieces[c] = late[mine, :]
    both_ends(pieces.at[pl.ds(1, DEVICES - 1)], late_ssem, late_rsem).wait_recv()

    def add(i, total):
        return total + jnp.sum(pieces[pl.ds(i * 8, 8)].astype(F32), axis=0)

    late_sum[mine, :] = lax.fori_loop(0, DEVICES // 8, add, jnp.zeros((PIECE, 128), F32)).astype(BF16)

    def send_sum(g):
        for j, to in enumerate(step_devices(me, g, 1)):
            copy = remote(late_sum.at[mine], late_sum.at[mine], sum_ssem, sum_rsem, to)
            when(g > 0 if j == 0 else None, copy.start)

    loop(4, send_sum)
    small_phase(2, small_wait(1, small_x), small_y, y, y_peers)
    early_4()
    loop(6, lambda g: send_sum(g + 4))
    small_phase(3, small_wait(2, small_y), small_z, z, z_peers)
    early_5()
    loop(6, lambda g: send_sum(g + 10))

    def place_blocks(i):
        for j in range(8):
            onew[i * 8 + j] = onew_arr[inv_s[0, i * 8 + j] & 255]

    loop(blocks // 8, place_blocks)
    store = pltpu.make_async_copy(onew, onew_hbm, misc_sem.at[1])
    store.start()
    early_6()
    small[...] = small_wait(3, small_z)
    results = [
        pltpu.make_async_copy(early_sum, early_hbm, misc_sem.at[0]),
        pltpu.make_async_copy(small, small_hbm, misc_sem.at[2]),
        pltpu.make_async_copy(late_sum, late_hbm, misc_sem.at[3]),
    ]
    results[0].start()
    results[1].start()
    others = pl.ds(0, LATE - PIECE)
    both_ends(late_sum.at[others], sum_ssem, sum_rsem).wait_recv()
    results[2].start()
    both_ends(late.at[others], late_ssem, late_rsem).wait_send()
    both_ends(late.at[others], sum_ssem, sum_rsem).wait_send()
    for i, rows in ((0, 1), (1, 6), (2, 24), (3, 96)):
        both_ends(owners.at[pl.ds(0, rows)], own_ssem.at[i], own_rsem.at[i]).wait_send()
    for i, rows in enumerate((HALF, 3 * QUARTER, 3 * QUARTER, 3 * QUARTER, 3 * QUARTER, HALF)):
        sent = early_x if 0 < i < 4 else early
        both_ends(sent.at[pl.ds(0, rows)], early_ssem.at[i], early_rsem.at[i]).wait_send()
    for i, n in enumerate((1, 3, 3, 3)):
        both_ends(small_z.at[pl.ds(0, n)], small_ssem.at[i], small_rsem.at[i]).wait_send()

    both_ends(flux_out.at[pl.ds(ROWS, (DEVICES - 1) * ROWS)], flux_ssem, flux_rsem.at[0]).wait_send()
    both_ends(back_out.at[pl.ds(ROWS, (DEVICES - 1) * ROWS)], back_ssem, back_rsem.at[0]).wait_send()
    store.wait()
    for result in results:
        result.wait()


def finish(anew_in, onew_in, late_in, early_in, small_in, *refs):
    outs, (anew, onew, late, early, small), (gtaps, gagain, gup, gdown, gcouple, gogain, goup, godown), sem, osem = (
        refs[:10], refs[10:15], refs[15:23], refs[23], refs[24]
    )
    o_anew, o_onew, *o_grads = outs
    n = onew.shape[0] // 4
    parts = [pl.ds(i * n, n) for i in range(4)]
    loads = [
        pltpu.make_async_copy(src, dst, sem.at[i])
        for i, (src, dst) in enumerate(
            [(late_in, late), (early_in, early), (small_in, small), (anew_in, anew)]
            + [(onew_in.at[p], onew.at[p]) for p in parts]
        )
    ]
    for load in loads:
        load.start()
    stores = []

    def put(src, dst):
        stores.append(pltpu.make_async_copy(src, dst, osem.at[len(stores)]))
        stores[-1].start()

    loads[0].wait()
    for i in range(4):
        gup[:, 128 * i : 128 * (i + 1)] = late[256 * i : 256 * (i + 1), :].astype(F32)
    put(gup, o_grads[2])
    for i in range(2):
        gdown[:, 128 * i : 128 * (i + 1)] = late[1024 + 512 * i : 1024 + 512 * (i + 1), :].astype(F32)
    put(gdown, o_grads[3])
    for load in loads[1:4]:
        load.wait()
    put(anew, o_anew)
    for i in range(2):
        goup[:, 128 * i : 128 * (i + 1)] = early[128 * i : 128 * (i + 1), :].astype(F32)
    godown[...] = early[256:512, :].astype(F32)
    gcouple[...] = early[512:768, :].astype(F32)
    for a in range(3):
        for i in range(2):
            gtaps[a, :, 128 * i : 128 * (i + 1)] = small[9 * i + 3 * a : 9 * i + 3 * a + 3, :]
    gagain[:, 0:128] = small[18:19, :]
    gagain[:, 128:256] = small[19:20, :]
    gogain[...] = small[20:21, :]
    for i in (0, 1, 4, 5, 6, 7):
        put((gtaps, gagain, gup, gdown, gcouple, gogain, goup, godown)[i], o_grads[i])
    for load, p in zip(loads[4:], parts):
        load.wait()
        put(onew.at[p], o_onew.at[p])
    for store in stores:
        store.wait()


def body(
    atm_state, kernel_taps, atm_gain, atm_up, atm_down, couple_weight, ocean_gain, ocean_up, ocean_down,
    ocean_state, land_mask, margin_cell, margin_area, owner_slot, atm_cotangent, ocean_cotangent,
):
    height, breadth, channels = atm_state.shape
    blocks = ocean_state.shape[0]
    n_rows = blocks * 32
    n_cells = height * breadth
    vmem, any_ = pl.BlockSpec(memory_space=pltpu.VMEM), pl.BlockSpec(memory_space=pl.ANY)
    block = lambda: pltpu.VMEM((blocks, 32, 128), BF16)
    flat = lambda: pltpu.VMEM((n_rows, 128), BF16)
    scratch = [
        block(), block(),
        pltpu.VMEM((blocks, 32), F32),
        pltpu.VMEM((4, blocks // 4, 128), I32),
        pltpu.VMEM((4, blocks // 4, 128), F32),
        pltpu.VMEM((n_cells, n_rows), BF16),
        flat(), flat(), flat(), flat(),
        block(), block(),
        pltpu.VMEM((DEVICES, blocks), I32),
        pltpu.VMEM((DEVICES, 128), I32),
        pltpu.SMEM((DEVICES, 128), I32),
        pltpu.VMEM((8, blocks), I32),
        pltpu.SMEM((8, blocks), I32),
        pltpu.VMEM((height + 2, breadth + 16, channels), F32),
        pltpu.VMEM((n_cells, 256), F32),
        pltpu.VMEM((n_cells, 128), F32),
        pltpu.VMEM((n_cells, 256), BF16),
        pltpu.VMEM((n_cells, 512), F32),
        pltpu.VMEM((n_cells, 512), BF16),
        pltpu.VMEM((n_cells, 128), BF16),
        pltpu.VMEM((128, n_cells), BF16),
        pltpu.VMEM((n_cells, 256), BF16),
        pltpu.VMEM((n_cells, 512), BF16),
        pltpu.VMEM((512, n_cells), BF16),
        pltpu.VMEM((256, n_cells), BF16),
        pltpu.VMEM((256, n_cells), BF16),
        pltpu.VMEM((n_cells, 256), F32),
        pltpu.VMEM((512, 256), BF16),
        pltpu.VMEM((256, 512), BF16),
        pltpu.VMEM((128, 256), BF16),
        pltpu.VMEM((256, 128), BF16),
        pltpu.VMEM((128, 256), BF16),
        pltpu.VMEM((16, 256), F32),
        pltpu.VMEM((1, 256), F32),
        pltpu.VMEM((1, 128), F32),
        pltpu.VMEM((128, 256), F32),
        pltpu.VMEM((128, 256), F32),
        pltpu.VMEM((32, 128), F32),
        pltpu.VMEM((LATE, 128), BF16),
        pltpu.VMEM((DEVICES, PIECE, 128), BF16),
        pltpu.VMEM((LATE, 128), BF16),
        pltpu.VMEM((EARLY, 128), BF16),
        pltpu.VMEM((HALF, 128), BF16),
        pltpu.VMEM((HALF, 128), F32),
        pltpu.VMEM((HALF, 128), F32),
        pltpu.VMEM((HALF, 128), F32),
        pltpu.VMEM((HALF, 128), F32),
        pltpu.VMEM((EARLY, 128), BF16),
        pltpu.VMEM((2, 32, 128), F32),
        pltpu.VMEM((4, 32, 128), F32),
        pltpu.VMEM((4, 32, 128), F32),
        pltpu.VMEM((4, 32, 128), F32),
        pltpu.VMEM((16, channels), BF16),
        pltpu.VMEM((16, channels), BF16),
        pltpu.VMEM((breadth, channels), BF16),
        pltpu.VMEM((breadth, channels), BF16),
        pltpu.VMEM((6, 16, channels), BF16),
        pltpu.SemaphoreType.DMA((2,)),
        pltpu.SemaphoreType.DMA((8,)),
        pltpu.SemaphoreType.DMA((8,)),
        pltpu.SemaphoreType.DMA((4,)),
        pltpu.SemaphoreType.DMA((4,)),
        pltpu.SemaphoreType.DMA,
        pltpu.SemaphoreType.DMA((GROUPS,)),
        pltpu.SemaphoreType.DMA,
        pltpu.SemaphoreType.DMA((GROUPS,)),
        pltpu.SemaphoreType.DMA((5,)),
        pltpu.SemaphoreType.REGULAR((3,)),
        pltpu.SemaphoreType.DMA,
        pltpu.SemaphoreType.DMA,
        pltpu.SemaphoreType.DMA,
        pltpu.SemaphoreType.DMA,
        pltpu.SemaphoreType.DMA((6,)),
        pltpu.SemaphoreType.DMA((6,)),
        pltpu.SemaphoreType.DMA((4,)),
        pltpu.SemaphoreType.DMA((4,)),
    ]
    anew, onew, late, early, small = pl.pallas_call(
        kernel,
        out_shape=[
            jax.ShapeDtypeStruct((height, breadth, channels), BF16),
            jax.ShapeDtypeStruct((blocks, 32, 128), BF16),
            jax.ShapeDtypeStruct((LATE, 128), BF16),
            jax.ShapeDtypeStruct((EARLY, 128), BF16),
            jax.ShapeDtypeStruct((32, 128), F32),
        ],
        in_specs=[vmem] * 14 + [any_] * 2,
        out_specs=[vmem, any_, any_, any_, any_],
        scratch_shapes=scratch,
        compiler_params=pltpu.CompilerParams(
            collective_id=0, has_side_effects=True, vmem_limit_bytes=56 * 1024 * 1024
        ),
    )(
        atm_state, kernel_taps, atm_gain.reshape(1, -1), atm_up, atm_down, couple_weight,
        ocean_gain.reshape(1, -1), ocean_up, ocean_down, land_mask.T, margin_cell.transpose(1, 2, 0),
        margin_area.transpose(1, 2, 0), owner_slot.reshape(1, -1), atm_cotangent, ocean_state, ocean_cotangent,
    )
    anew, onew, gtaps, gagain, gup, gdown, gcouple, gogain, goup, godown = pl.pallas_call(
        finish,
        out_shape=[
            jax.ShapeDtypeStruct((height, breadth, channels), BF16),
            jax.ShapeDtypeStruct((blocks, 32, 128), BF16),
            jax.ShapeDtypeStruct((3, 3, 256), F32),
            jax.ShapeDtypeStruct((1, 256), F32),
            jax.ShapeDtypeStruct((256, 512), F32),
            jax.ShapeDtypeStruct((512, 256), F32),
            jax.ShapeDtypeStruct((256, 128), F32),
            jax.ShapeDtypeStruct((1, 128), F32),
            jax.ShapeDtypeStruct((128, 256), F32),
            jax.ShapeDtypeStruct((256, 128), F32),
        ],
        in_specs=[any_] * 5,
        out_specs=[any_] * 10,
        scratch_shapes=[
            pltpu.VMEM((height, breadth, channels), BF16), block(), pltpu.VMEM((LATE, 128), BF16),
            pltpu.VMEM((EARLY, 128), BF16), pltpu.VMEM((32, 128), F32),
            pltpu.VMEM((3, 3, 256), F32), pltpu.VMEM((1, 256), F32), pltpu.VMEM((256, 512), F32),
            pltpu.VMEM((512, 256), F32), pltpu.VMEM((256, 128), F32), pltpu.VMEM((1, 128), F32),
            pltpu.VMEM((128, 256), F32), pltpu.VMEM((256, 128), F32),
            pltpu.SemaphoreType.DMA((8,)), pltpu.SemaphoreType.DMA((13,)),
        ],
        compiler_params=pltpu.CompilerParams(vmem_limit_bytes=60 * 1024 * 1024),
    )(anew, onew, late, early, small)
    return (
        anew, onew, gtaps, gagain.reshape(-1), gup, gdown, gcouple, gogain.reshape(-1), goup, godown,
    )


def solution(mesh):
    both = ("tx", "ty")
    return jax.shard_map(
        body,
        mesh=mesh,
        in_specs=(P("ty", "tx", None),) + (P(),) * 8 + (
            P(both, None, None), P(both, None), P(both, None, None), P(both, None, None), P(both),
            P("ty", "tx", None), P(both, None, None),
        ),
        out_specs=(P("ty", "tx", None), P(both, None, None)) + (P(),) * 8,
        check_vma=False,
    )
```
